128 devices in a mesh: dp: 4 (over z), ctx: 8 (over y, x_hi), tensor: 4 (over x_lo, core).
Axes of the slice: x: 4 (x_hi: 2, x_lo: 2; x = x_hi * 2 + x_lo), y: 4, z: 4, core: 2. Of those that a mesh axis runs over, the one named last changes fastest.
Arguments:
- inputs: bfloat16 [16384, 1536], P(('dp', 'ctx', 'tensor')), may hold values from -6 to 6
- cotangent: bfloat16 [16384, 1536], P(('dp', 'ctx', 'tensor')), may hold values from -6 to 6
- lengths: int32 [4, 4], P('dp'), may hold values from 1 to 4093, as said below
- query_weight: float32 [1536, 1536], P(('dp', 'ctx'), 'tensor'), may hold values from -0.15625 to 0.15625
- query_mean: float32 [1536, 1536], P(('dp', 'ctx'), 'tensor'), may hold values from -64 to 64
- query_square: float32 [1536, 1536], P(('dp', 'ctx'), 'tensor'), may hold values from 425.984 to 1720.32
- pair_weight: float32 [1536, 512], P(('dp', 'ctx')), may hold values from -0.15625 to 0.15625
- pair_mean: float32 [1536, 512], P(('dp', 'ctx')), may hold values from -128 to 128
- pair_square: float32 [1536, 512], P(('dp', 'ctx')), may hold values from 2129.92 to 8683.52
- output_weight: float32 [1536, 1536], P(('dp', 'ctx'), 'tensor'), may hold values from -2.5 to 2.5
- output_mean: float32 [1536, 1536], P(('dp', 'ctx'), 'tensor'), may hold values from -5 to 5
- output_square: float32 [1536, 1536], P(('dp', 'ctx'), 'tensor'), may hold values from 3.11296 to 12.45184
- feed_weight: float32 [1536, 3, 8960], P(('dp', 'ctx'), None, 'tensor'), may hold values from -0.15625 to 0.15625
- feed_mean: float32 [1536, 3, 8960], P(('dp', 'ctx'), None, 'tensor'), may hold values from -48 to 48
- feed_square: float32 [1536, 3, 8960], P(('dp', 'ctx'), None, 'tensor'), may hold values from 311.296 to 1245.184
- gains: float32 [2, 1536], replicated, may hold values from 0.5 to 1.5
- gains_mean: float32 [2, 1536], replicated, may hold values from -128 to 128
- gains_square: float32 [2, 1536], replicated, may hold values from 1933.312 to 7700.48
- biases: float32 [2048], replicated, may hold values from -3 to 3
- biases_mean: float32 [2048], replicated, may hold values from -96 to 96
- biases_square: float32 [2048], replicated, may hold values from 1212.416 to 4751.36
Outputs:
- result: bfloat16 [16384, 1536], P(('dp', 'ctx', 'tensor'))
- input_grad: float32 [16384, 1536], P(('dp', 'ctx', 'tensor'))
- query_mean_next: float32 [1536, 1536], P(('dp', 'ctx'), 'tensor')
- query_square_next: float32 [1536, 1536], P(('dp', 'ctx'), 'tensor')
- query_weight_next: float32 [1536, 1536], P(('dp', 'ctx'), 'tensor')
- pair_mean_next: float32 [1536, 512], P(('dp', 'ctx'))
- pair_square_next: float32 [1536, 512], P(('dp', 'ctx'))
- pair_weight_next: float32 [1536, 512], P(('dp', 'ctx'))
- output_mean_next: float32 [1536, 1536], P(('dp', 'ctx'), 'tensor')
- output_square_next: float32 [1536, 1536], P(('dp', 'ctx'), 'tensor')
- output_weight_next: float32 [1536, 1536], P(('dp', 'ctx'), 'tensor')
- feed_mean_next: float32 [1536, 3, 8960], P(('dp', 'ctx'), None, 'tensor')
- feed_square_next: float32 [1536, 3, 8960], P(('dp', 'ctx'), None, 'tensor')
- feed_weight_next: float32 [1536, 3, 8960], P(('dp', 'ctx'), None, 'tensor')
- gains_mean_next: float32 [2, 1536], replicated
- gains_square_next: float32 [2, 1536], replicated
- gains_next: float32 [2, 1536], replicated
- biases_mean_next: float32 [2048], replicated
- biases_square_next: float32 [2048], replicated
- biases_next: float32 [2048], replicated
The draws below stay inside these ranges and needn't reach their ends.
Inputs may be any that keep to these rules, and one draw needn't show every extreme that they name: Row g lists, in order, the lengths of the 4 sequences packed into dp index g's 4096 rows and sums to 4096; in every row one sequence starts within the first 512 rows and ends within the last 512 rows; some row holds a sequence of 4093 rows.
All inputs are finite; a program needn't handle non-finite values.
Results may differ from the reference program's by a relative error of at most 0.015.
Values may be sent and summed in bfloat16 or wider, within the bound.
A program may use at most 320 MiB of HBM per device.

```python
import math
import jax
import jax.numpy as jnp
from jax import lax

D = 1536
HQ = 12
KV = 2
HD = 128
FF = 8960
LONGEST = 1024
STEP = 10
STRETCH = 512
GROUP = 4096
GROUPS = 4
TOKENS = 16384
QKV = 2048


def draw_lengths(key, part):
    key = jax.random.fold_in(key, 11)
    first_key, second_key, third_key, pick_key = jax.random.split(key, 4)
    first = jax.random.randint(first_key, (GROUPS,), 1, STRETCH)
    upper = GROUP - first - 2
    lower = jnp.maximum(GROUP - STRETCH - first + 1, jnp.minimum(LONGEST, upper))
    second = jax.random.randint(second_key, (GROUPS,), lower, upper + 1)
    remain = GROUP - first - second
    third = jax.random.randint(third_key, (GROUPS,), 1, remain)
    fourth = remain - third
    drawn = jnp.stack([first, second, third, fourth], axis=1).astype(jnp.int32)
    chosen = jax.random.randint(pick_key, (), 0, GROUPS)
    widest = jnp.array([1, GROUP - 3, 1, 1], dtype=jnp.int32)
    here = (jnp.arange(GROUPS, dtype=jnp.int32) == chosen)[:, None]
    return jnp.where(here, widest[None, :], drawn).astype(jnp.int32)


def steps_of(key, extent, cuts, smallest, largest):
    level, own = 1.0, jax.random.fold_in(key, 6)
    for dim, parts in cuts:
        steps = jnp.exp(jax.random.uniform(jax.random.fold_in(own, dim), (parts,), jnp.float32, smallest / len(cuts), largest / len(cuts)))
        level = level * jnp.repeat(steps, extent[dim] // parts).reshape([-1 if axis == dim else 1 for axis in range(len(extent))])
    return level


def gaussian(stream_key, extent, scale, most, pieces=(), kind=jnp.bfloat16):
    values = jax.random.normal(stream_key, extent, jnp.float32) * scale
    if len(pieces) > 0:
        values = steps_of(stream_key, extent, pieces, -0.22, 0.18) * values
    return jnp.clip(values, min=-most, max=most).astype(kind)


def setup_inputs(seed: int = 0) -> dict:
    seeds = jax.random.split(jax.random.key(seed), 22)
    return {
        "inputs": gaussian(seeds[0], (TOKENS, D), 1.0, 6.0, ((0, 128),)),
        "cotangent": gaussian(seeds[1], (TOKENS, D), 1.0, 6.0, ((0, 128),)),
        "lengths": draw_lengths(jax.random.fold_in(seeds[21], 71), 0),
        "query_weight": gaussian(seeds[3], (D, HQ * HD), D ** -0.5, 0.15625, ((0, 32), (1, 4)), jnp.float32),
        "query_mean": gaussian(seeds[4], (D, HQ * HD), (0.077 * TOKENS ** 0.5), 64.0, ((0, 32), (1, 4)), jnp.float32),
        "query_square": jnp.clip(jnp.exp(math.log(1720.32) - 1.3958638 * jax.random.uniform(seeds[5], (D, HQ * HD), jnp.float32) ** steps_of(seeds[5], (D, HQ * HD), ((0, 32), (1, 4)), -0.2, 0.2)), 425.984, 1720.32),
        "pair_weight": gaussian(seeds[6], (D, 2 * KV * HD), D ** -0.5, 0.15625, ((0, 32),), jnp.float32),
        "pair_mean": gaussian(seeds[7], (D, 2 * KV * HD), (0.18 * TOKENS ** 0.5), 128.0, ((0, 32),), jnp.float32),
        "pair_square": jnp.clip(jnp.exp(math.log(8683.52) - 1.40534254 * jax.random.uniform(seeds[8], (D, 2 * KV * HD), jnp.float32) ** steps_of(seeds[8], (D, 2 * KV * HD), ((0, 32),), -0.2, 0.2)), 2129.92, 8683.52),
        "output_weight": gaussian(seeds[9], (D, HQ * HD), (max(HQ * HD // 256, 1)) ** -0.5, 2.5, ((0, 32), (1, 4)), jnp.float32),
        "output_mean": gaussian(seeds[10], (D, HQ * HD), (0.0066 * TOKENS ** 0.5), 5.0, ((0, 32), (1, 4)), jnp.float32),
        "output_square": jnp.clip(jnp.exp(math.log(12.45184) - 1.3862944 * jax.random.uniform(seeds[11], (D, HQ * HD), jnp.float32) ** steps_of(seeds[11], (D, HQ * HD), ((0, 32), (1, 4)), -0.2, 0.2)), 3.11296, 12.45184),
        "feed_weight": gaussian(seeds[12], (D, 3, FF), D ** -0.5, 0.15625, ((0, 32), (2, 4)), jnp.float32),
        "feed_mean": gaussian(seeds[13], (D, 3, FF), (0.066 * TOKENS ** 0.5), 48.0, ((0, 32), (2, 4)), jnp.float32),
        "feed_square": jnp.clip(jnp.exp(math.log(1245.184) - 1.3862944 * jax.random.uniform(seeds[14], (D, 3, FF), jnp.float32) ** steps_of(seeds[14], (D, 3, FF), ((0, 32), (2, 4)), -0.2, 0.2)), 311.296, 1245.184),
        "gains": jnp.clip(1.0 + 0.1 * jax.random.normal(seeds[15], (2, D), jnp.float32), 0.5, 1.5),
        "gains_mean": gaussian(seeds[16], (2, D), (0.165 * TOKENS ** 0.5), 128.0, (), jnp.float32),
        "gains_square": jnp.clip(jnp.exp(jax.random.uniform(seeds[17], (2, D), jnp.float32, math.log(1933.312), math.log(7700.48))), 1933.312, 7700.48),
        "biases": gaussian(seeds[18], (QKV,), 0.5, 3.0, (), jnp.float32),
        "biases_mean": gaussian(seeds[19], (QKV,), (0.13 * TOKENS ** 0.5), 96.0, (), jnp.float32),
        "biases_square": jnp.clip(jnp.exp(jax.random.uniform(seeds[20], (QKV,), jnp.float32, math.log(1212.416), math.log(4751.36))), 1212.416, 4751.36),
    }


NORM_EPS = 1e-06
ROPE_BASE = 1000000.0
BETA_ONE = 0.9
BETA_TWO = 0.95
ADAM_EPS = 1e-08
MASKED = -1e+30

@jax.custom_vjp
def low(v):
    return lax.optimization_barrier(v.astype(jnp.bfloat16)).astype(jnp.float32)

@jax.custom_vjp
def low_back(v):
    return v

def low_keep(v):
    return (low(v), None)

def low_pass(kept, grad):
    return (grad,)

def back_keep(v):
    return (v, None)

def back_low(kept, grad):
    return (low(grad),)
low.defvjp(low_keep, low_pass)
low_back.defvjp(back_keep, back_low)

def highest(left, right):
    return jnp.dot(left, right, precision=lax.Precision.HIGHEST, preferred_element_type=jnp.float32)

def turn_half(values):
    half = values.shape[-1] // 2
    return jnp.concatenate([-values[..., half:], values[..., :half]], axis=-1)

def phases(position, width):
    steps = jnp.arange(width // 2, dtype=jnp.float32)
    inverse = jnp.exp(-(2.0 * steps / width) * math.log(ROPE_BASE))
    angle = position.astype(jnp.float32)[:, None] * inverse[None, :]
    angle = jnp.concatenate([angle, angle], axis=-1)
    return (jnp.cos(angle), jnp.sin(angle))

def rotate(values, cosine, sine):
    return values * cosine[:, None, :] + turn_half(values) * sine[:, None, :]

def layout(length_row, rows):
    ends = jnp.cumsum(length_row)
    index = jnp.arange(rows, dtype=jnp.int32)
    passed = (ends[None, :] <= index[:, None]).astype(jnp.int32)
    segment = lax.optimization_barrier(jnp.sum(passed, axis=1)).astype(jnp.int32)
    begins = lax.optimization_barrier(jnp.sum(passed * length_row[None, :], axis=1)).astype(jnp.int32)
    return (segment, index - begins)

def rms_norm(values, gain):
    return values * lax.rsqrt(lax.optimization_barrier(jnp.mean(values * values, axis=-1, keepdims=True)) + NORM_EPS) * gain

def attention(queries, keys, values, segment):
    rows = queries.shape[0]
    span = math.gcd(rows, 512)
    blocks = rows // span
    key_rep = jnp.repeat(keys, HQ // KV, axis=1)
    value_rep = jnp.repeat(values, HQ // KV, axis=1)
    index = jnp.arange(rows, dtype=jnp.int32)

    def one_block(item):
        query_rows, query_seg, query_idx = item
        raw = jnp.einsum('qhd,khd->qhk', query_rows, key_rep, precision=lax.Precision.HIGHEST)
        raw = low_back(raw * (1.0 / math.sqrt(HD)))
        allowed = ((query_seg[:, None] == segment[None, :]) & (index[None, :] <= query_idx[:, None]))[:, None, :]
        masked = jnp.where(allowed, raw, MASKED)
        top = lax.optimization_barrier(jnp.max(masked, axis=-1, keepdims=True))
        log_total = top + jnp.log(lax.optimization_barrier(jnp.sum(jnp.exp(masked - top), axis=-1, keepdims=True)))
        probs = low(jnp.exp(masked - log_total))
        return jnp.einsum('qhk,khd->qhd', probs, value_rep, precision=lax.Precision.HIGHEST)
    mapped = lax.map(jax.checkpoint(one_block), (queries.reshape(blocks, span, HQ, HD), segment.reshape(blocks, span), index.reshape(blocks, span)))
    return mapped.reshape(rows, HQ, HD)

def layer(flat, query_w, pair_w, output_w, feed_w, gain_pair, bias_all, segment, position):
    rows = flat.shape[0]
    normed = low(rms_norm(flat, gain_pair[0]))
    proj_q = low_back(highest(normed, low(query_w)) + bias_all[:HQ * HD])
    proj_p = low_back(highest(normed, low(pair_w)) + bias_all[HQ * HD:])
    cosine, sine = phases(position, HD)
    queries = low(rotate(proj_q.reshape(rows, HQ, HD), cosine, sine))
    keys = low(rotate(proj_p[:, :KV * HD].reshape(rows, KV, HD), cosine, sine))
    values = low(proj_p[:, KV * HD:].reshape(rows, KV, HD))
    attended = attention(queries, keys, values, segment)
    mixed = low(low_back(attended)).reshape(rows, HQ * HD)
    hidden = flat + low_back(highest(mixed, low(output_w).T))
    normed2 = low(rms_norm(hidden, gain_pair[1]))
    feed_low = low(feed_w)
    gate = low_back(highest(normed2, feed_low[:, 0, :]))
    up = low_back(highest(normed2, feed_low[:, 1, :]))
    act = low(jax.nn.silu(gate) * up)
    return hidden + low_back(highest(act, feed_low[:, 2, :].T))

def adamw(weight, mean_old, square_old, grad, rate, decay):
    mean_new = BETA_ONE * mean_old + (1.0 - BETA_ONE) * grad
    square_new = BETA_TWO * square_old + (1.0 - BETA_TWO) * grad * grad
    mean_hat = mean_new / (1.0 - BETA_ONE ** STEP)
    square_hat = square_new / (1.0 - BETA_TWO ** STEP)
    weight_new = weight - rate * (mean_hat / (jnp.sqrt(square_hat) + ADAM_EPS) + decay * weight)
    return (mean_new, square_new, weight_new)

def reference(inputs, cotangent, lengths, query_weight, query_mean, query_square, pair_weight, pair_mean, pair_square, output_weight, output_mean, output_square, feed_weight, feed_mean, feed_square, gains, gains_mean, gains_square, biases, biases_mean, biases_square):
    params = (query_weight, pair_weight, output_weight, feed_weight, gains, biases)
    rows = inputs.shape[0] // GROUPS
    flats = inputs.astype(jnp.float32).reshape(GROUPS, rows, D)
    backs = cotangent.astype(jnp.float32).reshape(GROUPS, rows, D)

    def per_group(totals, item):
        flat, back, length_row = item
        segment, position = layout(length_row, rows)
        out, pull = jax.vjp(lambda values, *weights: layer(values, *weights, segment, position), flat, *params)
        grads = pull(back)
        totals = tuple((a + b for a, b in zip(totals, grads[1:])))
        return (totals, (out, grads[0]))
    zeros = tuple((jnp.zeros_like(p) for p in params))
    totals, (outs, input_grads) = lax.scan(per_group, zeros, (flats, backs, lengths))
    result = outs.reshape(TOKENS, D).astype(jnp.bfloat16)
    input_grad = input_grads.reshape(TOKENS, D)
    pair_rate = 3.0 / math.sqrt(D)
    output_rate = 3.0 / math.sqrt(max(HQ * HD // 256, 1))
    query_new = adamw(query_weight, query_mean, query_square, totals[0], 0.05, 0.1)
    pair_new = adamw(pair_weight, pair_mean, pair_square, totals[1], pair_rate, 0.1)
    output_new = adamw(output_weight, output_mean, output_square, totals[2], output_rate, 0.1)
    feed_new = adamw(feed_weight, feed_mean, feed_square, totals[3], 0.05, 0.1)
    gains_new = adamw(gains, gains_mean, gains_square, totals[4], 1.5, 0.0)
    biases_new = adamw(biases, biases_mean, biases_square, totals[5], 0.5, 0.0)
    return (result, input_grad, query_new[0], query_new[1], query_new[2], pair_new[0], pair_new[1], pair_new[2], output_new[0], output_new[1], output_new[2], feed_new[0], feed_new[1], feed_new[2], gains_new[0], gains_new[1], gains_new[2], biases_new[0], biases_new[1], biases_new[2])
```

```python
import math

import jax
import jax.numpy as jnp
from jax import lax
from jax.experimental import pallas as pl
from jax.experimental.pallas import tpu as pltpu
from jax.sharding import Mesh
from jax.sharding import PartitionSpec as P

D = 1536
HQ = 12
KV = 2
HD = 128
FF = 8960
STEP = 10
ROWS = 128
HALF = 256
GROUP = 4096
PIECE = 48
FCUT = 1120
FPAD = 1152
QW = 384
SMALL = 1024
SPAN = 512

NORM_EPS = 1e-06
ROPE_BASE = 1000000.0
BETA_ONE = 0.9
BETA_TWO = 0.95
ADAM_EPS = 1e-08
MASKED = -1e30
LOG2E = math.log2(math.e)
ROOT2 = LOG2E / math.sqrt(HD)
INV_ROOT = 1.0 / math.sqrt(HD)

MESH_ID = pl.DeviceIdType.MESH
BF16 = jnp.bfloat16
F32 = jnp.float32
AXES = ("dp", "y", "xh", "tensor")


def up(v):
    return lax.rem(v + 1, 4)


def down(v):
    return lax.rem(v + 3, 4)


def opposite(v):
    return lax.rem(v + 2, 4)


def dot_nn(a, b):
    return lax.dot_general(a, b, (((1,), (0,)), ((), ())), preferred_element_type=F32)


def dot_nt(a, b):
    return lax.dot_general(a, b, (((1,), (1,)), ((), ())), preferred_element_type=F32)


def dot_tn(a, b):
    return lax.dot_general(a, b, (((0,), (0,)), ((), ())), preferred_element_type=F32)


class Place:
    def __init__(self):
        self.z = lax.axis_index("dp")
        self.y = lax.axis_index("y")
        self.h = lax.axis_index("xh")
        self.t = lax.axis_index("tensor")
        self.xl = self.t // 2
        self.k = lax.rem(self.t, 2)
        self.x = self.h * 2 + self.xl
        self.c = self.y * 2 + self.h

    def ring(self, z, y, h):
        return (z, y, h, self.t)

    def chip(self, x, k):
        return (self.z, self.y, x // 2, lax.rem(x, 2) * 2 + k)

    def block(self, c, k):
        return (self.z, c // 2, lax.rem(c, 2), self.xl * 2 + k)

    @property
    def core(self):
        return (self.z, self.y, self.h, self.xl * 2 + 1 - self.k)

    @property
    def side(self):
        return (self.z, self.y, self.h, (1 - self.xl) * 2 + self.k)

    @property
    def mirror(self):
        return (self.z, 3 - self.y, 1 - self.h, self.t)


class Net:
    def __init__(self, send, recv, local):
        self.send, self.recv, self.local = send, recv, local
        self.n, self.m = 0, 0
        self.started, self.kept = [], []

    def make(self, src, dst, dev):
        i = self.n
        self.n += 1
        return pltpu.make_async_remote_copy(
            src_ref=src,
            dst_ref=dst,
            send_sem=self.send.at[i],
            recv_sem=self.recv.at[i],
            device_id=dev,
            device_id_type=MESH_ID,
        )

    def copy(self, src, dst, dev):
        made = self.make(src, dst, dev)
        made.start()
        self.started.append(made)
        return made

    def here(self, src, dst):
        made = pltpu.make_async_copy(src, dst, self.local.at[self.m])
        self.m += 1
        made.start()
        return made

    def keep(self, src, dst):
        self.kept.append(self.here(src, dst))

    def finish(self):
        for made in self.started:
            made.wait_send()
        for made in self.kept:
            made.wait()


def barrier(devices):
    sem = pltpu.get_barrier_semaphore()
    for dev in devices:
        pl.semaphore_signal(sem, inc=1, device_id=dev, device_id_type=MESH_ID)
    pl.semaphore_wait(sem, len(devices))


def gather_ring(net, me, own, other, out, lead, lanes):
    z, y, h = me.z, me.y, me.h
    g = 1 - h
    low, high = lanes
    every = slice(None)

    def at(z, y, h, lane=None):
        index = [every] * lead + [z, y, h]
        if lane is not None:
            index += [every, lane]
        return out.at[tuple(index)]

    def same(piece, dev):
        return net.copy(piece, piece, dev)

    x = net.copy(other, at(z, y, h), me.ring(z, y, g))
    a_up = net.copy(own, at(z, y, h), me.ring(z, up(y), h))
    a_down = net.copy(own, at(z, y, h), me.ring(z, down(y), h))
    kept = net.here(own, at(z, y, h))
    yield
    x.wait_recv()
    b_up = same(at(z, y, g), me.ring(up(z), y, h))
    b_down = same(at(z, y, g), me.ring(down(z), y, h))
    yield
    a_up.wait_recv()
    a2_up = same(at(z, down(y), h, low), me.ring(z, up(y), h))
    a_down.wait_recv()
    a2_down = same(at(z, up(y), h, high), me.ring(z, down(y), h))
    yield
    b_up.wait_recv()
    b2_up = same(at(down(z), y, g, low), me.ring(up(z), y, h))
    b_down.wait_recv()
    b2_down = same(at(up(z), y, g, high), me.ring(down(z), y, h))
    yield
    kept.wait()
    a2_up.wait_recv()
    a2_down.wait_recv()
    c_up = same(at(z, every, h), me.ring(up(z), y, h))
    c_down = same(at(z, every, h), me.ring(down(z), y, h))
    yield
    b2_up.wait_recv()
    b2_down.wait_recv()
    d_up = same(at(every, y, g), me.ring(z, up(y), h))
    d_down = same(at(every, y, g), me.ring(z, down(y), h))
    yield
    c_up.wait_recv()
    c2_up = same(at(down(z), slice(0, 2), h), me.ring(up(z), y, h))
    c_down.wait_recv()
    c2_down = same(at(up(z), slice(2, 4), h), me.ring(down(z), y, h))
    yield
    d_up.wait_recv()
    d2_up = same(at(slice(0, 2), down(y), g), me.ring(z, up(y), h))
    d_down.wait_recv()
    d2_down = same(at(slice(2, 4), up(y), g), me.ring(z, down(y), h))
    yield
    for made in (c2_up, c2_down, d2_up, d2_down):
        made.wait_recv()


def gather_chips(net, me, buf):
    x, k = me.x, me.k
    first, last = slice(0, ROWS // 2), slice(ROWS // 2, ROWS)

    def send(x_at, rows, dev):
        piece = buf.at[x_at * 2 + k] if rows is None else buf.at[x_at * 2 + k, rows]
        return net.copy(piece, piece, dev)

    to_up, to_down = me.chip(up(x), k), me.chip(down(x), k)
    a1 = send(x, first, to_up)
    b1 = send(x, last, to_down)
    a2 = send(x, last, to_up)
    b2 = send(x, first, to_down)
    c0 = send(x, None, me.core)
    yield
    a1.wait_recv()
    f1 = send(down(x), first, to_up)
    b1.wait_recv()
    f2 = send(up(x), last, to_down)
    yield
    a2.wait_recv()
    g1 = send(down(x), None, me.core)
    b2.wait_recv()
    g2 = send(up(x), None, me.core)
    yield
    f1.wait_recv()
    f2.wait_recv()
    g3 = send(opposite(x), None, me.core)
    yield
    for made in (c0, g1, g2, g3):
        made.wait_recv()


def gather_block(net, me, buf):
    own = buf.at[me.t]
    far = buf.at[(1 - me.xl) * 2 + me.k]
    b = net.copy(own, own, me.side)
    a = net.copy(own, own, me.core)
    yield
    b.wait_recv()
    c = net.copy(far, far, me.core)
    yield
    a.wait_recv()
    c.wait_recv()


def sum_block(net, me, part, s1, r1, s2, r2):
    for i in range(2):
        s1[i] = part[i * 2 + 1 - me.k].astype(BF16)
    a = net.copy(s1, r1, me.core)
    yield None
    a.wait_recv()
    far = 1 - me.xl
    s2[...] = (part[far * 2 + me.k] + r1[far].astype(F32)).astype(BF16)
    b = net.copy(s2, r2, me.side)
    yield None
    near = part[me.t] + r1[me.xl].astype(F32)
    b.wait_recv()
    yield near + r2[...].astype(F32)


def rms(v):
    return lax.rsqrt(jnp.mean(v * v, axis=-1, keepdims=True) + NORM_EPS)


def spin(v, cosine, sine):
    return v * cosine + pltpu.roll(v, HD // 2, 1) * sine


def half_start(me, half):
    return me.c * 512 if half == 0 else GROUP - HALF - me.c * 512


def half_slot(c, half):
    return c * 2 if half == 0 else 15 - c * 2


def slot_of(c, k):
    return lax.select(k == 0, c * 2, 15 - c * 2)


def mask_of(me, half, begin, j, last):
    key = lax.broadcasted_iota(jnp.int32, (SPAN, HALF), 0) + j * SPAN
    allowed = key >= begin
    if last:
        query = lax.broadcasted_iota(jnp.int32, (SPAN, HALF), 1) + half_start(me, half)
        allowed = allowed & (key <= query)
    return allowed


def span_of(kv_ref, j, which):
    return kv_ref[pl.ds(2 * j, 2), which].reshape(SPAN, HD)


def attend(me, half, q_ref, kv_ref, begin_ref, att_ref, lse_ref):
    begin = begin_ref[half : half + 1, :]
    top = me.c if half == 0 else 7 - me.c

    def step(j, carry, last):
        keys = span_of(kv_ref, j, 0)
        values = span_of(kv_ref, j, 1).astype(F32).T.astype(BF16)
        allowed = mask_of(me, half, begin, j, last)
        out = []
        for head in range(3):
            high, total, summed = carry[head]
            raw = dot_nt(keys, q_ref[half, head]) * ROOT2
            raw = jnp.where(allowed, raw, MASKED)
            new = jnp.maximum(high, jnp.max(raw, axis=0, keepdims=True))
            probs = jnp.exp2(raw - new)
            fade = jnp.exp2(high - new)
            total = total * fade + jnp.sum(probs, axis=0, keepdims=True)
            summed = summed * fade + dot_nn(values, probs.astype(BF16))
            out.append((new, total, summed))
        return tuple(out)

    zero = (
        jnp.full((1, HALF), MASKED, F32),
        jnp.zeros((1, HALF), F32),
        jnp.zeros((HD, HALF), F32),
    )
    carry = step(top, (zero,) * 3, True)
    carry = lax.fori_loop(0, top, lambda i, carry: step(top - 1 - i, carry, False), carry)
    for head in range(3):
        high, total, summed = carry[head]
        att_ref[half, head] = (summed / total).T
        lse_ref[half * 3 + head : half * 3 + head + 1, :] = high + jnp.log2(total)


def front_kernel(
    x_ref,
    cot_ref,
    gains_ref,
    bias_ref,
    cos_ref,
    sin_ref,
    begin_ref,
    p1_ref,
    p2_ref,
    feed_ref,
    small_ref,
    normed_ref,
    q_ref,
    kv_ref,
    att_ref,
    lse_ref,
    xs_ref,
    hid_ref,
    n2_ref,
    cot8_ref,
    part,
    s1,
    r1,
    s2,
    r2,
    send,
    recv,
    local,
):
    me = Place()
    net = Net(send, recv, local)
    z, y, h, x, k, c = me.z, me.y, me.h, me.x, me.k, me.c
    slot = x * 2 + k
    barrier(
        [me.block(lax.rem(c + j, 8), k) for j in range(1, 8)]
        + [me.ring(up(z), y, h), me.ring(down(z), y, h)]
        + [me.chip(up(x), k), me.chip(down(x), k), me.core]
    )
    swap_x = net.make(x_ref, xs_ref, me.mirror)
    swap_cot = net.make(cot_ref, cot8_ref.at[(1 - h) * 4 + me.t], me.mirror)

    @pl.when(me.xl == 1)
    def _():
        swap_x.start()

    ring = gather_ring(
        net, me, p1_ref, p1_ref, small_ref, 0, (slice(0, 512), slice(512, 1024))
    )
    next(ring)

    @pl.when(me.xl == 0)
    def _():
        xs_ref[...] = x_ref[...]
        cot8_ref[slot] = cot_ref[...]

    @pl.when(me.xl == 1)
    def _():
        swap_x.wait()
        swap_cot.start()

    flat = xs_ref[...].astype(F32)
    normed_ref[me.t] = (flat * rms(flat) * gains_ref[0:1, :]).astype(BF16)
    block = gather_block(net, me, normed_ref)
    next(block)
    next(ring)
    next(ring)
    next(block)
    for _ in ring:
        pass
    for _ in block:
        pass
    feed = gather_ring(
        net, me, p2_ref.at[h], p2_ref.at[1 - h], feed_ref, 1, (slice(0, 640), slice(640, FPAD))
    )
    next(feed)

    proj = dot_nn(
        normed_ref[...].reshape(512, D), small_ref[:, :, :, :, 0:640].reshape(D, 640)
    )
    proj = proj + bias_ref[...]
    cosine, sine = cos_ref[...], sin_ref[...]
    keys = spin(proj[:, QW : QW + HD], cosine, sine).astype(BF16)
    values = proj[:, QW + HD : QW + 2 * HD].astype(BF16)
    for half in range(2):
        rows = slice(half * HALF, (half + 1) * HALF)
        kv_ref[half_slot(c, half), 0] = keys[rows]
        kv_ref[half_slot(c, half), 1] = values[rows]
    own_kv = kv_ref.at[slot_of(c, k)]
    kv_sent = [
        net.copy(own_kv, own_kv, me.block(lax.rem(c + j, 8), k)) for j in (4, 3, 5, 2, 6, 1, 7)
    ]
    for head in range(3):
        query = spin(proj[:, head * HD : (head + 1) * HD], cosine, sine).astype(BF16)
        for half in range(2):
            q_ref[half, head] = query[half * HALF : (half + 1) * HALF]

    @pl.when(me.xl == 1)
    def _():
        swap_cot.wait()

    cots = gather_chips(net, me, cot8_ref)
    next(feed)
    passed = []
    for j, made in zip((4, 3, 5, 2, 6, 1, 7), kv_sent):
        made.wait_recv()
        there = kv_ref.at[slot_of(lax.rem(c + 8 - j, 8), k)]
        passed.append(net.copy(there, there, me.core))
    next(feed)
    next(feed)
    next(cots)
    for made in passed:
        made.wait_recv()
    next(feed)
    next(feed)

    attend(me, 0, q_ref, kv_ref, begin_ref, att_ref, lse_ref)
    next(cots)
    next(cots)
    attend(me, 1, q_ref, kv_ref, begin_ref, att_ref, lse_ref)
    next(cots)

    wo = small_ref[:, :, :, :, 640:SMALL].reshape(D, QW)
    for half in range(2):
        mixed = jnp.concatenate(
            [att_ref[half, head].astype(BF16) for head in range(3)], axis=1
        )
        out = dot_nt(mixed, wo)
        part[2 * half] = out[:ROWS]
        part[2 * half + 1] = out[ROWS:]
    summed = sum_block(net, me, part, s1, r1, s2, r2)
    next(summed)
    next(summed)
    next(feed)
    branch = next(summed)
    hidden = flat + branch
    hid_ref[...] = hidden
    n2_ref[slot] = (hidden * rms(hidden) * gains_ref[1:2, :]).astype(BF16)
    rows = gather_chips(net, me, n2_ref)
    next(rows)
    next(rows)
    next(feed)
    for _ in rows:
        pass
    for _ in cots:
        pass
    for _ in feed:
        pass
    net.finish()


def front(x, cot, gains, bias, cosine, sine, begin, p1, p2):
    vmem = pl.BlockSpec(memory_space=pltpu.VMEM)
    hbm = pl.BlockSpec(memory_space=pl.ANY)
    shape = jax.ShapeDtypeStruct
    return pl.pallas_call(
        front_kernel,
        out_shape=(
            shape((3, 4, 4, 2, PIECE, FPAD), BF16),
            shape((4, 4, 2, PIECE, SMALL), BF16),
            shape((4, ROWS, D), BF16),
            shape((2, 3, HALF, HD), BF16),
            shape((16, 2, HALF, HD), BF16),
            shape((2, 3, HALF, HD), F32),
            shape((8, HALF), F32),
            shape((ROWS, D), BF16),
            shape((ROWS, D), F32),
            shape((8, ROWS, D), BF16),
            shape((8, ROWS, D), BF16),
        ),
        in_specs=[vmem] * 8 + [hbm],
        out_specs=(hbm,) + (vmem,) * 10,
        scratch_shapes=[
            pltpu.VMEM((4, ROWS, D), F32),
            pltpu.VMEM((2, ROWS, D), BF16),
            pltpu.VMEM((2, ROWS, D), BF16),
            pltpu.VMEM((ROWS, D), BF16),
            pltpu.VMEM((ROWS, D), BF16),
            pltpu.SemaphoreType.DMA((80,)),
            pltpu.SemaphoreType.DMA((80,)),
            pltpu.SemaphoreType.DMA((8,)),
        ],
        compiler_params=pltpu.CompilerParams(
            collective_id=0, has_side_effects=True, vmem_limit_bytes=60 * 2**20
        ),
        name="front",
    )(x, cot, gains, bias, cosine, sine, begin, p1, p2)


def contract(left, right, left_dim, right_dim):
    return lax.dot_general(
        left, right, (((left_dim,), (right_dim,)), ((), ())), preferred_element_type=F32
    )


def adamw(weight, mean_old, square_old, grad, rate, decay):
    mean_new = BETA_ONE * mean_old + (1.0 - BETA_ONE) * grad
    square_new = BETA_TWO * square_old + (1.0 - BETA_TWO) * grad * grad
    mean_hat = mean_new / (1.0 - BETA_ONE**STEP)
    square_hat = square_new / (1.0 - BETA_TWO**STEP)
    weight_new = weight - rate * (mean_hat / (jnp.sqrt(square_hat) + ADAM_EPS) + decay * weight)
    return (mean_new, square_new, weight_new)


def body(
    inputs,
    cotangent,
    lengths,
    query_weight,
    query_mean,
    query_square,
    pair_weight,
    pair_mean,
    pair_square,
    output_weight,
    output_mean,
    output_square,
    feed_weight,
    feed_mean,
    feed_square,
    gains,
    gains_mean,
    gains_square,
    biases,
    biases_mean,
    biases_square,
):
    y, h, t = (lax.axis_index(a) for a in AXES[1:])
    xl = t // 2
    ctx = y * 2 + h
    ends = jnp.cumsum(lengths[0])
    step = jnp.arange(HALF, dtype=jnp.int32)
    index = jnp.concatenate([ctx * 512 + step, GROUP - HALF - ctx * 512 + step])
    passed = (ends[None, :] <= index[:, None]).astype(jnp.int32)
    begin = jnp.sum(passed * lengths, axis=1)
    inverse = jnp.exp(
        -(2.0 * jnp.arange(HD // 2, dtype=jnp.float32) / HD) * math.log(ROPE_BASE)
    )
    angle = (index - begin).astype(F32)[:, None] * inverse[None, :]
    cosine, sine = jnp.cos(angle), jnp.sin(angle)
    cosine = jnp.concatenate([cosine, cosine], axis=1)
    sine = jnp.concatenate([-sine, sine], axis=1)
    begin = begin.reshape(2, HALF)
    key_at = xl * HD
    value_at = KV * HD + xl * HD
    p1 = jnp.concatenate(
        [
            query_weight,
            lax.dynamic_slice_in_dim(pair_weight, key_at, HD, 1),
            lax.dynamic_slice_in_dim(pair_weight, value_at, HD, 1),
            output_weight,
        ],
        axis=1,
    ).astype(BF16)
    p2 = jnp.pad(
        feed_weight.astype(BF16).reshape(PIECE, 3, 2, FCUT).transpose(2, 1, 0, 3),
        ((0, 0), (0, 0), (0, 0), (0, FPAD - FCUT)),
    )
    bias = jnp.concatenate(
        [
            lax.dynamic_slice_in_dim(biases, t * QW, QW),
            lax.dynamic_slice_in_dim(biases, HQ * HD + key_at, HD),
            lax.dynamic_slice_in_dim(biases, HQ * HD + value_at, HD),
        ]
    )[None]
    feed, small, normed, q, kv, att, lse, xs, hid, n2, cot8 = front(
        inputs, cotangent, gains, bias, cosine, sine, begin, p1, p2
    )
    small = small.reshape(D, SMALL)
    wq, wk, wv, wo = small[:, :QW], small[:, QW : QW + HD], small[:, QW + HD : 640], small[:, 640:]
    feed = feed.reshape(3, D, FPAD)
    x8 = n2.reshape(1024, D)
    c8 = cot8.reshape(1024, D)
    gate = contract(x8, feed[0], 1, 0)
    lift = contract(x8, feed[1], 1, 0)
    sig = jax.nn.sigmoid(gate)
    act = (gate * sig * lift).astype(BF16)
    d_act = contract(c8, feed[2], 1, 0)
    d_gate = (d_act * lift * sig * (1.0 + gate * (1.0 - sig))).astype(BF16)
    d_lift = (d_act * gate * sig).astype(BF16)
    out_p = contract(act, feed[2], 1, 1).reshape(8, ROWS, D)
    dn2_p = (contract(d_gate, feed[0], 1, 1) + contract(d_lift, feed[1], 1, 1)).reshape(8, ROWS, D)
    g_feed = jnp.stack(
        [contract(x8, d_gate, 0, 0), contract(x8, d_lift, 0, 0), contract(c8, act, 0, 0)]
    ).astype(BF16)
    own_cot = lax.dynamic_index_in_dim(cot8, h * 4 + t, 0, keepdims=False).astype(F32)
    scat = lambda v: lax.psum_scatter(v, ("xh", "tensor"), scatter_dimension=0, tiled=False)
    result = hid + scat(out_p)
    d_norm2 = scat(dn2_p)
    sc2 = rms(hid)
    xh2 = hid * sc2
    e2 = d_norm2 * gains[1]
    d_hidden = own_cot + sc2 * (e2 - xh2 * jnp.mean(e2 * xh2, axis=-1, keepdims=True))
    gain_two = jnp.sum(d_norm2 * xh2, axis=0)
    d_branch = lax.all_gather(d_hidden.astype(BF16), "tensor", axis=0, tiled=True)
    mixed = att.transpose(0, 2, 1, 3).reshape(512, QW).astype(BF16)
    g_out = contract(d_branch, mixed, 0, 0)
    d_mixed = contract(d_branch, wo, 1, 0).astype(BF16).reshape(2, HALF, 3, HD).transpose(0, 2, 1, 3)
    delta = jnp.sum(d_mixed.astype(F32) * att, axis=-1)
    lse6 = lse[:6].reshape(2, 3, HALF)
    keys = kv[:, 0].reshape(GROUP, HD)
    values = kv[:, 1].reshape(GROUP, HD)
    s = jnp.einsum("ahqd,kd->ahqk", q, keys, preferred_element_type=F32) * ROOT2
    ki = jnp.arange(GROUP)
    allowed = (ki[None, None, :] >= begin[:, :, None]) & (ki[None, None, :] <= index.reshape(2, HALF)[:, :, None])
    probs = jnp.where(allowed[:, None], jnp.exp2(s - lse6[..., None]), 0.0)
    dp = jnp.einsum("ahqd,kd->ahqk", d_mixed, values, preferred_element_type=F32)
    ds = (probs * (dp - delta[..., None])).astype(BF16)
    d_v = jnp.einsum("ahqk,ahqd->kd", probs.astype(BF16), d_mixed, preferred_element_type=F32)
    d_k = jnp.einsum("ahqk,ahqd->kd", ds, q, preferred_element_type=F32) * INV_ROOT
    d_q = jnp.einsum("ahqk,kd->ahqd", ds, keys, preferred_element_type=F32) * INV_ROOT
    d_q = d_q.transpose(0, 2, 1, 3).reshape(512, 3, HD)
    roll = lambda v: jnp.roll(v, HD // 2, axis=-1)
    d_q = (d_q * cosine[:, None] - roll(d_q) * sine[:, None]).reshape(512, QW).astype(BF16)
    d_kv = lax.psum(jnp.concatenate([d_k, d_v], 1), ("y", "xh"))
    core_sum = lax.psum(d_kv, "tensor", axis_index_groups=[[0, 1], [2, 3]])
    d_kv = jnp.take(core_sum, index, axis=0)
    d_kr = d_kv[:, :HD] * cosine - roll(d_kv[:, :HD]) * sine
    d_pair = jnp.concatenate([d_kr, d_kv[:, HD:]], 1).astype(BF16)
    k = t % 2
    mine = (jnp.arange(512) // HALF == k)[:, None]
    d_pair = jnp.where(mine, d_pair, 0)
    nrm = normed.reshape(512, D)
    g_small = jnp.concatenate([contract(nrm, d_q, 0, 0), contract(nrm, d_pair, 0, 0), g_out], 1)
    d_n1 = contract(d_q, wq, 1, 1) + contract(d_pair, small[:, QW:640], 1, 1)
    d_n1 = lax.psum_scatter(d_n1, "tensor", scatter_dimension=0, tiled=True)
    flat = xs.astype(F32)
    sc1 = rms(flat)
    xh1 = flat * sc1
    e1 = d_n1 * gains[0]
    input_grad = d_hidden + sc1 * (e1 - xh1 * jnp.mean(e1 * xh1, axis=-1, keepdims=True))
    gain_one = jnp.sum(d_n1 * xh1, axis=0)
    slots = jnp.zeros((2048,), F32)
    slots = lax.dynamic_update_slice(slots, jnp.sum(d_q.astype(F32), 0), (t * QW,))
    dps = jnp.sum(d_pair.astype(F32), 0)
    slots = lax.dynamic_update_slice(slots, dps[:HD], (HQ * HD + key_at,))
    slots = lax.dynamic_update_slice(slots, dps[HD:], (HQ * HD + value_at,))
    bias_total, gains_total = lax.psum((slots, jnp.stack([gain_one, gain_two])), AXES)
    g_small = lax.psum_scatter(g_small, ("dp", "y", "xh"), scatter_dimension=0, tiled=True)
    g_pair = g_small[:, QW:640]
    g_pair = lax.psum(g_pair, "tensor", axis_index_groups=[[0, 1], [2, 3]])
    g_pair = lax.all_gather(g_pair, "tensor", axis=0, tiled=False)
    g_pair = jnp.concatenate([g_pair[0, :, :HD], g_pair[2, :, :HD], g_pair[0, :, HD:], g_pair[2, :, HD:]], 1)
    g_feed = lax.psum_scatter(
        g_feed.reshape(3, 4, 4, 2, PIECE, FPAD).transpose(1, 2, 3, 0, 4, 5).reshape(4 * 4, 2, 3, PIECE, FPAD)[..., :FCUT],
        ("dp", "y"), scatter_dimension=0, tiled=False,
    )
    g_feed = lax.all_to_all(g_feed, "xh", 0, 0, tiled=True)
    g_feed = g_feed.transpose(2, 1, 0, 3).reshape(PIECE, 3, 2 * FCUT).astype(F32)
    perm = []
    for yy in range(4):
        for hh in range(2):
            for tt in range(4):
                src = (yy * 2 + hh) * 4 + tt
                dst = ((3 - yy) * 2 + 1 - hh) * 4 + tt if tt >= 2 else src
                perm.append((src, dst))
    back = lambda v: lax.ppermute(v, ("y", "xh", "tensor"), perm)
    result = back(result.astype(BF16))
    input_grad = back(input_grad)
    g_query, g_output = g_small[:, :QW], g_small[:, 640:]
    pair_rate = 3.0 / math.sqrt(D)
    output_rate = 3.0 / math.sqrt(max(HQ * HD // 256, 1))
    return (
        result,
        input_grad,
        *adamw(query_weight, query_mean, query_square, g_query, 0.05, 0.1),
        *adamw(pair_weight, pair_mean, pair_square, g_pair, pair_rate, 0.1),
        *adamw(output_weight, output_mean, output_square, g_output, output_rate, 0.1),
        *adamw(feed_weight, feed_mean, feed_square, g_feed, 0.05, 0.1),
        *adamw(gains, gains_mean, gains_square, gains_total, 1.5, 0.0),
        *adamw(biases, biases_mean, biases_square, bias_total, 0.5, 0.0),
    )


def solution(mesh):
    mesh = Mesh(mesh.devices.reshape(4, 4, 2, 4), AXES)
    rows = P(("dp", "y", "xh", "tensor"), None)
    cut = P(("dp", "y", "xh"), "tensor")
    pair = P(("dp", "y", "xh"), None)
    feed = P(("dp", "y", "xh"), None, "tensor")
    whole = P()
    in_specs = (rows, rows, P("dp", None))
    in_specs += (cut,) * 3 + (pair,) * 3 + (cut,) * 3 + (feed,) * 3 + (whole,) * 6
    out_specs = (rows, rows) + (cut,) * 3 + (pair,) * 3 + (cut,) * 3 + (feed,) * 3 + (whole,) * 6
    return jax.shard_map(body, mesh=mesh, in_specs=in_specs, out_specs=out_specs, check_vma=False)
```

```python
import math

import jax
import jax.numpy as jnp
from jax import lax
from jax.experimental import pallas as pl
from jax.experimental.pallas import tpu as pltpu
from jax.sharding import Mesh
from jax.sharding import PartitionSpec as P

D = 1536
HQ = 12
KV = 2
HD = 128
FF = 8960
STEP = 10
QKV = 2048
ROWS = 128
HALF = 256
GROUP = 4096
PIECE = 48
FCOLS = 2240
FPAD = 1152
QW = 384
SMALL = 1024
SPAN = 512

NORM_EPS = 1e-06
ROPE_BASE = 1000000.0
BETA_ONE = 0.9
BETA_TWO = 0.95
ADAM_EPS = 1e-08
MASKED = -1e30
LOG2E = math.log2(math.e)
ROOT2 = LOG2E / math.sqrt(HD)
INV_ROOT = 1.0 / math.sqrt(HD)

MESH_ID = pl.DeviceIdType.MESH
BF16 = jnp.bfloat16
F32 = jnp.float32
AXES = ("dp", "y", "xh", "tensor")


def up(v):
    return lax.rem(v + 1, 4)


def down(v):
    return lax.rem(v + 3, 4)


def opposite(v):
    return lax.rem(v + 2, 4)


def dot_nn(a, b):
    return lax.dot_general(a, b, (((1,), (0,)), ((), ())), preferred_element_type=F32)


def dot_nt(a, b):
    return lax.dot_general(a, b, (((1,), (1,)), ((), ())), preferred_element_type=F32)


def dot_tn(a, b):
    return lax.dot_general(a, b, (((0,), (0,)), ((), ())), preferred_element_type=F32)


class Place:
    def __init__(self):
        self.z = lax.axis_index("dp")
        self.y = lax.axis_index("y")
        self.h = lax.axis_index("xh")
        self.t = lax.axis_index("tensor")
        self.xl = self.t // 2
        self.k = lax.rem(self.t, 2)
        self.x = self.h * 2 + self.xl
        self.c = self.y * 2 + self.h

    def ring(self, z, y, h):
        return (z, y, h, self.t)

    def chip(self, x, k):
        return (self.z, self.y, x // 2, lax.rem(x, 2) * 2 + k)

    def block(self, c, k):
        return (self.z, c // 2, lax.rem(c, 2), self.xl * 2 + k)

    @property
    def core(self):
        return (self.z, self.y, self.h, self.xl * 2 + 1 - self.k)

    @property
    def side(self):
        return (self.z, self.y, self.h, (1 - self.xl) * 2 + self.k)


class Net:
    def __init__(self, send, recv, local):
        self.send, self.recv, self.local = send, recv, local
        self.n, self.m = 0, 0
        self.started, self.kept = [], []

    def make(self, src, dst, dev):
        i = self.n
        self.n += 1
        return pltpu.make_async_remote_copy(
            src_ref=src,
            dst_ref=dst,
            send_sem=self.send.at[i],
            recv_sem=self.recv.at[i],
            device_id=dev,
            device_id_type=MESH_ID,
        )

    def copy(self, src, dst, dev):
        made = self.make(src, dst, dev)
        made.start()
        self.started.append(made)
        return made

    def here(self, src, dst):
        made = pltpu.make_async_copy(src, dst, self.local.at[self.m])
        self.m += 1
        made.start()
        return made

    def keep(self, src, dst):
        self.kept.append(self.here(src, dst))

    def finish(self, done=()):
        for made in self.started:
            if all(made is not other for other in done):
                made.wait_send()
        for made in self.kept:
            made.wait()


def barrier(devices):
    sem = pltpu.get_barrier_semaphore()
    for dev in devices:
        pl.semaphore_signal(sem, inc=1, device_id=dev, device_id_type=MESH_ID)
    pl.semaphore_wait(sem, len(devices))


def gather_ring(net, me, own, other, out, lead, lanes, near=True, far=True):
    z, y, h = me.z, me.y, me.h
    g = 1 - h
    low, high = lanes
    every = slice(None)

    def at(z, y, h, lane=None):
        index = [every] * lead + [z, y, h]
        if lane is not None:
            index += [every, lane]
        return out.at[tuple(index)]

    def same(piece, dev):
        return net.copy(piece, piece, dev)

    waits_a, waits_b = [], []
    if near:
        x = net.copy(other, at(z, y, h), me.ring(z, y, g))
        a_up = net.copy(own, at(z, y, h), me.ring(z, up(y), h))
        a_down = net.copy(own, at(z, y, h), me.ring(z, down(y), h))
        kept = net.here(own, at(z, y, h))
        yield
        x.wait_recv()
        b_up = same(at(z, y, g), me.ring(up(z), y, h))
        b_down = same(at(z, y, g), me.ring(down(z), y, h))
        yield
        a_up.wait_recv()
        a2_up = same(at(z, down(y), h, low), me.ring(z, up(y), h))
        a_down.wait_recv()
        a2_down = same(at(z, up(y), h, high), me.ring(z, down(y), h))
        yield
        b_up.wait_recv()
        b2_up = same(at(down(z), y, g, low), me.ring(up(z), y, h))
        b_down.wait_recv()
        b2_down = same(at(up(z), y, g, high), me.ring(down(z), y, h))
        yield
        kept.wait()
        waits_a, waits_b = [a2_up, a2_down], [b2_up, b2_down]
    for made in waits_a:
        made.wait_recv()
    if far:
        c_up = same(at(z, every, h), me.ring(up(z), y, h))
        c_down = same(at(z, every, h), me.ring(down(z), y, h))
        yield
    for made in waits_b:
        made.wait_recv()
    if far:
        d_up = same(at(every, y, g), me.ring(z, up(y), h))
        d_down = same(at(every, y, g), me.ring(z, down(y), h))
        yield
        c_up.wait_recv()
        c2_up = same(at(down(z), slice(0, 2), h), me.ring(up(z), y, h))
        c_down.wait_recv()
        c2_down = same(at(up(z), slice(2, 4), h), me.ring(down(z), y, h))
        yield
        d_up.wait_recv()
        d2_up = same(at(slice(0, 2), down(y), g), me.ring(z, up(y), h))
        d_down.wait_recv()
        d2_down = same(at(slice(2, 4), up(y), g), me.ring(z, down(y), h))
        yield
        for made in (c2_up, c2_down, d2_up, d2_down):
            made.wait_recv()


def gather_chips(net, me, buf):
    x, k = me.x, me.k
    first, last = slice(0, ROWS // 2), slice(ROWS // 2, ROWS)

    def send(x_at, rows, dev):
        piece = buf.at[x_at * 2 + k] if rows is None else buf.at[x_at * 2 + k, rows]
        return net.copy(piece, piece, dev)

    to_up, to_down = me.chip(up(x), k), me.chip(down(x), k)
    c0 = send(x, None, me.core)
    a1 = send(x, first, to_up)
    b1 = send(x, last, to_down)
    a2 = send(x, last, to_up)
    b2 = send(x, first, to_down)
    yield
    c0.wait_recv()
    yield
    a1.wait_recv()
    f1 = send(down(x), first, to_up)
    b1.wait_recv()
    f2 = send(up(x), last, to_down)
    yield
    a2.wait_recv()
    g1 = send(down(x), None, me.core)
    b2.wait_recv()
    g2 = send(up(x), None, me.core)
    yield
    g1.wait_recv()
    g2.wait_recv()
    yield
    f1.wait_recv()
    f2.wait_recv()
    g3 = send(opposite(x), None, me.core)
    yield
    g3.wait_recv()


def gather_block(net, me, buf):
    own = buf.at[me.t]
    far = buf.at[(1 - me.xl) * 2 + me.k]
    b = net.copy(own, own, me.side)
    a = net.copy(own, own, me.core)
    yield
    b.wait_recv()
    c = net.copy(far, far, me.core)
    yield
    a.wait_recv()
    c.wait_recv()


def sum_block(net, me, part, s1, r1, s2, r2):
    for i in range(2):
        s1[i] = part[i * 2 + 1 - me.k].astype(BF16)
    a = net.copy(s1, r1, me.core)
    yield None
    a.wait_recv()
    far = 1 - me.xl
    s2[...] = (part[far * 2 + me.k] + r1[far].astype(F32)).astype(BF16)
    b = net.copy(s2, r2, me.side)
    yield None
    near = part[me.t] + r1[me.xl].astype(F32)
    b.wait_recv()
    yield near + r2[...].astype(F32)


def rms(v):
    return lax.rsqrt(jnp.mean(v * v, axis=-1, keepdims=True) + NORM_EPS)


def spin(v, cosine, sine):
    return v * cosine + pltpu.roll(v, HD // 2, 1) * sine


def half_start(me, half):
    return me.c * 512 + half * HALF


def mask_of(me, half, begin, j, last):
    key = lax.broadcasted_iota(jnp.int32, (SPAN, HALF), 0) + j * SPAN
    allowed = key >= begin
    if last:
        query = lax.broadcasted_iota(jnp.int32, (SPAN, HALF), 1) + half_start(me, half)
        allowed = allowed & (key <= query)
    return allowed


def span_of(kv_ref, j, which):
    return kv_ref[pl.ds(2 * j, 2), which].reshape(SPAN, HD)


def attend(me, half, q_ref, kv_ref, begin_ref, att_ref, lse_ref):
    begin = begin_ref[half : half + 1, :]
    top = me.c

    def step(j, carry, last):
        keys = span_of(kv_ref, j, 0)
        values = span_of(kv_ref, j, 1).astype(F32).T.astype(BF16)
        allowed = mask_of(me, half, begin, j, last)
        out = []
        for head in range(3):
            high, total, summed = carry[head]
            raw = dot_nt(keys, q_ref[half, head]) * ROOT2
            raw = jnp.where(allowed, raw, MASKED)
            new = jnp.maximum(high, jnp.max(raw, axis=0, keepdims=True))
            probs = jnp.exp2(raw - new)
            fade = jnp.exp2(high - new)
            total = total * fade + jnp.sum(probs, axis=0, keepdims=True)
            summed = summed * fade + dot_nn(values, probs.astype(BF16))
            out.append((new, total, summed))
        return tuple(out)

    zero = (
        jnp.full((1, HALF), MASKED, F32),
        jnp.zeros((1, HALF), F32),
        jnp.zeros((HD, HALF), F32),
    )
    carry = step(top, (zero,) * 3, True)
    carry = lax.fori_loop(0, top, lambda i, carry: step(top - 1 - i, carry, False), carry)
    for head in range(3):
        high, total, summed = carry[head]
        att_ref[half, head] = (summed / total).T
        lse_ref[half * 3 + head : half * 3 + head + 1, :] = high + jnp.log2(total)

class Refs:
    def __init__(self, names, refs):
        for name, ref in zip(names, refs):
            setattr(self, name, ref)


class ChipSum:
    def __init__(self, net, me, src, mine, bufs):
        self.net, self.me, self.src, self.mine = net, me, src, mine
        self.r1, self.a1, self.a2, self.ru, self.rd = bufs
        self.pushed = {}
        x = me.x
        self.order = {"far": opposite(x), "above": up(x), "below": down(x), "own": x}

    def push(self, name):
        i = self.order[name]
        self.pushed[name] = self.net.copy(
            self.src.at[i, 1 - self.me.k], self.r1.at[i], self.me.core
        )

    def add(self, name):
        i = self.order[name]
        self.pushed[name].wait_recv()
        self.r1[i] = (self.r1[i].astype(F32) + self.mine(i).astype(F32)).astype(BF16)
        return i

    def steps(self):
        net, me = self.net, self.me
        r1, a1, a2, ru, rd = self.r1, self.a1, self.a2, self.ru, self.rd
        first, last = slice(0, ROWS // 2), slice(ROWS // 2, ROWS)
        to_up, to_down = me.chip(up(me.x), me.k), me.chip(down(me.x), me.k)
        far = self.add("far")
        e1 = net.copy(r1.at[far, first], a1, to_up)
        e2 = net.copy(r1.at[far, last], a2, to_down)
        yield None
        above = self.add("above")
        e3 = net.copy(r1.at[above, last], ru.at[last], to_up)
        below = self.add("below")
        e4 = net.copy(r1.at[below, first], rd.at[first], to_down)
        yield None
        x = self.add("own")
        e1.wait_recv()
        a1[...] = (a1[...].astype(F32) + r1[above, first].astype(F32)).astype(BF16)
        e5 = net.copy(a1, ru.at[first], to_up)
        e2.wait_recv()
        a2[...] = (a2[...].astype(F32) + r1[below, last].astype(F32)).astype(BF16)
        e6 = net.copy(a2, rd.at[last], to_down)
        yield None
        for made in (e3, e4, e5, e6):
            made.wait_recv()
        yield r1[x].astype(F32) + ru[...].astype(F32) + rd[...].astype(F32)


CHIP_BUFS = [
    ((4, ROWS, D), BF16),
    ((ROWS // 2, D), BF16),
    ((ROWS // 2, D), BF16),
    ((ROWS, D), BF16),
    ((ROWS, D), BF16),
]


FRONT_IN = ["x", "cot", "gains", "bias", "cos", "sin", "begin", "p1", "po", "p2", "pd"]
FRONT_OUT = ["feed", "wd", "small", "wo", "normed", "q", "kv", "att", "lse", "hid", "n2", "cot8"]
FRONT_SCRATCH = {
    "cs": ((8, ROWS, D), BF16),
    "part": ((4, ROWS, D), F32),
    "s1": ((2, ROWS, D), BF16),
    "r1": ((2, ROWS, D), BF16),
    "s2": ((ROWS, D), BF16),
    "r2": ((ROWS, D), BF16),
}


def front_kernel(*refs):
    names = FRONT_IN + FRONT_OUT + list(FRONT_SCRATCH)
    r = Refs(names, refs)
    send, recv, local = refs[len(names) :]
    me = Place()
    net = Net(send, recv, local)
    z, y, h, x, k, c = me.z, me.y, me.h, me.x, me.k, me.c
    slot = x * 2 + k
    barrier(
        [me.block(lax.rem(c + j, 8), k) for j in range(1, 8)]
        + [me.ring(up(z), y, h), me.ring(down(z), y, h)]
        + [me.chip(up(x), k), me.chip(down(x), k), me.core]
    )
    ring = gather_ring(net, me, r.p1, r.p1, r.small, 0, (slice(0, 384), slice(384, 640)))
    next(ring)
    r.cs[slot] = r.cot[...]
    own = r.x[...].astype(F32)
    r.normed[me.t] = (own * rms(own) * r.gains[0:1, :]).astype(BF16)
    block = gather_block(net, me, r.normed)
    next(block)
    next(ring)
    next(ring)
    next(ring)
    next(ring)
    next(block)
    next(ring)
    for _ in block:
        pass
    for _ in ring:
        pass
    feed = gather_ring(
        net, me, r.p2.at[h], r.p2.at[1 - h], r.feed, 1, (slice(0, 640), slice(640, FPAD))
    )
    lanes = (slice(0, 640), slice(640, FPAD))
    down_near = gather_ring(net, me, r.pd.at[h], r.pd.at[1 - h], r.wd, 0, lanes, far=False)
    outer = gather_ring(net, me, r.po, r.po, r.wo, 0, (slice(0, 256), slice(256, QW)))
    next(feed)
    normed = r.normed[...].reshape(512, D)
    cosine, sine = r.cos[...], r.sin[...]
    proj = dot_nn(normed, r.small[:, :, :, :, QW:640].reshape(D, 2 * HD)) + r.bias[:, QW:640]
    keys = spin(proj[:, :HD], cosine, sine).astype(BF16)
    values = proj[:, HD:].astype(BF16)
    for half in range(2):
        rows = slice(half * HALF, (half + 1) * HALF)
        r.kv[2 * c + half, 0] = keys[rows]
        r.kv[2 * c + half, 1] = values[rows]
    own_kv = r.kv.at[2 * c + k]
    order = (4, 3, 5, 2, 6, 1, 7)
    kv_sent = [net.copy(own_kv, own_kv, me.block(lax.rem(c + j, 8), k)) for j in order]
    next(outer)
    proj = dot_nn(normed, r.small[:, :, :, :, 0:QW].reshape(D, QW)) + r.bias[:, 0:QW]
    for head in range(3):
        query = spin(proj[:, head * HD : (head + 1) * HD], cosine, sine).astype(BF16)
        r.q[0, head] = query[:HALF]
        r.q[1, head] = query[HALF:]
    next(feed)
    next(feed)
    next(outer)
    next(outer)
    next(feed)
    next(outer)
    next(feed)
    passed = []
    for j, made in zip(order, kv_sent):
        made.wait_recv()
        there = r.kv.at[2 * lax.rem(c + 8 - j, 8) + k]
        passed.append(net.copy(there, there, me.core))
    next(feed)
    cots = gather_chips(net, me, r.cs)
    next(cots)
    next(outer)
    next(outer)
    for made in passed:
        made.wait_recv()
    next(down_near)
    attend(me, 0, r.q, r.kv, r.begin, r.att, r.lse)
    next(outer)
    next(outer)
    next(down_near)
    next(cots)
    next(cots)
    attend(me, 1, r.q, r.kv, r.begin, r.att, r.lse)
    next(down_near)
    next(down_near)
    next(feed)
    next(cots)
    for _ in outer:
        pass
    wo = r.wo[...].reshape(D, QW)
    for half in range(2):
        mixed = jnp.concatenate([r.att[half, head].astype(BF16) for head in range(3)], axis=1)
        out = dot_nt(mixed, wo)
        r.part[2 * half] = out[:ROWS]
        r.part[2 * half + 1] = out[ROWS:]
    summed = sum_block(net, me, r.part, r.s1, r.r1, r.s2, r.r2)
    next(summed)
    next(cots)
    next(cots)
    next(summed)
    next(feed)
    for _ in down_near:
        pass
    for _ in cots:
        pass
    net.keep(r.cs, r.cot8)
    branch = next(summed)
    hidden = own + branch
    r.hid[...] = hidden
    r.n2[...] = (hidden * rms(hidden) * r.gains[1:2, :]).astype(BF16)
    for _ in feed:
        pass
    net.finish()


def call(kernel, ins, arrays, outs, far, scratch, collective, limit, name):
    vmem = pl.BlockSpec(memory_space=pltpu.VMEM)
    hbm = pl.BlockSpec(memory_space=pl.ANY)
    return pl.pallas_call(
        kernel,
        out_shape=tuple(jax.ShapeDtypeStruct(*s) for s in outs.values()),
        in_specs=[hbm if n in far else vmem for n in ins],
        out_specs=tuple(hbm if n in far else vmem for n in outs),
        scratch_shapes=scratch,
        compiler_params=pltpu.CompilerParams(
            collective_id=collective, has_side_effects=True, vmem_limit_bytes=limit * 2**20
        ),
        name=name,
    )(*arrays)


def semaphores(*counts):
    return [pltpu.SemaphoreType.DMA((n,)) for n in counts]


def scratch_of(shapes):
    return [pltpu.VMEM(*s) for s in shapes.values()]


def front(*arrays):
    shapes = (
        ((2, 4, 4, 2, PIECE, FPAD), BF16),
        ((4, 4, 2, PIECE, FPAD), BF16),
        ((4, 4, 2, PIECE, 640), BF16),
        ((4, 4, 2, PIECE, QW), BF16),
        ((4, ROWS, D), BF16),
        ((2, 3, HALF, HD), BF16),
        ((16, 2, HALF, HD), BF16),
        ((2, 3, HALF, HD), F32),
        ((8, HALF), F32),
        ((ROWS, D), F32),
        ((ROWS, D), BF16),
        ((8, ROWS, D), BF16),
    )
    return call(
        front_kernel,
        FRONT_IN,
        arrays,
        dict(zip(FRONT_OUT, shapes)),
        ("p2", "pd", "feed", "wd", "cot8"),
        scratch_of(FRONT_SCRATCH) + semaphores(110, 110, 10),
        0,
        63,
        "front",
    )


def ring_sum(net, pick, here, to_up, to_down, cut, add, a1, a2, ru, rd, terms=None):
    above, below, far = up(here), down(here), opposite(here)
    if terms is None:
        terms = (pick(above, 0), pick(below, 1))
    e1 = net.copy(pick(far, 0), a1, to_up)
    e2 = net.copy(pick(far, 1), a2, to_down)
    e3 = net.copy(pick(above, 1), cut(ru, 1), to_up)
    e4 = net.copy(pick(below, 0), cut(rd, 0), to_down)
    yield
    e1.wait_recv()
    add(a1, terms[0])
    e5 = net.copy(a1, cut(ru, 0), to_up)
    e2.wait_recv()
    add(a2, terms[1])
    e6 = net.copy(a2, cut(rd, 1), to_down)
    yield
    for made in (e3, e4, e5, e6):
        made.wait_recv()


def add_pieces(lead):
    def add(dst, *srcs):
        count = math.prod(dst.shape[:-2])
        inner = dst.shape[lead] if len(dst.shape) > lead + 2 else 1

        def one(i, carry):
            if len(dst.shape) == 2:
                at = (slice(None), slice(None))
            elif len(dst.shape) == 3:
                at = (i,)
            else:
                at = (i // inner, lax.rem(i, inner))
            total = dst[at].astype(F32)
            for src in srcs:
                total = total + src[at].astype(F32)
            dst[at] = total.astype(dst.dtype)
            return carry

        if count == 1:
            one(0, 0)
        else:
            lax.fori_loop(0, count, one, 0)

    return add


RING_BUFS = ("a1", "a2", "ru", "rd", "b1", "b2", "su", "sd")


def ring_bufs(lead, width, low):
    pair = (*lead, 2, PIECE, width)
    four = (*lead, 4, PIECE, width)
    one = (*lead, PIECE, width)
    shapes = (
        pair,
        pair,
        four,
        four,
        (*lead, PIECE, low),
        (*lead, PIECE, width - low),
        one,
        one,
    )
    return [pltpu.VMEM(s, BF16) for s in shapes] * 2


def reduce_ring(net, me, grad, lead, low, bufs, landing, loads=None):
    z, y, h = me.z, me.y, me.h
    g = 1 - h
    every = slice(None)
    width = grad.shape[-1]
    lanes = (slice(0, low), slice(low, width))
    pairs = (slice(0, 2), slice(2, 4))
    own = dict(zip(RING_BUFS, bufs[:8]))
    other = dict(zip(RING_BUFS, bufs[8:]))
    add = add_pieces(lead)

    def front_of(ref, *index):
        return ref.at[(every,) * lead + index]

    def cut_pair(ref, part):
        return front_of(ref, pairs[part])

    def cut_lane(ref, part):
        return front_of(ref, every, lanes[part])

    ring_z = (me.ring(up(z), y, h), me.ring(down(z), y, h))
    ring_y = (me.ring(z, up(y), h), me.ring(z, down(y), h))
    a_at = lambda i, part: front_of(grad, i, pairs[part], h)
    b_at = lambda i, part: front_of(grad, pairs[part], i, g)
    a_terms = (a_at(up(z), 0), a_at(down(z), 1), front_of(grad, z, every, h))
    b_terms = (b_at(up(y), 0), b_at(down(y), 1), front_of(grad, every, y, g))
    loading = []
    if loads is not None:
        loading = [net.here(s, d) for s, d in zip(a_terms + b_terms, loads)]
        a_terms, b_terms = loads[:3], loads[3:]
    a = ring_sum(
        net, a_at, z, *ring_z, cut_pair, add, *(own[n] for n in RING_BUFS[:4]), a_terms
    )
    b = ring_sum(
        net, b_at, y, *ring_y, cut_pair, add, *(other[n] for n in RING_BUFS[:4]), b_terms
    )
    next(a)
    next(b)
    yield
    for made in loading:
        made.wait()
    next(a)
    next(b)
    yield
    for _ in a:
        pass
    add(own["ru"], own["rd"], a_terms[2])
    a = ring_sum(
        net,
        lambda i, part: front_of(own["ru"], i, every, lanes[part]),
        y,
        *ring_y,
        cut_lane,
        add,
        *(own[n] for n in RING_BUFS[4:]),
    )
    next(a)
    for _ in b:
        pass
    add(other["ru"], other["rd"], b_terms[2])
    b = ring_sum(
        net,
        lambda i, part: front_of(other["ru"], i, every, lanes[part]),
        z,
        *ring_z,
        cut_lane,
        add,
        *(other[n] for n in RING_BUFS[4:]),
    )
    next(b)
    yield
    next(a)
    next(b)
    yield
    for _ in b:
        pass
    add(other["su"], other["sd"], front_of(other["ru"], z))
    last = net.copy(other["su"], landing, me.ring(z, y, g))
    for _ in a:
        pass
    add(own["su"], own["sd"], front_of(own["ru"], y))
    yield
    last.wait_recv()


MID_IN = ["n2", "cot8", "w", "wdn", "hid", "gains"]
MID_OUT = ["out", "g", "gd", "dbr", "dh", "gain"]
MID_SCRATCH = {
    "x8": ((8, ROWS, D), BF16),
    "c8": ((8, ROWS, D), BF16),
    "w8": ((2, D, FPAD), BF16),
    "wd": ((4, 4, 2, PIECE, FPAD), BF16),
    "act": ((8, ROWS, FPAD), BF16),
    "dg": ((8, ROWS, FPAD), BF16),
    "du": ((8, ROWS, FPAD), BF16),
    "out8": ((4, 2, ROWS, D), BF16),
    "dn2": ((4, 2, ROWS, D), BF16),
    "g8": ((2, D, FPAD), BF16),
    "gd8": ((4, 4, 2, PIECE, FPAD), BF16),
}
LANES = [slice(i * 256, i * 256 + 256) for i in range(4)] + [slice(1024, FPAD)]


def tile(i, size):
    return pl.ds(pl.multiple_of(i * size, size), size)


def hidden_units(r, chip):
    at = pl.ds(2 * chip, 2)
    left = r.x8[at].reshape(2 * ROWS, D)
    for lanes in LANES:
        gate = dot_nn(left, r.w8[0, :, lanes])
        lift = dot_nn(left, r.w8[1, :, lanes])
        sigma = 1.0 / (1.0 + jnp.exp(-gate))
        silu = gate * sigma
        pieces = (
            (r.act, silu * lift),
            (r.du, silu),
            (r.dg, lift * (sigma * (1.0 + gate * (1.0 - sigma)))),
        )
        for ref, value in pieces:
            ref[at, :, lanes] = value.astype(BF16).reshape(2, ROWS, value.shape[1])


def unit_gradients(r):
    back = r.c8[...].reshape(8 * ROWS, D)
    for lanes in LANES:
        d_act = dot_nn(back, r.wd[:, :, :, :, lanes].reshape(D, lanes.stop - lanes.start))
        d_act = d_act.reshape(8, ROWS, lanes.stop - lanes.start)
        for ref in (r.du, r.dg):
            ref[:, :, lanes] = (d_act * ref[:, :, lanes].astype(F32)).astype(BF16)


def gradient_rows(r, chip):
    at = pl.ds(2 * chip, 2)
    dg, du = (ref[at].reshape(2 * ROWS, FPAD) for ref in (r.dg, r.du))

    def one(j, carry):
        wide = tile(j, 512)
        both = dot_nt(dg, r.w8[0, wide, :]) + dot_nt(du, r.w8[1, wide, :])
        r.dn2[chip, :, :, wide] = both.astype(BF16).reshape(2, ROWS, 512)
        return carry

    lax.fori_loop(0, 3, one, 0)


def mid_kernel(*refs):
    names = MID_IN + MID_OUT + list(MID_SCRATCH)
    r = Refs(names, refs)
    rest = refs[len(names) :]
    bufs, ring_bufs_d = rest[:5], rest[5:21]
    send, recv, local = rest[21:]
    me = Place()
    net = Net(send, recv, local)
    x, k, t = me.x, me.k, me.t
    z, y, h = me.z, me.y, me.h
    lines = [(z, slice(None), h), (slice(None), y, 1 - h)]
    near = [net.here(r.wdn.at[at], r.wd.at[at]) for at in lines]
    load_w = net.here(r.w, r.w8)
    load_c = net.here(r.cot8, r.c8)
    barrier(
        [me.chip(up(x), k), me.chip(down(x), k), me.core]
        + [me.ring(up(z), y, h), me.ring(down(z), y, h)]
        + [me.ring(z, up(y), h), me.ring(z, down(y), h)]
    )
    r.x8[x * 2 + k] = r.n2[...]
    rows = gather_chips(net, me, r.x8)
    next(rows)
    ring = gather_ring(net, me, None, None, r.wd, 0, (None, None), near=False)
    for made in near:
        made.wait()
    next(ring)
    next(ring)
    load_w.wait()
    next(rows)
    next(rows)
    hidden_units(r, x)
    next(rows)
    next(rows)
    hidden_units(r, down(x))
    next(ring)
    next(ring)
    next(rows)
    hidden_units(r, up(x))
    for _ in rows:
        pass
    hidden_units(r, opposite(x))
    for _ in ring:
        pass
    load_c.wait()
    unit_gradients(r)
    norm2 = ChipSum(net, me, r.dn2, lambda i: r.dn2[i, k], bufs)
    steps = norm2.steps()
    gradient_rows(r, opposite(x))
    norm2.push("far")
    gradient_rows(r, up(x))
    norm2.push("above")
    next(steps)
    gradient_rows(r, down(x))
    norm2.push("below")
    gradient_rows(r, x)
    norm2.push("own")
    next(steps)

    act, dg, du = (ref[...].reshape(8 * ROWS, FPAD) for ref in (r.act, r.dg, r.du))

    def grads(i):
        wide = slice(i * 768, i * 768 + 768)
        left = r.x8[:, :, wide].reshape(8 * ROWS, 768).T
        r.g8[0, wide, :] = dot_nn(left, dg).astype(BF16)
        r.g8[1, wide, :] = dot_nn(left, du).astype(BF16)

    def grads_out(i):
        wide = slice(i * 768, i * 768 + 768)
        left = r.c8[:, :, wide].reshape(8 * ROWS, 768).T
        r.gd8[2 * i : 2 * i + 2] = (
            dot_nn(left, act).astype(BF16).reshape(2, 4, 2, PIECE, FPAD)
        )

    grads_out(0)
    grads_out(1)
    down_ring = reduce_ring(net, me, r.gd8, 0, 640, ring_bufs_d, r.gd.at[h])
    next(down_ring)
    next(steps)
    grads(0)
    grads(1)
    net.keep(r.g8, r.g)
    next(down_ring)
    d_norm2 = next(steps)
    hidden = r.hid[...]
    scale2 = rms(hidden)
    xh2 = hidden * scale2
    e2 = d_norm2 * r.gains[1:2, :]
    d_hidden = r.c8[x * 2 + k].astype(F32) + scale2 * (
        e2 - xh2 * jnp.mean(e2 * xh2, axis=-1, keepdims=True)
    )
    r.dh[...] = d_hidden
    r.gain[...] = jnp.sum(d_norm2 * xh2, axis=0, keepdims=True)
    r.dbr[t] = d_hidden.astype(BF16)
    branch = gather_block(net, me, r.dbr)
    next(branch)

    def one(j, carry):
        wide = tile(j, 384)
        right = r.wd[j].reshape(384, FPAD)
        r.out8[:, :, :, wide] = dot_nt(act, right).astype(BF16).reshape(4, 2, ROWS, 384)
        return carry

    lax.fori_loop(0, 2, one, 0)
    next(down_ring)
    lax.fori_loop(2, 4, one, 0)
    net.keep(r.out8, r.out)
    next(branch)
    next(down_ring)
    next(down_ring)
    for _ in branch:
        pass
    for _ in down_ring:
        pass
    r.gd[h] = ring_bufs_d[6][...]
    net.finish()


def mid(*arrays):
    shapes = (
        ((4, 2, ROWS, D), BF16),
        ((2, D, FPAD), BF16),
        ((2, PIECE, FPAD), BF16),
        ((4, ROWS, D), BF16),
        ((ROWS, D), F32),
        ((1, D), F32),
    )
    return call(
        mid_kernel,
        MID_IN,
        arrays,
        dict(zip(MID_OUT, shapes)),
        ("cot8", "w", "wdn", "out", "g"),
        scratch_of(MID_SCRATCH) + [pltpu.VMEM(*s) for s in CHIP_BUFS]
        + ring_bufs((), FPAD, 640)
        + semaphores(64, 64, 12),
        1,
        63,
        "mid",
    )


def columns_by_row(rows_ref, blocks, right, out):
    count = right.shape[0]
    for i in range(4):
        left = rows_ref[blocks, :, i * 384 : (i + 1) * 384].reshape(count, 384)
        out[i] = dot_tn(left, right).astype(BF16).reshape(out.shape[1:])


def attend_back(me, half, r, delta):
    begin = r.begin[half : half + 1, :]
    top = me.c

    def step(j, carry, last):
        keys = span_of(r.kv, j, 0)
        values = span_of(r.kv, j, 1)
        keys_t = keys.astype(F32).T.astype(BF16)
        allowed = mask_of(me, half, begin, j, last)
        d_keys = jnp.zeros((SPAN, HD), F32)
        d_values = jnp.zeros((SPAN, HD), F32)
        out = []
        for head in range(3):
            row = half * 3 + head
            query, d_out = r.q[half, head], r.dm[half, head]
            raw = dot_nt(keys, query) * ROOT2 - r.lse[row : row + 1, :]
            probs = jnp.exp2(jnp.where(allowed, raw, MASKED))
            d_probs = dot_nt(values, d_out)
            d_raw = (probs * (d_probs - delta[head])).astype(BF16)
            d_values = d_values + dot_nn(probs.astype(BF16), d_out)
            d_keys = d_keys + dot_nn(d_raw, query)
            out.append(carry[head] + dot_nn(keys_t, d_raw))
        at = pl.ds(2 * j, 2)
        r.dkv[at, 0] += d_keys.reshape(2, HALF, HD)
        r.dkv[at, 1] += d_values.reshape(2, HALF, HD)
        return tuple(out)

    zero = jnp.zeros((HD, HALF), F32)
    carry = step(top, (zero,) * 3, True)
    carry = lax.fori_loop(0, top, lambda i, carry: step(top - 1 - i, carry, False), carry)
    rows = slice(half * HALF, (half + 1) * HALF)
    cosine, sine = r.cos[rows, :], r.sin[rows, :]
    for head in range(3):
        back = carry[head].T * INV_ROOT
        back = back * cosine - pltpu.roll(back, HD // 2, 1) * sine
        r.dq[rows, head * HD : (head + 1) * HD] = back.astype(BF16)


def to_lines(ref, at, row):
    for i in range(row.shape[1] // HD):
        ref[pl.ds(at + i, 1), :] = row[:, i * HD : (i + 1) * HD]


class Total:
    def __init__(self, net, me, value, xb, yzb):
        self.net, self.me, self.xb, self.yzb = net, me, xb, yzb
        at = me.x * 2 + me.k
        xb[at] = value
        self.sent = []
        for j in range(4):
            for other in range(2):
                if j == 0 and other == 0:
                    continue
                core = me.k if other == 0 else 1 - me.k
                dev = me.chip(lax.rem(me.x + j, 4), core)
                self.sent.append(net.copy(xb.at[at], xb.at[at], dev))

    def second(self):
        net, me = self.net, self.me
        for made in self.sent:
            made.wait_recv()
        total = self.xb[0]
        for i in range(1, 8):
            total = total + self.xb[i]
        at = me.z * 4 + me.y
        self.yzb[at] = total
        self.sent = []
        for j in range(1, 16):
            z, y = lax.rem(me.z + j // 4, 4), lax.rem(me.y + j % 4, 4)
            piece = self.yzb.at[at]
            self.sent.append(net.copy(piece, piece, me.ring(z, y, me.h)))

    def final(self):
        for made in self.sent:
            made.wait_recv()
        total = self.yzb[0]
        for i in range(1, 16):
            total = total + self.yzb[i]
        return total


BACK_IN = ["outp", "gfeed", "dbr", "dh", "gain", "hid", "x", "small", "wo", "normed"]
BACK_IN += ["q", "kv", "att", "lse", "cos", "sin", "begin", "gains"]
BACK_OUT = ["result", "igrad", "gf", "gsm", "gpair", "total", "late"]
BACK_SCRATCH = {
    "v_small": ((4, 4, 2, PIECE, 640), BF16),
    "v_wo": ((4, 4, 2, PIECE, QW), BF16),
    "v_normed": ((4, ROWS, D), BF16),
    "v_dbr": ((4, ROWS, D), BF16),
    "v_outp": ((4, ROWS, D), BF16),
    "v_kv": ((16, 2, HALF, HD), BF16),
    "mixed": ((512, QW), BF16),
    "dm": ((2, 3, HALF, HD), BF16),
    "dq": ((512, QW), BF16),
    "dkv": ((16, 2, HALF, HD), F32),
    "k_send": ((8, 2, HALF, HD), BF16),
    "k_recv": ((8, 2, HALF, HD), BF16),
    "k_far": ((7, 2, HALF, HD), BF16),
    "dpair": ((HALF, 2 * HD), BF16),
    "part": ((4, ROWS, D), F32),
    "s1": ((2, ROWS, D), BF16),
    "r1": ((2, ROWS, D), BF16),
    "s2": ((ROWS, D), BF16),
    "r2": ((ROWS, D), BF16),
    "g_q": ((4, 4, 2, PIECE, QW), BF16),
    "g_o": ((4, 4, 2, PIECE, QW), BF16),
    "g_kv": ((4, 4, 2, PIECE, 2 * HD), BF16),
    "p_send": ((4, 4, 2, PIECE, 2 * HD), BF16),
    "p_recv": ((4, 4, 2, PIECE, 2 * HD), BF16),
    "l_q": ((PIECE, QW), BF16),
    "l_o": ((PIECE, QW), BF16),
    "l_kv": ((PIECE, 2 * HD), BF16),
    "kv_own": ((PIECE, 2 * HD), BF16),
    "kv_far": ((PIECE, 2 * HD), BF16),
    "tot": ((32, HD), F32),
    "t_x": ((8, 32, HD), F32),
    "t_yz": ((16, 32, HD), F32),
    "u_x": ((8, 16, HD), F32),
    "u_yz": ((16, 16, HD), F32),
    "u": ((16, HD), F32),
}


def back_kernel(*refs):
    names = BACK_IN + BACK_OUT + list(BACK_SCRATCH)
    r = Refs(names, refs)
    rest = refs[len(names) :]
    f0_bufs, f1_bufs, o_bufs, q_bufs, kv_bufs = (rest[16 * i : 16 * (i + 1)] for i in range(5))
    f0_loads, f1_loads, chip_bufs = rest[80:86], rest[86:92], rest[92:97]
    send, recv, local = rest[97:]
    me = Place()
    net = Net(send, recv, local)
    z, y, h, x, k, c, t = me.z, me.y, me.h, me.x, me.k, me.c, me.t
    load_dbr = net.here(r.dbr, r.v_dbr)
    load_wo = net.here(r.wo, r.v_wo)
    load_kv = net.here(r.kv, r.v_kv)
    load_normed = net.here(r.normed, r.v_normed)
    load_small = net.here(r.small, r.v_small)
    load_out = net.here(r.outp.at[:, k], r.v_outp)
    r.kv = r.v_kv
    barrier(
        [me.block(lax.rem(c + j, 8), k) for j in range(1, 8)]
        + [
            me.ring(lax.rem(z + j // 4, 4), lax.rem(y + j % 4, 4), h)
            for j in range(1, 16)
            if j // 4
        ]
        + [me.chip(lax.rem(x + j, 4), k) for j in range(1, 4)]
        + [me.chip(lax.rem(x + j, 4), 1 - k) for j in range(4)]
    )
    feed0 = reduce_ring(net, me, r.gfeed.at[0], 0, 640, f0_bufs, r.gf.at[h, 0], f0_loads)
    feed1 = reduce_ring(net, me, r.gfeed.at[1], 0, 640, f1_bufs, r.gf.at[h, 1], f1_loads)
    next(feed0)
    outs = ChipSum(net, me, r.outp, lambda i: r.v_outp[i], chip_bufs)
    for name in ("far", "above", "below", "own"):
        outs.push(name)
    out_steps = outs.steps()
    r.dkv[...] = jnp.zeros_like(r.dkv)
    r.tot[...] = jnp.zeros_like(r.tot)
    to_lines(r.tot, 0, r.gain[...])
    for half in range(2):
        for head in range(3):
            r.mixed[half * HALF : (half + 1) * HALF, head * HD : (head + 1) * HD] = r.att[
                half, head
            ].astype(BF16)
    load_wo.wait()
    load_dbr.wait()
    wo = r.v_wo[...].reshape(D, QW)
    d_mixed = dot_nn(r.v_dbr[...].reshape(512, D), wo)
    deltas = []
    for half in range(2):
        rows = slice(half * HALF, (half + 1) * HALF)
        for head in range(3):
            piece = d_mixed[rows, head * HD : (head + 1) * HD].astype(BF16)
            r.dm[half, head] = piece
            both = piece.astype(F32) * r.att[half, head]
            deltas.append(jnp.sum(both.T, axis=0, keepdims=True))
    load_out.wait()
    next(out_steps)
    load_kv.wait()
    attend_back(me, 1, r, deltas[3:])
    next(feed0)
    next(feed1)
    next(out_steps)
    attend_back(me, 0, r, deltas[:3])
    next(feed0)
    for p in range(8):
        r.k_send[p] = r.dkv[2 * p + 1 - k].astype(BF16)
    kx = net.copy(r.k_send, r.k_recv, me.core)
    next(out_steps)
    columns_by_row(r.v_dbr, slice(0, 4), r.mixed[...], r.g_o)
    ring_o = reduce_ring(net, me, r.g_o, 0, 256, o_bufs, r.l_o)
    kx.wait()
    for p in range(8):
        r.dkv[2 * p + k] += r.k_recv[p].astype(F32)
        r.k_send[p] = r.dkv[2 * p + k].astype(BF16)
    k_sent = []
    for i, j in enumerate((4, 3, 5, 2, 6, 1, 7)):
        there = lax.rem(c + j, 8)
        k_sent.append(net.copy(r.k_send.at[there], r.k_far.at[i], me.block(there, k)))
    load_normed.wait()
    load_small.wait()
    columns_by_row(r.v_normed, slice(0, 4), r.dq[...], r.g_q)
    ring_q = reduce_ring(net, me, r.g_q, 0, 256, q_bufs, r.l_q)
    next(ring_o)
    next(ring_q)
    next(feed1)
    next(feed0)
    to_lines(r.tot, 12 + 3 * t, jnp.sum(r.dq[...].astype(F32), axis=0, keepdims=True))
    wq = r.v_small[:, :, :, :, 0:QW].reshape(D, QW)
    for i in range(4):
        r.part[i] = dot_nt(r.dq[i * ROWS : (i + 1) * ROWS, :], wq)
    next(feed1)
    next(feed0)
    d_kv = r.dkv[2 * c + k]
    for i, made in enumerate(k_sent):
        made.wait_recv()
        d_kv = d_kv + r.k_far[i].astype(F32)
    half_rows = pl.ds(pl.multiple_of(k * HALF, HALF), HALF)
    cosine, sine = r.cos[half_rows, :], r.sin[half_rows, :]
    d_key = d_kv[0] * INV_ROOT
    r.dpair[:, 0:HD] = (d_key * cosine - pltpu.roll(d_key, HD // 2, 1) * sine).astype(BF16)
    r.dpair[:, HD : 2 * HD] = d_kv[1].astype(BF16)
    d_pair = r.dpair[...]
    wkv = r.v_small[:, :, :, :, QW:640].reshape(D, 2 * HD)
    for i in range(2):
        at = 2 * k + i
        r.part[at] = r.part[at] + dot_nt(d_pair[i * ROWS : (i + 1) * ROWS, :], wkv)
    norm1 = sum_block(net, me, r.part, r.s1, r.r1, r.s2, r.r2)
    next(norm1)
    columns_by_row(r.v_normed, pl.ds(2 * k, 2), d_pair, r.p_send)
    px = net.copy(r.p_send, r.p_recv, me.core)
    next(norm1)
    sums = jnp.sum(d_pair.astype(F32), axis=0, keepdims=True)
    to_lines(r.tot, 24 + me.xl, sums[:, :HD])
    to_lines(r.tot, 26 + me.xl, sums[:, HD:])
    px.wait_recv()
    r.g_kv[...] = (r.p_send[...].astype(F32) + r.p_recv[...].astype(F32)).astype(BF16)
    ring_kv = reduce_ring(net, me, r.g_kv, 0, HD, kv_bufs, r.l_kv)
    next(ring_kv)
    total = Total(net, me, r.tot[...], r.t_x, r.t_yz)
    next(ring_o)
    next(ring_q)
    next(feed1)
    d_norm1 = next(norm1)
    flat = r.x[...].astype(F32)
    scale1 = rms(flat)
    xh1 = flat * scale1
    gain = jnp.sum(d_norm1 * xh1, axis=0, keepdims=True)
    r.u[...] = jnp.zeros_like(r.u)
    to_lines(r.u, 0, gain)
    late = Total(net, me, r.u[...], r.u_x, r.u_yz)
    e1 = d_norm1 * r.gains[0:1, :]
    r.igrad[...] = r.dh[...] + scale1 * (
        e1 - xh1 * jnp.mean(e1 * xh1, axis=-1, keepdims=True)
    )
    total.second()
    next(ring_kv)
    next(ring_o)
    next(ring_q)
    result = r.hid[...] + next(out_steps)
    r.result[...] = result.astype(BF16)
    late.second()
    next(feed1)
    next(ring_kv)
    next(ring_o)
    next(ring_q)
    next(ring_kv)
    r.total[...] = total.final()
    for ring in (ring_o, ring_q, ring_kv):
        for _ in ring:
            pass
    r.late[...] = late.final()
    su_q, su_o, su_kv = q_bufs[6], o_bufs[6], kv_bufs[6]
    pair_own = su_kv[...].astype(F32) + r.l_kv[...].astype(F32)
    r.kv_own[...] = pair_own.astype(BF16)
    pair_sent = net.copy(r.kv_own, r.kv_far, me.side)
    r.gsm[:, 0:QW] = su_q[...].astype(F32) + r.l_q[...].astype(F32)
    r.gsm[:, QW:] = su_o[...].astype(F32) + r.l_o[...].astype(F32)
    for ring in (feed0, feed1):
        for _ in ring:
            pass
    r.gf[h, 0] = f0_bufs[6][...]
    r.gf[h, 1] = f1_bufs[6][...]
    pair_sent.wait_recv()
    pieces = (r.kv_own[...].astype(F32), r.kv_far[...].astype(F32))
    for i, at in enumerate((me.xl, 1 - me.xl)):
        r.gpair[:, pl.ds(pl.multiple_of(at * HD, HD), HD)] = pieces[i][:, :HD]
        r.gpair[:, pl.ds(pl.multiple_of((2 + at) * HD, HD), HD)] = pieces[i][:, HD:]

    net.finish((kx,))


def back(*arrays):
    shapes = (
        ((ROWS, D), BF16),
        ((ROWS, D), F32),
        ((2, 2, PIECE, FPAD), BF16),
        ((PIECE, 2 * QW), F32),
        ((PIECE, 4 * HD), F32),
        ((32, HD), F32),
        ((16, HD), F32),
    )
    return call(
        back_kernel,
        BACK_IN,
        arrays,
        dict(zip(BACK_OUT, shapes)),
        ("outp", "gfeed", "dbr", "small", "wo", "normed", "kv"),
        scratch_of(BACK_SCRATCH)
        + ring_bufs((), FPAD, 640)
        + ring_bufs((), FPAD, 640)
        + ring_bufs((), QW, 256)
        + ring_bufs((), QW, 256)
        + ring_bufs((), 2 * HD, HD)
        + [pltpu.VMEM((n, PIECE, FPAD), BF16) for n in (2, 2, 4)] * 4
        + [pltpu.VMEM(*s) for s in CHIP_BUFS]
        + semaphores(230, 230, 20),
        2,
        63,
        "back",
    )


def prep_kernel(lengths, wq, wp, wo, wf, biases, p1, po, p2, pd, bias, cos, sin, begin):
    me = Place()
    p1[:, 0:QW] = wq[...].astype(BF16)
    for i in range(2):
        at = pl.ds(pl.multiple_of(i * KV * HD + me.xl * HD, HD), HD)
        to = slice(QW + i * HD, QW + (i + 1) * HD)
        p1[:, to] = wp[:, at].astype(BF16)
        at = pl.ds(pl.multiple_of(HQ * HD + i * KV * HD + me.xl * HD, HD), HD)
        bias[:, to] = biases[:, at]
    bias[:, 0:QW] = biases[:, pl.ds(pl.multiple_of(me.t * QW, HD), QW)]
    po[...] = wo[...].astype(BF16)
    rest = FCOLS - FPAD
    for m in range(3):
        first, second = (p2.at[0, m], p2.at[1, m]) if m < 2 else (pd.at[0], pd.at[1])
        first[...] = wf[m, :, 0:FPAD].astype(BF16)
        tail = wf[m, :, FPAD:FCOLS].astype(BF16)
        second[...] = jnp.concatenate([tail, jnp.zeros((PIECE, FPAD - rest), BF16)], axis=1)

    def starts(index):
        end, found = lengths[0, 0], jnp.zeros_like(index)
        for i in range(3):
            found = jnp.where(index >= end, end, found)
            end = end + lengths[0, i + 1]
        return found

    first = me.c * 512
    along = lax.broadcasted_iota(jnp.int32, (2, HALF), 1)
    along = along + lax.broadcasted_iota(jnp.int32, (2, HALF), 0) * HALF + first
    begin[...] = starts(along)
    down_rows = lax.broadcasted_iota(jnp.int32, (512, HD), 0) + first
    position = (down_rows - starts(down_rows)).astype(F32)
    lane = lax.broadcasted_iota(jnp.int32, (512, HD), 1)
    steps = lax.rem(lane, HD // 2).astype(F32)
    angle = position * jnp.exp(-(2.0 * steps / HD) * math.log(ROPE_BASE))
    cos[...] = jnp.cos(angle)
    turned = jnp.sin(angle)
    sin[...] = jnp.where(lane < HD // 2, -turned, turned)


def prep(lengths, wq, wp, wo, wf, biases):
    shape = jax.ShapeDtypeStruct
    vmem = pl.BlockSpec(memory_space=pltpu.VMEM)
    return pl.pallas_call(
        prep_kernel,
        out_shape=(
            shape((PIECE, 640), BF16),
            shape((PIECE, QW), BF16),
            shape((2, 2, PIECE, FPAD), BF16),
            shape((2, PIECE, FPAD), BF16),
            shape((1, 640), F32),
            shape((512, HD), F32),
            shape((512, HD), F32),
            shape((2, HALF), jnp.int32),
        ),
        in_specs=[pl.BlockSpec(memory_space=pltpu.SMEM)] + [vmem] * 5,
        out_specs=(vmem,) * 8,
        compiler_params=pltpu.CompilerParams(vmem_limit_bytes=63 * 2**20),
        name="prep",
    )(lengths, wq, wp, wo, wf, biases)


def adamw(weight, mean_old, square_old, grad, rate, decay):
    mean_new = BETA_ONE * mean_old + (1.0 - BETA_ONE) * grad
    square_new = BETA_TWO * square_old + (1.0 - BETA_TWO) * grad * grad
    mean_hat = mean_new / (1.0 - BETA_ONE**STEP)
    square_hat = square_new / (1.0 - BETA_TWO**STEP)
    weight_new = weight - rate * (mean_hat / (jnp.sqrt(square_hat) + ADAM_EPS) + decay * weight)
    return (mean_new, square_new, weight_new)


RATES = {
    "query": (0.05, 0.1),
    "pair": (3.0 / math.sqrt(D), 0.1),
    "output": (3.0 / math.sqrt(max(HQ * HD // 256, 1)), 0.1),
    "feed": (0.05, 0.1),
    "gains": (1.5, 0.0),
    "biases": (0.5, 0.0),
}
STATE_SHAPES = {
    "query": (PIECE, QW),
    "pair": (PIECE, 2 * KV * HD),
    "output": (PIECE, QW),
    "feed": (3, PIECE, FCOLS),
    "gains": (2, D),
    "biases": (16, HD),
}


def as_row(ref, at):
    return jnp.concatenate([ref[at + i : at + i + 1, :] for i in range(D // HD)], axis=1)


def update_kernel(result, igrad, gf, gsm, gpair, total, late, gd, *refs):
    state, (result_out, igrad_out), news = refs[:18], refs[18:20], refs[20:]

    def update(i, name, grad, at=Ellipsis):
        olds = [ref[at] for ref in state[3 * i : 3 * i + 3]]
        for ref, new in zip(news[3 * i : 3 * i + 3], adamw(*olds, grad, *RATES[name])):
            ref[at] = new

    for lanes, at in ((slice(0, FPAD), 0), (slice(FPAD, FCOLS), 1)):
        some = slice(0, lanes.stop - lanes.start)
        grad = jnp.where(pl.program_id(0) == 2, gd[at, :, some], gf[at, 0, :, some]).astype(F32)
        update(3, "feed", grad, (0, slice(None), lanes))

    @pl.when(pl.program_id(0) == 0)
    def _():
        result_out[...] = result[...]
        igrad_out[...] = igrad[...]
        update(0, "query", gsm[:, 0:QW])
        update(1, "pair", gpair[...])
        update(2, "output", gsm[:, QW : 2 * QW])
        update(4, "gains", jnp.concatenate([as_row(late, 0), as_row(total, 0)], axis=0))
        update(5, "biases", total[12:28, :])


def update_all(grads, state):
    def whole(shape):
        return pl.BlockSpec(shape, lambda i: (0,) * len(shape))

    feed_grad = pl.BlockSpec((2, 1, PIECE, FPAD), lambda i: (0, lax.min(i, 1), 0, 0))
    feed = pl.BlockSpec((1, PIECE, FCOLS), lambda i: (i, 0, 0))
    grad_specs = [feed_grad if a.ndim == 4 else whole(a.shape) for a in grads]
    specs = []
    for name, shape in STATE_SHAPES.items():
        specs += [feed if name == "feed" else whole(shape)] * 3
    rows = [jax.ShapeDtypeStruct((ROWS, D), BF16), jax.ShapeDtypeStruct((ROWS, D), F32)]
    return pl.pallas_call(
        update_kernel,
        grid=(3,),
        out_shape=rows + [jax.ShapeDtypeStruct(s, F32) for s in STATE_SHAPES.values() for _ in range(3)],
        in_specs=grad_specs + specs,
        out_specs=[whole((ROWS, D))] * 2 + specs,
        compiler_params=pltpu.CompilerParams(vmem_limit_bytes=63 * 2**20),
        name="update",
    )(*grads, *state)


def body(
    inputs,
    cotangent,
    lengths,
    query_weight,
    query_mean,
    query_square,
    pair_weight,
    pair_mean,
    pair_square,
    output_weight,
    output_mean,
    output_square,
    feed_weight,
    feed_mean,
    feed_square,
    gains,
    gains_mean,
    gains_square,
    biases,
    biases_mean,
    biases_square,
):
    feeds = [a.transpose(1, 0, 2) for a in (feed_weight, feed_mean, feed_square)]
    p1, po, p2, pd, bias, cosine, sine, begin = prep(
        lengths, query_weight, pair_weight, output_weight, feeds[0], biases.reshape(1, QKV)
    )
    feed, wd, small, wo, normed, q, kv, att, lse, hid, n2, cot8 = front(
        inputs, cotangent, gains, bias, cosine, sine, begin, p1, po, p2, pd
    )
    out, g_feed, g_down, dbr, dh, gain = mid(n2, cot8, feed.reshape(2, D, FPAD), wd, hid, gains)
    grads = back(
        out,
        g_feed.reshape(2, 4, 4, 2, PIECE, FPAD),
        *(dbr, dh, gain, hid, inputs, small, wo, normed),
        *(q, kv, att, lse, cosine, sine, begin, gains),
    )
    lines = lambda *arrays: [a.reshape(-1, HD) for a in arrays]
    made = list(update_all(
        (*grads, g_down),
        [query_weight, query_mean, query_square]
        + [pair_weight, pair_mean, pair_square]
        + [output_weight, output_mean, output_square]
        + feeds
        + [gains, gains_mean, gains_square]
        + lines(biases, biases_mean, biases_square),
    ))
    made[11:14] = [a.transpose(1, 0, 2) for a in made[11:14]]
    made[17:20] = [a.reshape(QKV) for a in made[17:20]]
    return tuple(made)


def solution(mesh):
    mesh = Mesh(mesh.devices.reshape(4, 4, 2, 4), AXES)
    rows = P(("dp", "y", "xh", "tensor"), None)
    cut = P(("dp", "y", "xh"), "tensor")
    pair = P(("dp", "y", "xh"), None)
    feed = P(("dp", "y", "xh"), None, "tensor")
    whole = P()
    in_specs = (rows, rows, P("dp", None))
    in_specs += (cut,) * 3 + (pair,) * 3 + (cut,) * 3 + (feed,) * 3 + (whole,) * 6
    out_specs = (rows, rows) + (cut,) * 3 + (pair,) * 3 + (cut,) * 3 + (feed,) * 3 + (whole,) * 6
    return jax.shard_map(body, mesh=mesh, in_specs=in_specs, out_specs=out_specs, check_vma=False)
```

```python
import math

import jax
import jax.numpy as jnp
from jax import lax
from jax.experimental import pallas as pl
from jax.experimental.pallas import tpu as pltpu
from jax.sharding import Mesh
from jax.sharding import PartitionSpec as P

D = 1536
HQ = 12
KV = 2
HD = 128
FF = 8960
STEP = 10
QKV = 2048
ROWS = 128
HALF = 256
GROUP = 4096
PIECE = 48
FCOLS = 2240
FPAD = 1152
QW = 384
SMALL = 1024
SPAN = 512

NORM_EPS = 1e-06
ROPE_BASE = 1000000.0
BETA_ONE = 0.9
BETA_TWO = 0.95
ADAM_EPS = 1e-08
MASKED = -1e30
LOG2E = math.log2(math.e)
ROOT2 = LOG2E / math.sqrt(HD)
INV_ROOT = 1.0 / math.sqrt(HD)

MESH_ID = pl.DeviceIdType.MESH
BF16 = jnp.bfloat16
F32 = jnp.float32
AXES = ("dp", "y", "xh", "tensor")


def up(v):
    return lax.rem(v + 1, 4)


def down(v):
    return lax.rem(v + 3, 4)


def opposite(v):
    return lax.rem(v + 2, 4)


def dot_nn(a, b):
    return lax.dot_general(a, b, (((1,), (0,)), ((), ())), preferred_element_type=F32)


def dot_nt(a, b):
    return lax.dot_general(a, b, (((1,), (1,)), ((), ())), preferred_element_type=F32)


def dot_tn(a, b):
    return lax.dot_general(a, b, (((0,), (0,)), ((), ())), preferred_element_type=F32)


class Place:
    def __init__(self):
        self.z = lax.axis_index("dp")
        self.y = lax.axis_index("y")
        self.h = lax.axis_index("xh")
        self.t = lax.axis_index("tensor")
        self.xl = self.t // 2
        self.k = lax.rem(self.t, 2)
        self.x = self.h * 2 + self.xl
        self.c = self.y * 2 + self.h

    def ring(self, z, y, h):
        return (z, y, h, self.t)

    def chip(self, x, k):
        return (self.z, self.y, x // 2, lax.rem(x, 2) * 2 + k)

    def block(self, c, k):
        return (self.z, c // 2, lax.rem(c, 2), self.xl * 2 + k)

    @property
    def core(self):
        return (self.z, self.y, self.h, self.xl * 2 + 1 - self.k)

    @property
    def side(self):
        return (self.z, self.y, self.h, (1 - self.xl) * 2 + self.k)


class Net:
    def __init__(self, send, recv, local):
        self.send, self.recv, self.local = send, recv, local
        self.n, self.m = 0, 0
        self.started, self.kept, self.maybe = [], [], []

    def make(self, src, dst, dev):
        i = self.n
        self.n += 1
        return pltpu.make_async_remote_copy(
            src_ref=src,
            dst_ref=dst,
            send_sem=self.send.at[i],
            recv_sem=self.recv.at[i],
            device_id=dev,
            device_id_type=MESH_ID,
        )

    def copy(self, src, dst, dev):
        made = self.make(src, dst, dev)
        made.start()
        self.started.append(made)
        return made

    def copy_if(self, wanted, src, dst, dev):
        made = self.make(src, dst, dev)

        @pl.when(wanted)
        def _():
            made.start()

        self.maybe.append((wanted, made))
        return made

    def here(self, src, dst):
        made = pltpu.make_async_copy(src, dst, self.local.at[self.m])
        self.m += 1
        made.start()
        return made

    def keep(self, src, dst):
        self.kept.append(self.here(src, dst))

    def finish(self, done=()):
        for made in self.started:
            if all(made is not other for other in done):
                made.wait_send()
        for made in self.kept:
            made.wait()
        for wanted, made in self.maybe:
            pl.when(wanted)(made.wait_send)


def barrier(devices):
    sem = pltpu.get_barrier_semaphore()
    for dev in devices:
        pl.semaphore_signal(sem, inc=1, device_id=dev, device_id_type=MESH_ID)
    pl.semaphore_wait(sem, len(devices))


def gather_ring(net, me, own, other, out, lead, lanes, near=True, far=True):
    z, y, h = me.z, me.y, me.h
    g = 1 - h
    low, high = lanes
    every = slice(None)

    def at(z, y, h, lane=None):
        index = [every] * lead + [z, y, h]
        if lane is not None:
            index += [every, lane]
        return out.at[tuple(index)]

    def same(piece, dev):
        return net.copy(piece, piece, dev)

    waits_a, waits_b = [], []
    if near:
        x = net.copy(other, at(z, y, h), me.ring(z, y, g))
        a_up = net.copy(own, at(z, y, h), me.ring(z, up(y), h))
        a_down = net.copy(own, at(z, y, h), me.ring(z, down(y), h))
        kept = net.here(own, at(z, y, h))
        yield
        x.wait_recv()
        b_up = same(at(z, y, g), me.ring(up(z), y, h))
        b_down = same(at(z, y, g), me.ring(down(z), y, h))
        yield
        a_up.wait_recv()
        a2_up = same(at(z, down(y), h, low), me.ring(z, up(y), h))
        a_down.wait_recv()
        a2_down = same(at(z, up(y), h, high), me.ring(z, down(y), h))
        yield
        b_up.wait_recv()
        b2_up = same(at(down(z), y, g, low), me.ring(up(z), y, h))
        b_down.wait_recv()
        b2_down = same(at(up(z), y, g, high), me.ring(down(z), y, h))
        yield
        kept.wait()
        waits_a, waits_b = [a2_up, a2_down], [b2_up, b2_down]
    for made in waits_a:
        made.wait_recv()
    if far:
        c_up = same(at(z, every, h), me.ring(up(z), y, h))
        c_down = same(at(z, every, h), me.ring(down(z), y, h))
        yield
    for made in waits_b:
        made.wait_recv()
    if far:
        d_up = same(at(every, y, g), me.ring(z, up(y), h))
        d_down = same(at(every, y, g), me.ring(z, down(y), h))
        yield
        c_up.wait_recv()
        c2_up = same(at(down(z), slice(0, 2), h), me.ring(up(z), y, h))
        c_down.wait_recv()
        c2_down = same(at(up(z), slice(2, 4), h), me.ring(down(z), y, h))
        yield
        d_up.wait_recv()
        d2_up = same(at(slice(0, 2), down(y), g), me.ring(z, up(y), h))
        d_down.wait_recv()
        d2_down = same(at(slice(2, 4), up(y), g), me.ring(z, down(y), h))
        yield
        for made in (c2_up, c2_down, d2_up, d2_down):
            made.wait_recv()


def gather_direct(net, me, own, other, out):
    z, y, h = me.z, me.y, me.h
    g = 1 - h
    others = (2, 1, 3)

    def along_y(src, dst):
        return [net.copy(src, dst, me.ring(z, lax.rem(y + j, 4), h)) for j in others]

    def along_z(src, dst):
        return [net.copy(src, dst, me.ring(lax.rem(z + j, 4), y, h)) for j in others]

    x = net.copy(other, out.at[z, y, h], me.ring(z, y, g))
    a = along_y(own, out.at[z, y, h])
    kept = net.here(own, out.at[z, y, h])
    yield
    x.wait_recv()
    b = along_z(out.at[z, y, g], out.at[z, y, g])
    for made in a:
        made.wait_recv()
    kept.wait()
    line = out.at[z, :, h]
    c = along_z(line, line)
    yield
    for made in b:
        made.wait_recv()
    line = out.at[:, y, g]
    d = along_y(line, line)
    yield
    for made in c + d:
        made.wait_recv()


def gather_chips(net, me, buf):
    x, k = me.x, me.k
    first, last = slice(0, ROWS // 2), slice(ROWS // 2, ROWS)

    def send(x_at, rows, dev):
        piece = buf.at[x_at * 2 + k] if rows is None else buf.at[x_at * 2 + k, rows]
        return net.copy(piece, piece, dev)

    to_up, to_down = me.chip(up(x), k), me.chip(down(x), k)
    c0 = send(x, None, me.core)
    a1 = send(x, first, to_up)
    b1 = send(x, last, to_down)
    a2 = send(x, last, to_up)
    b2 = send(x, first, to_down)
    yield
    c0.wait_recv()
    yield
    a1.wait_recv()
    f1 = send(down(x), first, to_up)
    b1.wait_recv()
    f2 = send(up(x), last, to_down)
    yield
    a2.wait_recv()
    g1 = send(down(x), None, me.core)
    b2.wait_recv()
    g2 = send(up(x), None, me.core)
    yield
    g1.wait_recv()
    g2.wait_recv()
    yield
    f1.wait_recv()
    f2.wait_recv()
    g3 = send(opposite(x), None, me.core)
    yield
    g3.wait_recv()


def gather_block(net, me, buf):
    own = buf.at[me.t]
    far = buf.at[(1 - me.xl) * 2 + me.k]
    b = net.copy(own, own, me.side)
    a = net.copy(own, own, me.core)
    yield
    b.wait_recv()
    c = net.copy(far, far, me.core)
    yield
    a.wait_recv()
    c.wait_recv()


def sum_block(net, me, part, s1, r1, s2, r2, make=None):
    far, near, k = 1 - me.xl, me.xl, me.k
    sent = []
    for i in (far, near):
        if make is not None:
            make(i)
        s1[i] = part[i * 2 + 1 - k].astype(BF16)
        sent.append(net.copy(s1.at[i], r1.at[i], me.core))
    yield None
    sent[0].wait_recv()
    s2[...] = (part[far * 2 + k] + r1[far].astype(F32)).astype(BF16)
    last = net.copy(s2, r2, me.side)
    yield None
    sent[1].wait_recv()
    total = part[me.t] + r1[near].astype(F32)
    last.wait_recv()
    yield total + r2[...].astype(F32)


def rms(v):
    return lax.rsqrt(jnp.mean(v * v, axis=-1, keepdims=True) + NORM_EPS)


def spin(v, cosine, sine):
    return v * cosine + pltpu.roll(v, HD // 2, 1) * sine


def half_start(me, half):
    return me.c * 512 + half * HALF


def mask_of(me, half, begin, j, last):
    key = lax.broadcasted_iota(jnp.int32, (SPAN, HALF), 0) + j * SPAN
    allowed = key >= begin
    if last:
        query = lax.broadcasted_iota(jnp.int32, (SPAN, HALF), 1) + half_start(me, half)
        allowed = allowed & (key <= query)
    return allowed


def span_of(kv_ref, j, which):
    return kv_ref[pl.ds(2 * j, 2), which].reshape(SPAN, HD)


def attend(me, half, q_ref, kv_ref, begin_ref, att_ref, lse_ref):
    begin = begin_ref[half : half + 1, :]
    top = me.c

    def step(j, carry, last):
        keys = span_of(kv_ref, j, 0)
        values = span_of(kv_ref, j, 1).astype(F32).T.astype(BF16)
        allowed = mask_of(me, half, begin, j, last)
        out = []
        for head in range(3):
            high, total, summed = carry[head]
            raw = dot_nt(keys, q_ref[half, head]) * ROOT2
            raw = jnp.where(allowed, raw, MASKED)
            new = jnp.maximum(high, jnp.max(raw, axis=0, keepdims=True))
            probs = jnp.exp2(raw - new)
            fade = jnp.exp2(high - new)
            total = total * fade + jnp.sum(probs, axis=0, keepdims=True)
            summed = summed * fade + dot_nn(values, probs.astype(BF16))
            out.append((new, total, summed))
        return tuple(out)

    zero = (
        jnp.full((1, HALF), MASKED, F32),
        jnp.zeros((1, HALF), F32),
        jnp.zeros((HD, HALF), F32),
    )
    carry = step(top, (zero,) * 3, True)
    carry = lax.fori_loop(0, top, lambda i, carry: step(top - 1 - i, carry, False), carry)
    for head in range(3):
        high, total, summed = carry[head]
        att_ref[half, head] = (summed / total).T
        lse_ref[half * 3 + head : half * 3 + head + 1, :] = high + jnp.log2(total)

class Refs:
    def __init__(self, names, refs):
        for name, ref in zip(names, refs):
            setattr(self, name, ref)


class ChipSum:
    def __init__(self, net, me, src, mine, bufs):
        self.net, self.me, self.src, self.mine = net, me, src, mine
        self.r1, self.a1, self.a2, self.ru, self.rd = bufs
        self.pushed = {}
        x = me.x
        self.order = {"far": opposite(x), "above": up(x), "below": down(x), "own": x}

    def push(self, name):
        i = self.order[name]
        self.pushed[name] = self.net.copy(
            self.src.at[i, 1 - self.me.k], self.r1.at[i], self.me.core
        )

    def add(self, name):
        i = self.order[name]
        self.pushed[name].wait_recv()
        self.r1[i] = (self.r1[i].astype(F32) + self.mine(i).astype(F32)).astype(BF16)
        return i

    def steps(self):
        net, me = self.net, self.me
        r1, a1, a2, ru, rd = self.r1, self.a1, self.a2, self.ru, self.rd
        first, last = slice(0, ROWS // 2), slice(ROWS // 2, ROWS)
        to_up, to_down = me.chip(up(me.x), me.k), me.chip(down(me.x), me.k)
        far = self.add("far")
        e1 = net.copy(r1.at[far, first], a1, to_up)
        e2 = net.copy(r1.at[far, last], a2, to_down)
        yield None
        above = self.add("above")
        e3 = net.copy(r1.at[above, last], ru.at[last], to_up)
        yield None
        below = self.add("below")
        e4 = net.copy(r1.at[below, first], rd.at[first], to_down)
        yield None
        x = self.add("own")
        e1.wait_recv()
        a1[...] = (a1[...].astype(F32) + r1[above, first].astype(F32)).astype(BF16)
        e5 = net.copy(a1, ru.at[first], to_up)
        e2.wait_recv()
        a2[...] = (a2[...].astype(F32) + r1[below, last].astype(F32)).astype(BF16)
        e6 = net.copy(a2, rd.at[last], to_down)
        yield None
        for made in (e3, e4, e5, e6):
            made.wait_recv()
        yield r1[x].astype(F32) + ru[...].astype(F32) + rd[...].astype(F32)


CHIP_BUFS = [
    ((4, ROWS, D), BF16),
    ((ROWS // 2, D), BF16),
    ((ROWS // 2, D), BF16),
    ((ROWS, D), BF16),
    ((ROWS, D), BF16),
]


FRONT_IN = ["x", "cot", "gains", "bias", "cos", "sin", "begin", "p1", "po", "p2", "pd"]
FRONT_OUT = ["feed", "wd", "o_small", "o_wo", "o_normed", "o_q", "o_kv", "o_att"]
FRONT_OUT += ["lse", "hid", "n2", "cot8"]
FRONT_SCRATCH = {
    "small": ((4, 4, 2, PIECE, 640), BF16),
    "wo": ((4, 4, 2, PIECE, QW), BF16),
    "normed": ((4, ROWS, D), BF16),
    "q": ((2, 3, HALF, HD), BF16),
    "kv": ((16, 2, HALF, HD), BF16),
    "att": ((2, 3, HALF, HD), F32),
    "cs": ((8, ROWS, D), BF16),
    "part": ((4, ROWS, D), F32),
    "s1": ((2, ROWS, D), BF16),
    "r1": ((2, ROWS, D), BF16),
    "s2": ((ROWS, D), BF16),
    "r2": ((ROWS, D), BF16),
}


def front_kernel(*refs):
    names = FRONT_IN + FRONT_OUT + list(FRONT_SCRATCH)
    r = Refs(names, refs)
    send, recv, local = refs[len(names) :]
    me = Place()
    net = Net(send, recv, local)
    z, y, h, x, k, c = me.z, me.y, me.h, me.x, me.k, me.c
    slot = x * 2 + k
    barrier(
        [me.block(lax.rem(c + j, 8), k) for j in range(1, 8)]
        + [me.ring(lax.rem(z + j, 4), y, h) for j in (1, 2, 3)]
        + [me.chip(up(x), k), me.chip(down(x), k), me.core]
    )
    ring = gather_direct(net, me, r.p1, r.p1, r.small)
    next(ring)
    r.cs[slot] = r.cot[...]
    own = r.x[...].astype(F32)
    r.normed[me.t] = (own * rms(own) * r.gains[0:1, :]).astype(BF16)
    block = gather_block(net, me, r.normed)
    next(block)
    next(ring)
    feed = gather_ring(
        net, me, r.p2.at[h], r.p2.at[1 - h], r.feed, 1, (slice(0, 640), slice(640, FPAD))
    )
    lanes = (slice(0, 640), slice(640, FPAD))
    down_near = gather_ring(net, me, r.pd.at[h], r.pd.at[1 - h], r.wd, 0, lanes, far=False)
    outer = gather_direct(net, me, r.po, r.po, r.wo)
    next(ring)
    next(feed)
    next(block)
    for _ in block:
        pass
    for _ in ring:
        pass
    net.keep(r.small, r.o_small)
    net.keep(r.normed, r.o_normed)
    normed = r.normed[...].reshape(512, D)
    cosine, sine = r.cos[...], r.sin[...]
    proj = dot_nn(normed, r.small[:, :, :, :, QW:640].reshape(D, 2 * HD)) + r.bias[:, QW:640]
    keys = spin(proj[:, :HD], cosine, sine).astype(BF16)
    values = proj[:, HD:].astype(BF16)
    for half in range(2):
        rows = slice(half * HALF, (half + 1) * HALF)
        r.kv[2 * c + half, 0] = keys[rows]
        r.kv[2 * c + half, 1] = values[rows]
    own_kv = r.kv.at[2 * c + k]
    order = (4, 3, 5, 2, 6, 1, 7)
    kv_sent = [
        net.copy_if(c + j < 8, own_kv, own_kv, me.block(lax.rem(c + j, 8), k)) for j in order
    ]
    next(outer)
    proj = dot_nn(normed, r.small[:, :, :, :, 0:QW].reshape(D, QW)) + r.bias[:, 0:QW]
    for head in range(3):
        query = spin(proj[:, head * HD : (head + 1) * HD], cosine, sine).astype(BF16)
        r.q[0, head] = query[:HALF]
        r.q[1, head] = query[HALF:]
    net.keep(r.q, r.o_q)
    next(feed)
    next(feed)
    next(outer)
    next(feed)
    next(feed)
    next(feed)
    passed = []
    for j, made in zip(order, kv_sent):
        pl.when(c >= j)(made.wait_recv)
        there = r.kv.at[2 * lax.rem(c + 8 - j, 8) + k]
        passed.append(net.copy_if(c >= j, there, there, me.core))
    cots = gather_chips(net, me, r.cs)
    next(cots)
    next(outer)
    for j, made in zip(order, passed):
        pl.when(c >= j)(made.wait_recv)
    net.keep(r.kv, r.o_kv)
    next(down_near)
    attend(me, 0, r.q, r.kv, r.begin, r.att, r.lse)
    next(down_near)
    next(cots)
    next(cots)
    attend(me, 1, r.q, r.kv, r.begin, r.att, r.lse)
    next(down_near)
    next(down_near)
    next(feed)
    net.keep(r.att, r.o_att)
    next(cots)
    for _ in outer:
        pass
    net.keep(r.wo, r.o_wo)

    def project(half):
        mixed = jnp.concatenate([r.att[half, head].astype(BF16) for head in range(3)], axis=1)
        r.part[pl.ds(2 * half, 2)] = dot_nt(mixed, r.wo[...].reshape(D, QW)).reshape(2, ROWS, D)

    summed = sum_block(net, me, r.part, r.s1, r.r1, r.s2, r.r2, project)
    next(summed)
    next(cots)
    next(cots)
    next(summed)
    next(feed)
    for _ in down_near:
        pass
    for _ in cots:
        pass
    net.keep(r.cs, r.cot8)
    branch = next(summed)
    hidden = own + branch
    r.hid[...] = hidden
    r.n2[...] = (hidden * rms(hidden) * r.gains[1:2, :]).astype(BF16)
    for _ in feed:
        pass
    net.finish()


def call(kernel, ins, arrays, outs, far, scratch, collective, limit, name):
    vmem = pl.BlockSpec(memory_space=pltpu.VMEM)
    hbm = pl.BlockSpec(memory_space=pl.ANY)
    return pl.pallas_call(
        kernel,
        out_shape=tuple(jax.ShapeDtypeStruct(*s) for s in outs.values()),
        in_specs=[hbm if n in far else vmem for n in ins],
        out_specs=tuple(hbm if n in far else vmem for n in outs),
        scratch_shapes=scratch,
        compiler_params=pltpu.CompilerParams(
            collective_id=collective, has_side_effects=True, vmem_limit_bytes=limit * 2**20
        ),
        name=name,
    )(*arrays)


def semaphores(*counts):
    return [pltpu.SemaphoreType.DMA((n,)) for n in counts]


def scratch_of(shapes):
    return [pltpu.VMEM(*s) for s in shapes.values()]


def front(*arrays):
    shapes = (
        ((2, 4, 4, 2, PIECE, FPAD), BF16),
        ((4, 4, 2, PIECE, FPAD), BF16),
        ((4, 4, 2, PIECE, 640), BF16),
        ((4, 4, 2, PIECE, QW), BF16),
        ((4, ROWS, D), BF16),
        ((2, 3, HALF, HD), BF16),
        ((16, 2, HALF, HD), BF16),
        ((2, 3, HALF, HD), F32),
        ((8, HALF), F32),
        ((ROWS, D), F32),
        ((ROWS, D), BF16),
        ((8, ROWS, D), BF16),
    )
    return call(
        front_kernel,
        FRONT_IN,
        arrays,
        dict(zip(FRONT_OUT, shapes)),
        ("p2", "pd", "feed", "wd", "cot8", *FRONT_OUT[2:8]),
        scratch_of(FRONT_SCRATCH) + semaphores(110, 110, 16),
        0,
        63,
        "front",
    )


def ring_sum(net, pick, here, to_up, to_down, cut, add, a1, a2, ru, rd, terms=None):
    above, below, far = up(here), down(here), opposite(here)
    if terms is None:
        terms = (pick(above, 0), pick(below, 1))
    e1 = net.copy(pick(far, 0), a1, to_up)
    e2 = net.copy(pick(far, 1), a2, to_down)
    e3 = net.copy(pick(above, 1), cut(ru, 1), to_up)
    e4 = net.copy(pick(below, 0), cut(rd, 0), to_down)
    yield
    e1.wait_recv()
    add(a1, terms[0])
    e5 = net.copy(a1, cut(ru, 0), to_up)
    e2.wait_recv()
    add(a2, terms[1])
    e6 = net.copy(a2, cut(rd, 1), to_down)
    yield
    for made in (e3, e4, e5, e6):
        made.wait_recv()


def add_pieces(lead):
    def add(dst, *srcs):
        count = math.prod(dst.shape[:-2])
        inner = dst.shape[lead] if len(dst.shape) > lead + 2 else 1

        def one(i, carry):
            if len(dst.shape) == 2:
                at = (slice(None), slice(None))
            elif len(dst.shape) == 3:
                at = (i,)
            else:
                at = (i // inner, lax.rem(i, inner))
            total = dst[at].astype(F32)
            for src in srcs:
                total = total + src[at].astype(F32)
            dst[at] = total.astype(dst.dtype)
            return carry

        if count == 1:
            one(0, 0)
        else:
            lax.fori_loop(0, count, one, 0)

    return add


RING_BUFS = ("a1", "a2", "ru", "rd", "b1", "b2", "su", "sd")


def ring_bufs(lead, width, low):
    pair = (*lead, 2, PIECE, width)
    four = (*lead, 4, PIECE, width)
    one = (*lead, PIECE, width)
    shapes = (
        pair,
        pair,
        four,
        four,
        (*lead, PIECE, low),
        (*lead, PIECE, width - low),
        one,
        one,
    )
    return [pltpu.VMEM(s, BF16) for s in shapes] * 2


def reduce_ring(net, me, grad, lead, low, bufs, landing, loads=None):
    z, y, h = me.z, me.y, me.h
    g = 1 - h
    every = slice(None)
    width = grad.shape[-1]
    lanes = (slice(0, low), slice(low, width))
    pairs = (slice(0, 2), slice(2, 4))
    own = dict(zip(RING_BUFS, bufs[:8]))
    other = dict(zip(RING_BUFS, bufs[8:]))
    add = add_pieces(lead)

    def front_of(ref, *index):
        return ref.at[(every,) * lead + index]

    def cut_pair(ref, part):
        return front_of(ref, pairs[part])

    def cut_lane(ref, part):
        return front_of(ref, every, lanes[part])

    ring_z = (me.ring(up(z), y, h), me.ring(down(z), y, h))
    ring_y = (me.ring(z, up(y), h), me.ring(z, down(y), h))
    a_at = lambda i, part: front_of(grad, i, pairs[part], h)
    b_at = lambda i, part: front_of(grad, pairs[part], i, g)
    a_terms = (a_at(up(z), 0), a_at(down(z), 1), front_of(grad, z, every, h))
    b_terms = (b_at(up(y), 0), b_at(down(y), 1), front_of(grad, every, y, g))
    loading = []
    if loads is not None:
        loading = [net.here(s, d) for s, d in zip(a_terms + b_terms, loads)]
        a_terms, b_terms = loads[:3], loads[3:]
    a = ring_sum(
        net, a_at, z, *ring_z, cut_pair, add, *(own[n] for n in RING_BUFS[:4]), a_terms
    )
    b = ring_sum(
        net, b_at, y, *ring_y, cut_pair, add, *(other[n] for n in RING_BUFS[:4]), b_terms
    )
    next(a)
    next(b)
    yield
    for made in loading:
        made.wait()
    next(a)
    next(b)
    yield
    for _ in a:
        pass
    add(own["ru"], own["rd"], a_terms[2])
    a = ring_sum(
        net,
        lambda i, part: front_of(own["ru"], i, every, lanes[part]),
        y,
        *ring_y,
        cut_lane,
        add,
        *(own[n] for n in RING_BUFS[4:]),
    )
    next(a)
    for _ in b:
        pass
    add(other["ru"], other["rd"], b_terms[2])
    b = ring_sum(
        net,
        lambda i, part: front_of(other["ru"], i, every, lanes[part]),
        z,
        *ring_z,
        cut_lane,
        add,
        *(other[n] for n in RING_BUFS[4:]),
    )
    next(b)
    yield
    next(a)
    next(b)
    yield
    for _ in b:
        pass
    add(other["su"], other["sd"], front_of(other["ru"], z))
    last = net.copy(other["su"], landing, me.ring(z, y, g))
    for _ in a:
        pass
    add(own["su"], own["sd"], front_of(own["ru"], y))
    yield
    last.wait_recv()


MID_IN = ["n2", "cot8", "w", "wdn", "hid", "gains"]
MID_OUT = ["out", "g", "gd", "dbr", "dh", "gain"]
MID_SCRATCH = {
    "x8": ((8, ROWS, D), BF16),
    "c8": ((8, ROWS, D), BF16),
    "w8": ((2, D, FPAD), BF16),
    "wd": ((4, 4, 2, PIECE, FPAD), BF16),
    "act": ((8, ROWS, FPAD), BF16),
    "dg": ((8, ROWS, FPAD), BF16),
    "du": ((8, ROWS, FPAD), BF16),
    "out8": ((4, 2, ROWS, D), BF16),
    "dn2": ((4, 2, ROWS, D), BF16),
    "g8": ((2, D, FPAD), BF16),
    "gd8": ((4, 4, 2, PIECE, FPAD), BF16),
}
LANES = [slice(i * 256, i * 256 + 256) for i in range(4)] + [slice(1024, FPAD)]


def tile(i, size):
    return pl.ds(pl.multiple_of(i * size, size), size)


def hidden_units(r, chip):
    at = pl.ds(2 * chip, 2)
    left = r.x8[at].reshape(2 * ROWS, D)
    for lanes in LANES:
        gate = dot_nn(left, r.w8[0, :, lanes])
        lift = dot_nn(left, r.w8[1, :, lanes])
        sigma = 1.0 / (1.0 + jnp.exp(-gate))
        silu = gate * sigma
        pieces = (
            (r.act, silu * lift),
            (r.du, silu),
            (r.dg, lift * (sigma * (1.0 + gate * (1.0 - sigma)))),
        )
        for ref, value in pieces:
            ref[at, :, lanes] = value.astype(BF16).reshape(2, ROWS, value.shape[1])


def unit_gradients(r):
    back = r.c8[...].reshape(8 * ROWS, D)
    for lanes in LANES:
        d_act = dot_nn(back, r.wd[:, :, :, :, lanes].reshape(D, lanes.stop - lanes.start))
        d_act = d_act.reshape(8, ROWS, lanes.stop - lanes.start)
        for ref in (r.du, r.dg):
            ref[:, :, lanes] = (d_act * ref[:, :, lanes].astype(F32)).astype(BF16)


def gradient_rows(r, chip):
    at = pl.ds(2 * chip, 2)
    dg, du = (ref[at].reshape(2 * ROWS, FPAD) for ref in (r.dg, r.du))

    def one(j, carry):
        wide = tile(j, 512)
        both = dot_nt(dg, r.w8[0, wide, :]) + dot_nt(du, r.w8[1, wide, :])
        r.dn2[chip, :, :, wide] = both.astype(BF16).reshape(2, ROWS, 512)
        return carry

    lax.fori_loop(0, 3, one, 0)


def mid_kernel(*refs):
    names = MID_IN + MID_OUT + list(MID_SCRATCH)
    r = Refs(names, refs)
    rest = refs[len(names) :]
    bufs, ring_bufs_d = rest[:5], rest[5:21]
    send, recv, local = rest[21:]
    me = Place()
    net = Net(send, recv, local)
    x, k, t = me.x, me.k, me.t
    z, y, h = me.z, me.y, me.h
    lines = [(z, slice(None), h), (slice(None), y, 1 - h)]
    near = [net.here(r.wdn.at[at], r.wd.at[at]) for at in lines]
    load_w = net.here(r.w, r.w8)
    load_c = net.here(r.cot8, r.c8)
    barrier(
        [me.chip(up(x), k), me.chip(down(x), k), me.core]
        + [me.ring(up(z), y, h), me.ring(down(z), y, h)]
        + [me.ring(z, up(y), h), me.ring(z, down(y), h)]
    )
    r.x8[x * 2 + k] = r.n2[...]
    rows = gather_chips(net, me, r.x8)
    next(rows)
    ring = gather_ring(net, me, None, None, r.wd, 0, (None, None), near=False)
    for made in near:
        made.wait()
    next(ring)
    next(ring)
    load_w.wait()
    next(rows)
    next(rows)
    hidden_units(r, x)
    next(rows)
    next(rows)
    hidden_units(r, down(x))
    next(ring)
    next(ring)
    next(rows)
    hidden_units(r, up(x))
    for _ in rows:
        pass
    hidden_units(r, opposite(x))
    load_c.wait()
    act = r.act[...].reshape(8 * ROWS, FPAD)
    for i in range(2):
        left = r.c8[:, :, i * 768 : i * 768 + 768].reshape(8 * ROWS, 768).T
        r.gd8[2 * i : 2 * i + 2] = dot_nn(left, act).astype(BF16).reshape(2, 4, 2, PIECE, FPAD)
    for _ in ring:
        pass
    down_ring = reduce_ring(net, me, r.gd8, 0, 640, ring_bufs_d, r.gd.at[h])
    next(down_ring)
    unit_gradients(r)
    norm2 = ChipSum(net, me, r.dn2, lambda i: r.dn2[i, k], bufs)
    steps = norm2.steps()
    gradient_rows(r, opposite(x))
    norm2.push("far")
    gradient_rows(r, up(x))
    norm2.push("above")
    next(steps)
    next(down_ring)
    gradient_rows(r, down(x))
    norm2.push("below")
    next(steps)
    gradient_rows(r, x)
    norm2.push("own")
    next(steps)
    next(steps)
    dg, du = (ref[...].reshape(8 * ROWS, FPAD) for ref in (r.dg, r.du))

    def grads(i):
        wide = slice(i * 768, i * 768 + 768)
        left = r.x8[:, :, wide].reshape(8 * ROWS, 768).T
        r.g8[0, wide, :] = dot_nn(left, dg).astype(BF16)
        r.g8[1, wide, :] = dot_nn(left, du).astype(BF16)

    next(down_ring)
    grads(0)
    next(down_ring)

    def one(j, carry):
        wide = tile(j, 384)
        right = r.wd[j].reshape(384, FPAD)
        r.out8[:, :, :, wide] = dot_nt(act, right).astype(BF16).reshape(4, 2, ROWS, 384)
        return carry

    lax.fori_loop(0, 2, one, 0)
    next(down_ring)
    d_norm2 = next(steps)
    hidden = r.hid[...]
    scale2 = rms(hidden)
    xh2 = hidden * scale2
    e2 = d_norm2 * r.gains[1:2, :]
    d_hidden = r.c8[x * 2 + k].astype(F32) + scale2 * (
        e2 - xh2 * jnp.mean(e2 * xh2, axis=-1, keepdims=True)
    )
    r.dh[...] = d_hidden
    r.gain[...] = jnp.sum(d_norm2 * xh2, axis=0, keepdims=True)
    r.dbr[t] = d_hidden.astype(BF16)
    branch = gather_block(net, me, r.dbr)
    next(branch)
    grads(1)
    net.keep(r.g8, r.g)
    next(branch)
    lax.fori_loop(2, 4, one, 0)
    net.keep(r.out8, r.out)
    for _ in branch:
        pass
    for _ in down_ring:
        pass
    r.gd[h] = ring_bufs_d[6][...]
    net.finish()


def mid(*arrays):
    shapes = (
        ((4, 2, ROWS, D), BF16),
        ((2, D, FPAD), BF16),
        ((2, PIECE, FPAD), BF16),
        ((4, ROWS, D), BF16),
        ((ROWS, D), F32),
        ((1, D), F32),
    )
    return call(
        mid_kernel,
        MID_IN,
        arrays,
        dict(zip(MID_OUT, shapes)),
        ("cot8", "w", "wdn", "out", "g"),
        scratch_of(MID_SCRATCH) + [pltpu.VMEM(*s) for s in CHIP_BUFS]
        + ring_bufs((), FPAD, 640)
        + semaphores(64, 64, 12),
        1,
        63,
        "mid",
    )


def columns_by_row(rows_ref, blocks, right, out):
    count = right.shape[0]
    for i in range(4):
        left = rows_ref[blocks, :, i * 384 : (i + 1) * 384].reshape(count, 384)
        out[i] = dot_tn(left, right).astype(BF16).reshape(out.shape[1:])


def direct_bufs(width):
    far, line, one = (3, 4, PIECE, width), (4, PIECE, width), (PIECE, width)
    return [pltpu.VMEM(s, BF16) for s in (far, far, line, line, (3, *one), (3, *one), one, one)]


def reduce_direct(net, me, grad, bufs, landing):
    z, y, h = me.z, me.y, me.h
    g = 1 - h
    ra, rb, la, lb, sa, sb, own, other = bufs
    others = (2, 1, 3)

    def to_y(pick, bufs):
        at = [lax.rem(y + j, 4) for j in others]
        return [net.copy(pick(i), bufs.at[n], me.ring(z, i, h)) for n, i in enumerate(at)]

    def to_z(pick, bufs):
        at = [lax.rem(z + j, 4) for j in others]
        return [net.copy(pick(i), bufs.at[n], me.ring(i, y, h)) for n, i in enumerate(at)]

    def total(sent, first, bufs):
        for made in sent:
            made.wait_recv()
        return first.astype(F32) + (
            bufs[0].astype(F32) + bufs[1].astype(F32) + bufs[2].astype(F32)
        )

    a = to_z(lambda i: grad.at[i, :, h], ra)
    b = to_y(lambda i: grad.at[:, i, g], rb)
    yield
    lb[...] = total(b, grad[:, y, g], rb).astype(BF16)
    b = to_z(lambda i: lb.at[i], sb)
    la[...] = total(a, grad[z, :, h], ra).astype(BF16)
    a = to_y(lambda i: la.at[i], sa)
    yield
    other[...] = total(b, lb[z], sb).astype(BF16)
    last = net.copy(other, landing, me.ring(z, y, g))
    own[...] = total(a, la[y], sa).astype(BF16)
    yield
    last.wait_recv()


def attend_back(me, half, r, delta):
    begin = r.begin[half : half + 1, :]
    top = me.c

    def step(j, carry, last):
        keys = span_of(r.kv, j, 0)
        values = span_of(r.kv, j, 1)
        keys_t = keys.astype(F32).T.astype(BF16)
        allowed = mask_of(me, half, begin, j, last)
        d_keys = jnp.zeros((SPAN, HD), F32)
        d_values = jnp.zeros((SPAN, HD), F32)
        out = []
        for head in range(3):
            row = half * 3 + head
            query, d_out = r.q[half, head], r.dm[half, head]
            raw = dot_nt(keys, query) * ROOT2 - r.lse[row : row + 1, :]
            probs = jnp.exp2(jnp.where(allowed, raw, MASKED))
            d_probs = dot_nt(values, d_out)
            d_raw = (probs * (d_probs - delta[head])).astype(BF16)
            d_values = d_values + dot_nn(probs.astype(BF16), d_out)
            d_keys = d_keys + dot_nn(d_raw, query)
            out.append(carry[head] + dot_nn(keys_t, d_raw))
        at = pl.ds(2 * j, 2)
        r.dkv[at, 0] += d_keys.reshape(2, HALF, HD)
        r.dkv[at, 1] += d_values.reshape(2, HALF, HD)
        return tuple(out)

    zero = jnp.zeros((HD, HALF), F32)
    carry = step(top, (zero,) * 3, True)
    carry = lax.fori_loop(0, top, lambda i, carry: step(top - 1 - i, carry, False), carry)
    rows = slice(half * HALF, (half + 1) * HALF)
    cosine, sine = r.cos[rows, :], r.sin[rows, :]
    for head in range(3):
        back = carry[head].T * INV_ROOT
        back = back * cosine - pltpu.roll(back, HD // 2, 1) * sine
        r.dq[rows, head * HD : (head + 1) * HD] = back.astype(BF16)


def to_lines(ref, at, row):
    for i in range(row.shape[1] // HD):
        ref[pl.ds(at + i, 1), :] = row[:, i * HD : (i + 1) * HD]


class Total:
    def __init__(self, net, me, value, xb, yzb):
        self.net, self.me, self.xb, self.yzb = net, me, xb, yzb
        at = me.x * 2 + me.k
        xb[at] = value
        self.sent = []
        for j in range(4):
            for other in range(2):
                if j == 0 and other == 0:
                    continue
                core = me.k if other == 0 else 1 - me.k
                dev = me.chip(lax.rem(me.x + j, 4), core)
                self.sent.append(net.copy(xb.at[at], xb.at[at], dev))

    def second(self):
        net, me = self.net, self.me
        for made in self.sent:
            made.wait_recv()
        total = self.xb[0]
        for i in range(1, 8):
            total = total + self.xb[i]
        at = me.z * 4 + me.y
        self.yzb[at] = total
        self.sent = []
        for j in range(1, 16):
            z, y = lax.rem(me.z + j // 4, 4), lax.rem(me.y + j % 4, 4)
            piece = self.yzb.at[at]
            self.sent.append(net.copy(piece, piece, me.ring(z, y, me.h)))

    def final(self):
        for made in self.sent:
            made.wait_recv()
        total = self.yzb[0]
        for i in range(1, 16):
            total = total + self.yzb[i]
        return total


BACK_IN = ["outp", "gfeed", "dbr", "dh", "gain", "hid", "x", "small", "wo", "normed"]
BACK_IN += ["q", "kv", "att", "lse", "cos", "sin", "begin", "gains"]
BACK_OUT = ["result", "igrad", "gf", "gsm", "gpair", "total", "late"]
BACK_SCRATCH = {
    "v_small": ((4, 4, 2, PIECE, 640), BF16),
    "v_wo": ((4, 4, 2, PIECE, QW), BF16),
    "v_normed": ((4, ROWS, D), BF16),
    "v_dbr": ((4, ROWS, D), BF16),
    "v_outp": ((4, ROWS, D), BF16),
    "v_kv": ((16, 2, HALF, HD), BF16),
    "mixed": ((512, QW), BF16),
    "dm": ((2, 3, HALF, HD), BF16),
    "dq": ((512, QW), BF16),
    "dkv": ((16, 2, HALF, HD), F32),
    "k_send": ((8, 2, HALF, HD), BF16),
    "k_recv": ((8, 2, HALF, HD), BF16),
    "k_far": ((7, 2, HALF, HD), BF16),
    "d_kv": ((2, HALF, HD), F32),
    "dpair": ((HALF, 2 * HD), BF16),
    "part": ((4, ROWS, D), F32),
    "s1": ((2, ROWS, D), BF16),
    "r1": ((2, ROWS, D), BF16),
    "s2": ((ROWS, D), BF16),
    "r2": ((ROWS, D), BF16),
    "g_q": ((4, 4, 2, PIECE, QW), BF16),
    "g_o": ((4, 4, 2, PIECE, QW), BF16),
    "g_kv": ((4, 4, 2, PIECE, 2 * HD), BF16),
    "p_send": ((4, 4, 2, PIECE, 2 * HD), BF16),
    "p_recv": ((4, 4, 2, PIECE, 2 * HD), BF16),
    "l_q": ((PIECE, QW), BF16),
    "l_o": ((PIECE, QW), BF16),
    "l_kv": ((PIECE, 2 * HD), BF16),
    "kv_own": ((PIECE, 2 * HD), BF16),
    "kv_far": ((PIECE, 2 * HD), BF16),
    "tot": ((32, HD), F32),
    "t_x": ((8, 32, HD), F32),
    "t_yz": ((16, 32, HD), F32),
    "u_x": ((8, 16, HD), F32),
    "u_yz": ((16, 16, HD), F32),
    "u": ((16, HD), F32),
}


def back_kernel(*refs):
    names = BACK_IN + BACK_OUT + list(BACK_SCRATCH)
    r = Refs(names, refs)
    rest = refs[len(names) :]
    f0_bufs, f1_bufs = rest[:16], rest[16:32]
    o_bufs, q_bufs, kv_bufs = (rest[i : i + 8] for i in (32, 40, 48))
    f0_loads, f1_loads, chip_bufs = rest[56:62], rest[62:68], rest[68:73]
    send, recv, local = rest[73:]
    me = Place()
    net = Net(send, recv, local)
    z, y, h, x, k, c, t = me.z, me.y, me.h, me.x, me.k, me.c, me.t
    load_dbr = net.here(r.dbr, r.v_dbr)
    load_wo = net.here(r.wo, r.v_wo)
    load_kv = net.here(r.kv, r.v_kv)
    load_normed = net.here(r.normed, r.v_normed)
    load_small = net.here(r.small, r.v_small)
    load_out = net.here(r.outp.at[:, k], r.v_outp)
    r.kv = r.v_kv
    barrier(
        [me.block(lax.rem(c + j, 8), k) for j in range(1, 8)]
        + [
            me.ring(lax.rem(z + j // 4, 4), lax.rem(y + j % 4, 4), h)
            for j in range(1, 16)
            if j // 4
        ]
        + [me.chip(lax.rem(x + j, 4), k) for j in range(1, 4)]
        + [me.chip(lax.rem(x + j, 4), 1 - k) for j in range(4)]
    )
    feed0 = reduce_ring(net, me, r.gfeed.at[0], 0, 640, f0_bufs, r.gf.at[h, 0], f0_loads)
    feed1 = reduce_ring(net, me, r.gfeed.at[1], 0, 640, f1_bufs, r.gf.at[h, 1], f1_loads)
    next(feed0)
    outs = ChipSum(net, me, r.outp, lambda i: r.v_outp[i], chip_bufs)
    for name in ("far", "above", "below", "own"):
        outs.push(name)
    out_steps = outs.steps()
    r.dkv[...] = jnp.zeros_like(r.dkv)
    r.tot[...] = jnp.zeros_like(r.tot)
    to_lines(r.tot, 0, r.gain[...])
    for half in range(2):
        for head in range(3):
            r.mixed[half * HALF : (half + 1) * HALF, head * HD : (head + 1) * HD] = r.att[
                half, head
            ].astype(BF16)
    load_wo.wait()
    load_dbr.wait()
    wo = r.v_wo[...].reshape(D, QW)
    d_mixed = dot_nn(r.v_dbr[...].reshape(512, D), wo)
    deltas = []
    for half in range(2):
        rows = slice(half * HALF, (half + 1) * HALF)
        for head in range(3):
            piece = d_mixed[rows, head * HD : (head + 1) * HD].astype(BF16)
            r.dm[half, head] = piece
            both = piece.astype(F32) * r.att[half, head]
            deltas.append(jnp.sum(both.T, axis=0, keepdims=True))
    load_out.wait()
    next(out_steps)
    load_kv.wait()
    next(feed1)
    attend_back(me, 1, r, deltas[3:])
    attend_back(me, 0, r, deltas[:3])
    for p in range(8):
        r.k_send[p] = r.dkv[2 * p + 1 - k].astype(BF16)
    kx = net.copy(r.k_send, r.k_recv, me.core)
    next(feed0)
    kx.wait()
    for p in range(8):
        r.dkv[2 * p + k] += r.k_recv[p].astype(F32)
        r.k_send[p] = r.dkv[2 * p + k].astype(BF16)
    r.d_kv[...] = r.dkv[2 * c + k]
    k_sent = []
    order = (4, 3, 5, 2, 6, 1, 7)
    for i, j in enumerate(order):
        there = lax.rem(c + 8 - j, 8)
        k_sent.append(
            net.copy_if(c >= j, r.k_send.at[there], r.k_far.at[i], me.block(there, k))
        )
    next(feed1)
    next(out_steps)
    columns_by_row(r.v_dbr, slice(0, 4), r.mixed[...], r.g_o)
    ring_o = reduce_direct(net, me, r.g_o, o_bufs, r.l_o)
    next(ring_o)
    load_normed.wait()
    load_small.wait()
    columns_by_row(r.v_normed, slice(0, 4), r.dq[...], r.g_q)
    ring_q = reduce_direct(net, me, r.g_q, q_bufs, r.l_q)
    next(ring_q)
    next(feed0)
    next(out_steps)
    next(out_steps)
    to_lines(r.tot, 12 + 3 * t, jnp.sum(r.dq[...].astype(F32), axis=0, keepdims=True))
    wq = r.v_small[:, :, :, :, 0:QW].reshape(D, QW)
    for i in range(4):
        r.part[i] = dot_nt(r.dq[i * ROWS : (i + 1) * ROWS, :], wq)
    next(feed1)
    for i, (j, made) in enumerate(zip(order, k_sent)):

        @pl.when(c + j < 8)
        def _():
            made.wait_recv()
            r.d_kv[...] += r.k_far[i].astype(F32)

    d_kv = r.d_kv[...]
    half_rows = pl.ds(pl.multiple_of(k * HALF, HALF), HALF)
    cosine, sine = r.cos[half_rows, :], r.sin[half_rows, :]
    d_key = d_kv[0] * INV_ROOT
    r.dpair[:, 0:HD] = (d_key * cosine - pltpu.roll(d_key, HD // 2, 1) * sine).astype(BF16)
    r.dpair[:, HD : 2 * HD] = d_kv[1].astype(BF16)
    d_pair = r.dpair[...]
    wkv = r.v_small[:, :, :, :, QW:640].reshape(D, 2 * HD)
    for i in range(2):
        at = 2 * k + i
        r.part[at] = r.part[at] + dot_nt(d_pair[i * ROWS : (i + 1) * ROWS, :], wkv)
    norm1 = sum_block(net, me, r.part, r.s1, r.r1, r.s2, r.r2)
    next(norm1)
    columns_by_row(r.v_normed, pl.ds(2 * k, 2), d_pair, r.p_send)
    px = net.copy(r.p_send, r.p_recv, me.core)
    next(norm1)
    sums = jnp.sum(d_pair.astype(F32), axis=0, keepdims=True)
    to_lines(r.tot, 24 + me.xl, sums[:, :HD])
    to_lines(r.tot, 26 + me.xl, sums[:, HD:])
    px.wait_recv()
    r.g_kv[...] = (r.p_send[...].astype(F32) + r.p_recv[...].astype(F32)).astype(BF16)
    ring_kv = reduce_direct(net, me, r.g_kv, kv_bufs, r.l_kv)
    next(ring_kv)
    total = Total(net, me, r.tot[...], r.t_x, r.t_yz)
    next(feed0)
    next(ring_o)
    next(ring_q)
    next(feed1)
    d_norm1 = next(norm1)
    flat = r.x[...].astype(F32)
    scale1 = rms(flat)
    xh1 = flat * scale1
    gain = jnp.sum(d_norm1 * xh1, axis=0, keepdims=True)
    r.u[...] = jnp.zeros_like(r.u)
    to_lines(r.u, 0, gain)
    late = Total(net, me, r.u[...], r.u_x, r.u_yz)
    next(ring_kv)
    e1 = d_norm1 * r.gains[0:1, :]
    r.igrad[...] = r.dh[...] + scale1 * (
        e1 - xh1 * jnp.mean(e1 * xh1, axis=-1, keepdims=True)
    )
    total.second()
    next(feed0)
    late.second()
    next(ring_o)
    next(ring_q)
    next(ring_kv)
    next(feed1)
    r.result[...] = (r.hid[...] + next(out_steps)).astype(BF16)
    r.total[...] = total.final()
    for ring in (ring_o, ring_q, ring_kv):
        for _ in ring:
            pass
    r.late[...] = late.final()
    su_q, su_o, su_kv = q_bufs[6], o_bufs[6], kv_bufs[6]
    pair_own = su_kv[...].astype(F32) + r.l_kv[...].astype(F32)
    r.kv_own[...] = pair_own.astype(BF16)
    pair_sent = net.copy(r.kv_own, r.kv_far, me.side)
    r.gsm[:, 0:QW] = su_q[...].astype(F32) + r.l_q[...].astype(F32)
    r.gsm[:, QW:] = su_o[...].astype(F32) + r.l_o[...].astype(F32)
    for ring in (feed0, feed1):
        for _ in ring:
            pass
    r.gf[h, 0] = f0_bufs[6][...]
    r.gf[h, 1] = f1_bufs[6][...]
    pair_sent.wait_recv()
    pieces = (r.kv_own[...].astype(F32), r.kv_far[...].astype(F32))
    for i, at in enumerate((me.xl, 1 - me.xl)):
        r.gpair[:, pl.ds(pl.multiple_of(at * HD, HD), HD)] = pieces[i][:, :HD]
        r.gpair[:, pl.ds(pl.multiple_of((2 + at) * HD, HD), HD)] = pieces[i][:, HD:]

    net.finish((kx,))


def back(*arrays):
    shapes = (
        ((ROWS, D), BF16),
        ((ROWS, D), F32),
        ((2, 2, PIECE, FPAD), BF16),
        ((PIECE, 2 * QW), F32),
        ((PIECE, 4 * HD), F32),
        ((32, HD), F32),
        ((16, HD), F32),
    )
    return call(
        back_kernel,
        BACK_IN,
        arrays,
        dict(zip(BACK_OUT, shapes)),
        ("outp", "gfeed", "dbr", "small", "wo", "normed", "kv"),
        scratch_of(BACK_SCRATCH)
        + ring_bufs((), FPAD, 640)
        + ring_bufs((), FPAD, 640)
        + direct_bufs(QW)
        + direct_bufs(QW)
        + direct_bufs(2 * HD)
        + [pltpu.VMEM((n, PIECE, FPAD), BF16) for n in (2, 2, 4)] * 4
        + [pltpu.VMEM(*s) for s in CHIP_BUFS]
        + semaphores(230, 230, 20),
        2,
        63,
        "back",
    )


def prep_kernel(lengths, wq, wp, wo, wf, biases, p1, po, p2, pd, bias, cos, sin, begin):
    me = Place()
    p1[:, 0:QW] = wq[...].astype(BF16)
    for i in range(2):
        at = pl.ds(pl.multiple_of(i * KV * HD + me.xl * HD, HD), HD)
        to = slice(QW + i * HD, QW + (i + 1) * HD)
        p1[:, to] = wp[:, at].astype(BF16)
        at = pl.ds(pl.multiple_of(HQ * HD + i * KV * HD + me.xl * HD, HD), HD)
        bias[:, to] = biases[:, at]
    bias[:, 0:QW] = biases[:, pl.ds(pl.multiple_of(me.t * QW, HD), QW)]
    po[...] = wo[...].astype(BF16)
    rest = FCOLS - FPAD
    for m in range(3):
        first, second = (p2.at[0, m], p2.at[1, m]) if m < 2 else (pd.at[0], pd.at[1])
        first[...] = wf[m, :, 0:FPAD].astype(BF16)
        tail = wf[m, :, FPAD:FCOLS].astype(BF16)
        second[...] = jnp.concatenate([tail, jnp.zeros((PIECE, FPAD - rest), BF16)], axis=1)

    def starts(index):
        end, found = lengths[0, 0], jnp.zeros_like(index)
        for i in range(3):
            found = jnp.where(index >= end, end, found)
            end = end + lengths[0, i + 1]
        return found

    first = me.c * 512
    along = lax.broadcasted_iota(jnp.int32, (2, HALF), 1)
    along = along + lax.broadcasted_iota(jnp.int32, (2, HALF), 0) * HALF + first
    begin[...] = starts(along)
    down_rows = lax.broadcasted_iota(jnp.int32, (512, HD), 0) + first
    position = (down_rows - starts(down_rows)).astype(F32)
    lane = lax.broadcasted_iota(jnp.int32, (512, HD), 1)
    steps = lax.rem(lane, HD // 2).astype(F32)
    angle = position * jnp.exp(-(2.0 * steps / HD) * math.log(ROPE_BASE))
    cos[...] = jnp.cos(angle)
    turned = jnp.sin(angle)
    sin[...] = jnp.where(lane < HD // 2, -turned, turned)


def prep(lengths, wq, wp, wo, wf, biases):
    shape = jax.ShapeDtypeStruct
    vmem = pl.BlockSpec(memory_space=pltpu.VMEM)
    return pl.pallas_call(
        prep_kernel,
        out_shape=(
            shape((PIECE, 640), BF16),
            shape((PIECE, QW), BF16),
            shape((2, 2, PIECE, FPAD), BF16),
            shape((2, PIECE, FPAD), BF16),
            shape((1, 640), F32),
            shape((512, HD), F32),
            shape((512, HD), F32),
            shape((2, HALF), jnp.int32),
        ),
        in_specs=[pl.BlockSpec(memory_space=pltpu.SMEM)] + [vmem] * 5,
        out_specs=(vmem,) * 8,
        compiler_params=pltpu.CompilerParams(vmem_limit_bytes=63 * 2**20),
        name="prep",
    )(lengths, wq, wp, wo, wf, biases)


def adamw(weight, mean_old, square_old, grad, rate, decay):
    mean_new = BETA_ONE * mean_old + (1.0 - BETA_ONE) * grad
    square_new = BETA_TWO * square_old + (1.0 - BETA_TWO) * grad * grad
    mean_hat = mean_new / (1.0 - BETA_ONE**STEP)
    square_hat = square_new / (1.0 - BETA_TWO**STEP)
    weight_new = weight - rate * (mean_hat / (jnp.sqrt(square_hat) + ADAM_EPS) + decay * weight)
    return (mean_new, square_new, weight_new)


RATES = {
    "query": (0.05, 0.1),
    "pair": (3.0 / math.sqrt(D), 0.1),
    "output": (3.0 / math.sqrt(max(HQ * HD // 256, 1)), 0.1),
    "feed": (0.05, 0.1),
    "gains": (1.5, 0.0),
    "biases": (0.5, 0.0),
}
STATE_SHAPES = {
    "query": (PIECE, QW),
    "pair": (PIECE, 2 * KV * HD),
    "output": (PIECE, QW),
    "feed": (3, PIECE, FCOLS),
    "gains": (2, D),
    "biases": (16, HD),
}


def as_row(ref, at):
    return jnp.concatenate([ref[at + i : at + i + 1, :] for i in range(D // HD)], axis=1)


def update_kernel(result, igrad, gf, gsm, gpair, total, late, gd, *refs):
    state, (result_out, igrad_out), news = refs[:18], refs[18:20], refs[20:]

    def update(i, name, grad, at=Ellipsis):
        olds = [ref[at] for ref in state[3 * i : 3 * i + 3]]
        for ref, new in zip(news[3 * i : 3 * i + 3], adamw(*olds, grad, *RATES[name])):
            ref[at] = new

    for m in range(3):
        for half, lanes in enumerate((slice(0, FPAD), slice(FPAD, FCOLS))):
            some = slice(0, lanes.stop - lanes.start)
            grad = gf[half, m, :, some] if m < 2 else gd[half, :, some]
            update(3, "feed", grad.astype(F32), (m, slice(None), lanes))
    result_out[...] = result[...]
    igrad_out[...] = igrad[...]
    update(0, "query", gsm[:, 0:QW])
    update(1, "pair", gpair[...])
    update(2, "output", gsm[:, QW : 2 * QW])
    update(4, "gains", jnp.concatenate([as_row(late, 0), as_row(total, 0)], axis=0))
    update(5, "biases", total[12:28, :])


def update_all(grads, state):
    vmem = pl.BlockSpec(memory_space=pltpu.VMEM)
    rows = [jax.ShapeDtypeStruct((ROWS, D), BF16), jax.ShapeDtypeStruct((ROWS, D), F32)]
    return pl.pallas_call(
        update_kernel,
        out_shape=rows + [jax.ShapeDtypeStruct(s, F32) for s in STATE_SHAPES.values() for _ in range(3)],
        in_specs=[vmem] * (len(grads) + len(state)),
        out_specs=[vmem] * (len(state) + 2),
        compiler_params=pltpu.CompilerParams(vmem_limit_bytes=63 * 2**20),
        name="update",
    )(*grads, *state)


def body(
    inputs,
    cotangent,
    lengths,
    query_weight,
    query_mean,
    query_square,
    pair_weight,
    pair_mean,
    pair_square,
    output_weight,
    output_mean,
    output_square,
    feed_weight,
    feed_mean,
    feed_square,
    gains,
    gains_mean,
    gains_square,
    biases,
    biases_mean,
    biases_square,
):
    feeds = [a.transpose(1, 0, 2) for a in (feed_weight, feed_mean, feed_square)]
    p1, po, p2, pd, bias, cosine, sine, begin = prep(
        lengths, query_weight, pair_weight, output_weight, feeds[0], biases.reshape(1, QKV)
    )
    feed, wd, small, wo, normed, q, kv, att, lse, hid, n2, cot8 = front(
        inputs, cotangent, gains, bias, cosine, sine, begin, p1, po, p2, pd
    )
    out, g_feed, g_down, dbr, dh, gain = mid(n2, cot8, feed.reshape(2, D, FPAD), wd, hid, gains)
    grads = back(
        out,
        g_feed.reshape(2, 4, 4, 2, PIECE, FPAD),
        *(dbr, dh, gain, hid, inputs, small, wo, normed),
        *(q, kv, att, lse, cosine, sine, begin, gains),
    )
    lines = lambda *arrays: [a.reshape(-1, HD) for a in arrays]
    made = list(update_all(
        (*grads, g_down),
        [query_weight, query_mean, query_square]
        + [pair_weight, pair_mean, pair_square]
        + [output_weight, output_mean, output_square]
        + feeds
        + [gains, gains_mean, gains_square]
        + lines(biases, biases_mean, biases_square),
    ))
    made[11:14] = [a.transpose(1, 0, 2) for a in made[11:14]]
    made[17:20] = [a.reshape(QKV) for a in made[17:20]]
    return tuple(made)


def solution(mesh):
    mesh = Mesh(mesh.devices.reshape(4, 4, 2, 4), AXES)
    rows = P(("dp", "y", "xh", "tensor"), None)
    cut = P(("dp", "y", "xh"), "tensor")
    pair = P(("dp", "y", "xh"), None)
    feed = P(("dp", "y", "xh"), None, "tensor")
    whole = P()
    in_specs = (rows, rows, P("dp", None))
    in_specs += (cut,) * 3 + (pair,) * 3 + (cut,) * 3 + (feed,) * 3 + (whole,) * 6
    out_specs = (rows, rows) + (cut,) * 3 + (pair,) * 3 + (cut,) * 3 + (feed,) * 3 + (whole,) * 6
    return jax.shard_map(body, mesh=mesh, in_specs=in_specs, out_specs=out_specs, check_vma=False)
```

```python
import math

import jax
import jax.numpy as jnp
from jax import lax
from jax.experimental import pallas as pl
from jax.experimental.pallas import tpu as pltpu
from jax.sharding import Mesh
from jax.sharding import PartitionSpec as P

D = 1536
HQ = 12
KV = 2
HD = 128
FF = 8960
STEP = 10
QKV = 2048
ROWS = 128
HALF = 256
GROUP = 4096
PIECE = 48
FCOLS = 2240
FPAD = 1152
QW = 384
SMALL = 1024
SPAN = 512

NORM_EPS = 1e-06
ROPE_BASE = 1000000.0
BETA_ONE = 0.9
BETA_TWO = 0.95
ADAM_EPS = 1e-08
MASKED = -1e30
LOG2E = math.log2(math.e)
ROOT2 = LOG2E / math.sqrt(HD)
INV_ROOT = 1.0 / math.sqrt(HD)

MESH_ID = pl.DeviceIdType.MESH
BF16 = jnp.bfloat16
F32 = jnp.float32
AXES = ("dp", "y", "xh", "tensor")


def up(v):
    return lax.rem(v + 1, 4)


def down(v):
    return lax.rem(v + 3, 4)


def opposite(v):
    return lax.rem(v + 2, 4)


def dot_nn(a, b):
    return lax.dot_general(a, b, (((1,), (0,)), ((), ())), preferred_element_type=F32)


def dot_nt(a, b):
    return lax.dot_general(a, b, (((1,), (1,)), ((), ())), preferred_element_type=F32)


def dot_tn(a, b):
    return lax.dot_general(a, b, (((0,), (0,)), ((), ())), preferred_element_type=F32)


class Place:
    def __init__(self):
        self.z = lax.axis_index("dp")
        self.y = lax.axis_index("y")
        self.h = lax.axis_index("xh")
        self.t = lax.axis_index("tensor")
        self.xl = self.t // 2
        self.k = lax.rem(self.t, 2)
        self.x = self.h * 2 + self.xl
        self.c = self.y * 2 + self.h

    def ring(self, z, y, h):
        return (z, y, h, self.t)

    def chip(self, x, k):
        return (self.z, self.y, x // 2, lax.rem(x, 2) * 2 + k)

    def block(self, c, k):
        return (self.z, c // 2, lax.rem(c, 2), self.xl * 2 + k)

    @property
    def core(self):
        return (self.z, self.y, self.h, self.xl * 2 + 1 - self.k)

    @property
    def side(self):
        return (self.z, self.y, self.h, (1 - self.xl) * 2 + self.k)


class Net:
    def __init__(self, send, recv, local):
        self.send, self.recv, self.local = send, recv, local
        self.n, self.m = 0, 0
        self.started, self.kept, self.maybe = [], [], []

    def make(self, src, dst, dev):
        i = self.n
        self.n += 1
        return pltpu.make_async_remote_copy(
            src_ref=src,
            dst_ref=dst,
            send_sem=self.send.at[i],
            recv_sem=self.recv.at[i],
            device_id=dev,
            device_id_type=MESH_ID,
        )

    def copy(self, src, dst, dev):
        made = self.make(src, dst, dev)
        made.start()
        self.started.append(made)
        return made

    def copy_if(self, wanted, src, dst, dev):
        made = self.make(src, dst, dev)

        @pl.when(wanted)
        def _():
            made.start()

        self.maybe.append((wanted, made))
        return made

    def here(self, src, dst):
        made = pltpu.make_async_copy(src, dst, self.local.at[self.m])
        self.m += 1
        made.start()
        return made

    def keep(self, src, dst):
        self.kept.append(self.here(src, dst))

    def finish(self, done=()):
        for made in self.started:
            if all(made is not other for other in done):
                made.wait_send()
        for made in self.kept:
            made.wait()
        for wanted, made in self.maybe:
            pl.when(wanted)(made.wait_send)


def barrier(devices):
    sem = pltpu.get_barrier_semaphore()
    for dev in devices:
        pl.semaphore_signal(sem, inc=1, device_id=dev, device_id_type=MESH_ID)
    pl.semaphore_wait(sem, len(devices))


def gather_ring(net, me, own, other, out, lead, lanes, near=True, far=True):
    z, y, h = me.z, me.y, me.h
    g = 1 - h
    low, high = lanes
    every = slice(None)

    def at(z, y, h, lane=None):
        index = [every] * lead + [z, y, h]
        if lane is not None:
            index += [every, lane]
        return out.at[tuple(index)]

    def same(piece, dev):
        return net.copy(piece, piece, dev)

    waits_a, waits_b = [], []
    if near:
        x = net.copy(other, at(z, y, h), me.ring(z, y, g))
        a_up = net.copy(own, at(z, y, h), me.ring(z, up(y), h))
        a_down = net.copy(own, at(z, y, h), me.ring(z, down(y), h))
        kept = net.here(own, at(z, y, h))
        yield
        x.wait_recv()
        b_up = same(at(z, y, g), me.ring(up(z), y, h))
        b_down = same(at(z, y, g), me.ring(down(z), y, h))
        yield
        a_up.wait_recv()
        a2_up = same(at(z, down(y), h, low), me.ring(z, up(y), h))
        a_down.wait_recv()
        a2_down = same(at(z, up(y), h, high), me.ring(z, down(y), h))
        yield
        b_up.wait_recv()
        b2_up = same(at(down(z), y, g, low), me.ring(up(z), y, h))
        b_down.wait_recv()
        b2_down = same(at(up(z), y, g, high), me.ring(down(z), y, h))
        yield
        kept.wait()
        waits_a, waits_b = [a2_up, a2_down], [b2_up, b2_down]
    for made in waits_a:
        made.wait_recv()
    if far:
        c_up = same(at(z, every, h), me.ring(up(z), y, h))
        c_down = same(at(z, every, h), me.ring(down(z), y, h))
        yield
    for made in waits_b:
        made.wait_recv()
    if far:
        d_up = same(at(every, y, g), me.ring(z, up(y), h))
        d_down = same(at(every, y, g), me.ring(z, down(y), h))
        yield
        c_up.wait_recv()
        c2_up = same(at(down(z), slice(0, 2), h), me.ring(up(z), y, h))
        c_down.wait_recv()
        c2_down = same(at(up(z), slice(2, 4), h), me.ring(down(z), y, h))
        yield
        d_up.wait_recv()
        d2_up = same(at(slice(0, 2), down(y), g), me.ring(z, up(y), h))
        d_down.wait_recv()
        d2_down = same(at(slice(2, 4), up(y), g), me.ring(z, down(y), h))
        yield
        for made in (c2_up, c2_down, d2_up, d2_down):
            made.wait_recv()


def gather_direct(net, me, own, other, out):
    z, y, h = me.z, me.y, me.h
    g = 1 - h
    others = (2, 1, 3)

    def along_y(src, dst):
        return [net.copy(src, dst, me.ring(z, lax.rem(y + j, 4), h)) for j in others]

    def along_z(src, dst):
        return [net.copy(src, dst, me.ring(lax.rem(z + j, 4), y, h)) for j in others]

    x = net.copy(other, out.at[z, y, h], me.ring(z, y, g))
    a = along_y(own, out.at[z, y, h])
    kept = net.here(own, out.at[z, y, h])
    yield
    x.wait_recv()
    b = along_z(out.at[z, y, g], out.at[z, y, g])
    for made in a:
        made.wait_recv()
    kept.wait()
    line = out.at[z, :, h]
    c = along_z(line, line)
    yield
    for made in b:
        made.wait_recv()
    line = out.at[:, y, g]
    d = along_y(line, line)
    yield
    for made in c + d:
        made.wait_recv()


def gather_chips(net, me, buf):
    x, k = me.x, me.k
    first, last = slice(0, ROWS // 2), slice(ROWS // 2, ROWS)

    def send(x_at, rows, dev):
        piece = buf.at[x_at * 2 + k] if rows is None else buf.at[x_at * 2 + k, rows]
        return net.copy(piece, piece, dev)

    to_up, to_down = me.chip(up(x), k), me.chip(down(x), k)
    c0 = send(x, None, me.core)
    a1 = send(x, first, to_up)
    b1 = send(x, last, to_down)
    a2 = send(x, last, to_up)
    b2 = send(x, first, to_down)
    yield
    c0.wait_recv()
    yield
    a1.wait_recv()
    f1 = send(down(x), first, to_up)
    b1.wait_recv()
    f2 = send(up(x), last, to_down)
    yield
    a2.wait_recv()
    g1 = send(down(x), None, me.core)
    b2.wait_recv()
    g2 = send(up(x), None, me.core)
    yield
    g1.wait_recv()
    g2.wait_recv()
    yield
    f1.wait_recv()
    f2.wait_recv()
    g3 = send(opposite(x), None, me.core)
    yield
    g3.wait_recv()


def gather_block(net, me, buf):
    own = buf.at[me.t]
    far = buf.at[(1 - me.xl) * 2 + me.k]
    b = net.copy(own, own, me.side)
    a = net.copy(own, own, me.core)
    yield
    b.wait_recv()
    c = net.copy(far, far, me.core)
    yield
    a.wait_recv()
    c.wait_recv()


def sum_block(net, me, part, s1, r1, s2, r2, make=None):
    far, near, k = 1 - me.xl, me.xl, me.k
    sent = []
    for i in (far, near):
        if make is not None:
            make(i)
        s1[i] = part[i * 2 + 1 - k].astype(BF16)
        sent.append(net.copy(s1.at[i], r1.at[i], me.core))
    yield None
    sent[0].wait_recv()
    s2[...] = (part[far * 2 + k] + r1[far].astype(F32)).astype(BF16)
    last = net.copy(s2, r2, me.side)
    yield None
    sent[1].wait_recv()
    total = part[me.t] + r1[near].astype(F32)
    last.wait_recv()
    yield total + r2[...].astype(F32)


def rms(v):
    return lax.rsqrt(jnp.mean(v * v, axis=-1, keepdims=True) + NORM_EPS)


def spin(v, cosine, sine):
    return v * cosine + pltpu.roll(v, HD // 2, 1) * sine


def half_start(me, half):
    return me.c * 512 + half * HALF


def mask_of(me, half, begin, j, last):
    key = lax.broadcasted_iota(jnp.int32, (SPAN, HALF), 0) + j * SPAN
    allowed = key >= begin
    if last:
        query = lax.broadcasted_iota(jnp.int32, (SPAN, HALF), 1) + half_start(me, half)
        allowed = allowed & (key <= query)
    return allowed


def span_of(kv_ref, j, which):
    return kv_ref[pl.ds(2 * j, 2), which].reshape(SPAN, HD)


TILES = [(half, head) for half in range(2) for head in range(3)]


def tile_lanes(i):
    return slice(i * HALF, (i + 1) * HALF)


def masks_of(me, begin_ref, j, last):
    return [mask_of(me, half, begin_ref[half : half + 1, :], j, last) for half in range(2)]


def attend(me, half, q_ref, kv_ref, begin_ref, att_ref, lse_ref):
    begin = begin_ref[half : half + 1, :]
    top = me.c

    def step(j, carry, last):
        keys = span_of(kv_ref, j, 0)
        values = span_of(kv_ref, j, 1).astype(F32).T.astype(BF16)
        allowed = mask_of(me, half, begin, j, last)
        out = []
        for head in range(3):
            high, total, summed = carry[head]
            raw = dot_nt(keys, q_ref[half, head]) * ROOT2
            raw = jnp.where(allowed, raw, MASKED)
            new = jnp.maximum(high, jnp.max(raw, axis=0, keepdims=True))
            probs = jnp.exp2(raw - new)
            fade = jnp.exp2(high - new)
            total = total * fade + jnp.sum(probs, axis=0, keepdims=True)
            summed = summed * fade + dot_nn(values, probs.astype(BF16))
            out.append((new, total, summed))
        return tuple(out)

    zero = (
        jnp.full((1, HALF), MASKED, F32),
        jnp.zeros((1, HALF), F32),
        jnp.zeros((HD, HALF), F32),
    )
    carry = step(top, (zero,) * 3, True)
    carry = lax.fori_loop(0, top, lambda i, carry: step(top - 1 - i, carry, False), carry)
    for head in range(3):
        high, total, summed = carry[head]
        att_ref[half, head] = (summed / total).T
        lse_ref[half * 3 + head : half * 3 + head + 1, :] = high + jnp.log2(total)

class Refs:
    def __init__(self, names, refs):
        for name, ref in zip(names, refs):
            setattr(self, name, ref)


class ChipSum:
    def __init__(self, net, me, src, mine, bufs):
        self.net, self.me, self.src, self.mine = net, me, src, mine
        self.r1, self.a1, self.a2, self.ru, self.rd = bufs
        self.pushed = {}
        x = me.x
        self.order = {"far": opposite(x), "above": up(x), "below": down(x), "own": x}

    def push(self, name):
        i = self.order[name]
        self.pushed[name] = self.net.copy(
            self.src.at[i, 1 - self.me.k], self.r1.at[i], self.me.core
        )

    def add(self, name):
        i = self.order[name]
        self.pushed[name].wait_recv()
        self.r1[i] = (self.r1[i].astype(F32) + self.mine(i).astype(F32)).astype(BF16)
        return i

    def steps(self):
        net, me = self.net, self.me
        r1, a1, a2, ru, rd = self.r1, self.a1, self.a2, self.ru, self.rd
        first, last = slice(0, ROWS // 2), slice(ROWS // 2, ROWS)
        to_up, to_down = me.chip(up(me.x), me.k), me.chip(down(me.x), me.k)
        far = self.add("far")
        e1 = net.copy(r1.at[far, first], a1, to_up)
        e2 = net.copy(r1.at[far, last], a2, to_down)
        yield None
        above = self.add("above")
        e3 = net.copy(r1.at[above, last], ru.at[last], to_up)
        yield None
        below = self.add("below")
        e4 = net.copy(r1.at[below, first], rd.at[first], to_down)
        yield None
        x = self.add("own")
        e1.wait_recv()
        a1[...] = (a1[...].astype(F32) + r1[above, first].astype(F32)).astype(BF16)
        e5 = net.copy(a1, ru.at[first], to_up)
        e2.wait_recv()
        a2[...] = (a2[...].astype(F32) + r1[below, last].astype(F32)).astype(BF16)
        e6 = net.copy(a2, rd.at[last], to_down)
        yield None
        for made in (e3, e4, e5, e6):
            made.wait_recv()
        yield r1[x].astype(F32) + ru[...].astype(F32) + rd[...].astype(F32)


CHIP_BUFS = [
    ((4, ROWS, D), BF16),
    ((ROWS // 2, D), BF16),
    ((ROWS // 2, D), BF16),
    ((ROWS, D), BF16),
    ((ROWS, D), BF16),
]


FRONT_IN = ["x", "cot", "gains", "bias", "cos", "sin", "begin", "p1", "po", "p2", "pd"]
FRONT_OUT = ["feed", "wd", "o_small", "o_wo", "o_normed", "o_q", "o_kv", "o_att"]
FRONT_OUT += ["lse", "hid", "n2", "cot8"]
FRONT_SCRATCH = {
    "small": ((4, 4, 2, PIECE, 640), BF16),
    "wo": ((4, 4, 2, PIECE, QW), BF16),
    "normed": ((4, ROWS, D), BF16),
    "q": ((2, 3, HALF, HD), BF16),
    "kv": ((16, 2, HALF, HD), BF16),
    "att": ((2, 3, HALF, HD), F32),
    "cs": ((8, ROWS, D), BF16),
    "part": ((4, ROWS, D), F32),
    "s1": ((2, ROWS, D), BF16),
    "r1": ((2, ROWS, D), BF16),
    "s2": ((ROWS, D), BF16),
    "r2": ((ROWS, D), BF16),
}


def front_kernel(*refs):
    names = FRONT_IN + FRONT_OUT + list(FRONT_SCRATCH)
    r = Refs(names, refs)
    send, recv, local = refs[len(names) :]
    me = Place()
    net = Net(send, recv, local)
    z, y, h, x, k, c = me.z, me.y, me.h, me.x, me.k, me.c
    slot = x * 2 + k
    barrier(
        [me.block(lax.rem(c + j, 8), k) for j in range(1, 8)]
        + [me.ring(lax.rem(z + j, 4), y, h) for j in (1, 2, 3)]
        + [me.chip(up(x), k), me.chip(down(x), k), me.core]
    )
    ring = gather_direct(net, me, r.p1, r.p1, r.small)
    next(ring)
    r.cs[slot] = r.cot[...]
    own = r.x[...].astype(F32)
    r.normed[me.t] = (own * rms(own) * r.gains[0:1, :]).astype(BF16)
    block = gather_block(net, me, r.normed)
    next(block)
    next(ring)
    feed = gather_ring(
        net, me, r.p2.at[h], r.p2.at[1 - h], r.feed, 1, (slice(0, 640), slice(640, FPAD))
    )
    lanes = (slice(0, 640), slice(640, FPAD))
    down_near = gather_ring(net, me, r.pd.at[h], r.pd.at[1 - h], r.wd, 0, lanes, far=False)
    outer = gather_direct(net, me, r.po, r.po, r.wo)
    next(ring)
    next(feed)
    next(block)
    for _ in block:
        pass
    for _ in ring:
        pass
    net.keep(r.small, r.o_small)
    net.keep(r.normed, r.o_normed)
    normed = r.normed[...].reshape(512, D)
    cosine, sine = r.cos[...], r.sin[...]
    proj = dot_nn(normed, r.small[:, :, :, :, QW:640].reshape(D, 2 * HD)) + r.bias[:, QW:640]
    keys = spin(proj[:, :HD], cosine, sine).astype(BF16)
    values = proj[:, HD:].astype(BF16)
    for half in range(2):
        rows = slice(half * HALF, (half + 1) * HALF)
        r.kv[2 * c + half, 0] = keys[rows]
        r.kv[2 * c + half, 1] = values[rows]
    own_kv = r.kv.at[2 * c + k]
    order = (4, 3, 5, 2, 6, 1, 7)
    kv_sent = [
        net.copy_if(c + j < 8, own_kv, own_kv, me.block(lax.rem(c + j, 8), k)) for j in order
    ]
    next(outer)
    proj = dot_nn(normed, r.small[:, :, :, :, 0:QW].reshape(D, QW)) + r.bias[:, 0:QW]
    for head in range(3):
        query = spin(proj[:, head * HD : (head + 1) * HD], cosine, sine).astype(BF16)
        r.q[0, head] = query[:HALF]
        r.q[1, head] = query[HALF:]
    net.keep(r.q, r.o_q)
    next(feed)
    next(feed)
    next(outer)
    next(feed)
    next(feed)
    next(feed)
    passed = []
    for j, made in zip(order, kv_sent):
        pl.when(c >= j)(made.wait_recv)
        there = r.kv.at[2 * lax.rem(c + 8 - j, 8) + k]
        passed.append(net.copy_if(c >= j, there, there, me.core))
    cots = gather_chips(net, me, r.cs)
    next(cots)
    next(outer)
    for j, made in zip(order, passed):
        pl.when(c >= j)(made.wait_recv)
    net.keep(r.kv, r.o_kv)
    next(down_near)
    attend(me, 0, r.q, r.kv, r.begin, r.att, r.lse)
    next(down_near)
    next(cots)
    next(cots)
    attend(me, 1, r.q, r.kv, r.begin, r.att, r.lse)
    next(down_near)
    next(down_near)
    next(feed)
    net.keep(r.att, r.o_att)
    next(cots)
    for _ in outer:
        pass
    net.keep(r.wo, r.o_wo)

    def project(half):
        mixed = jnp.concatenate([r.att[half, head].astype(BF16) for head in range(3)], axis=1)
        r.part[pl.ds(2 * half, 2)] = dot_nt(mixed, r.wo[...].reshape(D, QW)).reshape(2, ROWS, D)

    summed = sum_block(net, me, r.part, r.s1, r.r1, r.s2, r.r2, project)
    next(summed)
    next(cots)
    next(cots)
    next(summed)
    next(feed)
    for _ in down_near:
        pass
    for _ in cots:
        pass
    net.keep(r.cs, r.cot8)
    branch = next(summed)
    hidden = own + branch
    r.hid[...] = hidden
    r.n2[...] = (hidden * rms(hidden) * r.gains[1:2, :]).astype(BF16)
    for _ in feed:
        pass
    net.finish()


def call(kernel, ins, arrays, outs, far, scratch, collective, limit, name):
    vmem = pl.BlockSpec(memory_space=pltpu.VMEM)
    hbm = pl.BlockSpec(memory_space=pl.ANY)
    return pl.pallas_call(
        kernel,
        out_shape=tuple(jax.ShapeDtypeStruct(*s) for s in outs.values()),
        in_specs=[hbm if n in far else vmem for n in ins],
        out_specs=tuple(hbm if n in far else vmem for n in outs),
        scratch_shapes=scratch,
        compiler_params=pltpu.CompilerParams(
            collective_id=collective, has_side_effects=True, vmem_limit_bytes=limit * 2**20
        ),
        name=name,
    )(*arrays)


def semaphores(*counts):
    return [pltpu.SemaphoreType.DMA((n,)) for n in counts]


def scratch_of(shapes):
    return [pltpu.VMEM(*s) for s in shapes.values()]


def front(*arrays):
    shapes = (
        ((2, 4, 4, 2, PIECE, FPAD), BF16),
        ((4, 4, 2, PIECE, FPAD), BF16),
        ((4, 4, 2, PIECE, 640), BF16),
        ((4, 4, 2, PIECE, QW), BF16),
        ((4, ROWS, D), BF16),
        ((2, 3, HALF, HD), BF16),
        ((16, 2, HALF, HD), BF16),
        ((2, 3, HALF, HD), F32),
        ((8, HALF), F32),
        ((ROWS, D), F32),
        ((ROWS, D), BF16),
        ((8, ROWS, D), BF16),
    )
    return call(
        front_kernel,
        FRONT_IN,
        arrays,
        dict(zip(FRONT_OUT, shapes)),
        ("p2", "pd", "feed", "wd", "cot8", *FRONT_OUT[2:8]),
        scratch_of(FRONT_SCRATCH) + semaphores(110, 110, 16),
        0,
        63,
        "front",
    )


def ring_sum(net, pick, here, to_up, to_down, cut, add, a1, a2, ru, rd, terms=None):
    above, below, far = up(here), down(here), opposite(here)
    if terms is None:
        terms = (pick(above, 0), pick(below, 1))
    e1 = net.copy(pick(far, 0), a1, to_up)
    e2 = net.copy(pick(far, 1), a2, to_down)
    e3 = net.copy(pick(above, 1), cut(ru, 1), to_up)
    e4 = net.copy(pick(below, 0), cut(rd, 0), to_down)
    yield
    e1.wait_recv()
    add(a1, terms[0])
    e5 = net.copy(a1, cut(ru, 0), to_up)
    e2.wait_recv()
    add(a2, terms[1])
    e6 = net.copy(a2, cut(rd, 1), to_down)
    yield
    for made in (e3, e4, e5, e6):
        made.wait_recv()


def add_pieces(lead):
    def add(dst, *srcs):
        count = math.prod(dst.shape[:-2])
        inner = dst.shape[lead] if len(dst.shape) > lead + 2 else 1

        def one(i, carry):
            if len(dst.shape) == 2:
                at = (slice(None), slice(None))
            elif len(dst.shape) == 3:
                at = (i,)
            else:
                at = (i // inner, lax.rem(i, inner))
            total = dst[at].astype(F32)
            for src in srcs:
                total = total + src[at].astype(F32)
            dst[at] = total.astype(dst.dtype)
            return carry

        if count == 1:
            one(0, 0)
        else:
            lax.fori_loop(0, count, one, 0)

    return add


RING_BUFS = ("a1", "a2", "ru", "rd", "b1", "b2", "su", "sd")


def ring_bufs(lead, width, low):
    pair = (*lead, 2, PIECE, width)
    four = (*lead, 4, PIECE, width)
    one = (*lead, PIECE, width)
    shapes = (
        pair,
        pair,
        four,
        four,
        (*lead, PIECE, low),
        (*lead, PIECE, width - low),
        one,
        one,
    )
    return [pltpu.VMEM(s, BF16) for s in shapes] * 2


def reduce_ring(net, me, grad, lead, low, bufs, landing, loads=None):
    z, y, h = me.z, me.y, me.h
    g = 1 - h
    every = slice(None)
    width = grad.shape[-1]
    lanes = (slice(0, low), slice(low, width))
    pairs = (slice(0, 2), slice(2, 4))
    own = dict(zip(RING_BUFS, bufs[:8]))
    other = dict(zip(RING_BUFS, bufs[8:]))
    add = add_pieces(lead)

    def front_of(ref, *index):
        return ref.at[(every,) * lead + index]

    def cut_pair(ref, part):
        return front_of(ref, pairs[part])

    def cut_lane(ref, part):
        return front_of(ref, every, lanes[part])

    ring_z = (me.ring(up(z), y, h), me.ring(down(z), y, h))
    ring_y = (me.ring(z, up(y), h), me.ring(z, down(y), h))
    a_at = lambda i, part: front_of(grad, i, pairs[part], h)
    b_at = lambda i, part: front_of(grad, pairs[part], i, g)
    a_terms = (a_at(up(z), 0), a_at(down(z), 1), front_of(grad, z, every, h))
    b_terms = (b_at(up(y), 0), b_at(down(y), 1), front_of(grad, every, y, g))
    loading = []
    if loads is not None:
        loading = [net.here(s, d) for s, d in zip(a_terms + b_terms, loads)]
        a_terms, b_terms = loads[:3], loads[3:]
    a = ring_sum(
        net, a_at, z, *ring_z, cut_pair, add, *(own[n] for n in RING_BUFS[:4]), a_terms
    )
    b = ring_sum(
        net, b_at, y, *ring_y, cut_pair, add, *(other[n] for n in RING_BUFS[:4]), b_terms
    )
    next(a)
    next(b)
    yield
    for made in loading:
        made.wait()
    next(a)
    next(b)
    yield
    for _ in a:
        pass
    add(own["ru"], own["rd"], a_terms[2])
    a = ring_sum(
        net,
        lambda i, part: front_of(own["ru"], i, every, lanes[part]),
        y,
        *ring_y,
        cut_lane,
        add,
        *(own[n] for n in RING_BUFS[4:]),
    )
    next(a)
    for _ in b:
        pass
    add(other["ru"], other["rd"], b_terms[2])
    b = ring_sum(
        net,
        lambda i, part: front_of(other["ru"], i, every, lanes[part]),
        z,
        *ring_z,
        cut_lane,
        add,
        *(other[n] for n in RING_BUFS[4:]),
    )
    next(b)
    yield
    next(a)
    next(b)
    yield
    for _ in b:
        pass
    add(other["su"], other["sd"], front_of(other["ru"], z))
    last = net.copy(other["su"], landing, me.ring(z, y, g))
    for _ in a:
        pass
    add(own["su"], own["sd"], front_of(own["ru"], y))
    yield
    last.wait_recv()


MID_IN = ["n2", "cot8", "w", "wdn", "hid", "gains"]
MID_OUT = ["out", "g", "gd", "dbr", "dh", "gain"]
MID_SCRATCH = {
    "x8": ((8, ROWS, D), BF16),
    "c8": ((8, ROWS, D), BF16),
    "w8": ((2, D, FPAD), BF16),
    "wd": ((4, 4, 2, PIECE, FPAD), BF16),
    "act": ((8, ROWS, FPAD), BF16),
    "dg": ((8, ROWS, FPAD), BF16),
    "du": ((8, ROWS, FPAD), BF16),
    "out8": ((4, 2, ROWS, D), BF16),
    "dn2": ((4, 2, ROWS, D), BF16),
    "g8": ((2, D, FPAD), BF16),
    "gd8": ((4, 4, 2, PIECE, FPAD), BF16),
}
LANES = [slice(i * 256, i * 256 + 256) for i in range(4)] + [slice(1024, FPAD)]


def tile(i, size):
    return pl.ds(pl.multiple_of(i * size, size), size)


def hidden_units(r, chip):
    at = pl.ds(2 * chip, 2)
    left = r.x8[at].reshape(2 * ROWS, D)
    for lanes in LANES:
        gate = dot_nn(left, r.w8[0, :, lanes])
        lift = dot_nn(left, r.w8[1, :, lanes])
        sigma = 1.0 / (1.0 + jnp.exp(-gate))
        silu = gate * sigma
        pieces = (
            (r.act, silu * lift),
            (r.du, silu),
            (r.dg, lift * (sigma * (1.0 + gate * (1.0 - sigma)))),
        )
        for ref, value in pieces:
            ref[at, :, lanes] = value.astype(BF16).reshape(2, ROWS, value.shape[1])


def unit_gradients(r):
    back = r.c8[...].reshape(8 * ROWS, D)
    for lanes in LANES:
        d_act = dot_nn(back, r.wd[:, :, :, :, lanes].reshape(D, lanes.stop - lanes.start))
        d_act = d_act.reshape(8, ROWS, lanes.stop - lanes.start)
        for ref in (r.du, r.dg):
            ref[:, :, lanes] = (d_act * ref[:, :, lanes].astype(F32)).astype(BF16)


def gradient_rows(r, chip):
    at = pl.ds(2 * chip, 2)
    dg, du = (ref[at].reshape(2 * ROWS, FPAD) for ref in (r.dg, r.du))

    def one(j, carry):
        wide = tile(j, 512)
        both = dot_nt(dg, r.w8[0, wide, :]) + dot_nt(du, r.w8[1, wide, :])
        r.dn2[chip, :, :, wide] = both.astype(BF16).reshape(2, ROWS, 512)
        return carry

    lax.fori_loop(0, 3, one, 0)


def mid_kernel(*refs):
    names = MID_IN + MID_OUT + list(MID_SCRATCH)
    r = Refs(names, refs)
    rest = refs[len(names) :]
    bufs, ring_bufs_d = rest[:5], rest[5:21]
    send, recv, local = rest[21:]
    me = Place()
    net = Net(send, recv, local)
    x, k, t = me.x, me.k, me.t
    z, y, h = me.z, me.y, me.h
    lines = [(z, slice(None), h), (slice(None), y, 1 - h)]
    near = [net.here(r.wdn.at[at], r.wd.at[at]) for at in lines]
    load_w = net.here(r.w, r.w8)
    load_c = net.here(r.cot8, r.c8)
    barrier(
        [me.chip(up(x), k), me.chip(down(x), k), me.core]
        + [me.ring(up(z), y, h), me.ring(down(z), y, h)]
        + [me.ring(z, up(y), h), me.ring(z, down(y), h)]
    )
    r.x8[x * 2 + k] = r.n2[...]
    rows = gather_chips(net, me, r.x8)
    next(rows)
    ring = gather_ring(net, me, None, None, r.wd, 0, (None, None), near=False)
    for made in near:
        made.wait()
    next(ring)
    next(ring)
    load_w.wait()
    next(rows)
    next(rows)
    hidden_units(r, x)
    next(rows)
    next(rows)
    hidden_units(r, down(x))
    next(ring)
    next(ring)
    next(rows)
    hidden_units(r, up(x))
    for _ in rows:
        pass
    hidden_units(r, opposite(x))
    load_c.wait()
    act = r.act[...].reshape(8 * ROWS, FPAD)
    for i in range(2):
        left = r.c8[:, :, i * 768 : i * 768 + 768].reshape(8 * ROWS, 768).T
        r.gd8[2 * i : 2 * i + 2] = dot_nn(left, act).astype(BF16).reshape(2, 4, 2, PIECE, FPAD)
    for _ in ring:
        pass
    down_ring = reduce_ring(net, me, r.gd8, 0, 640, ring_bufs_d, r.gd.at[h])
    next(down_ring)
    unit_gradients(r)
    norm2 = ChipSum(net, me, r.dn2, lambda i: r.dn2[i, k], bufs)
    steps = norm2.steps()
    gradient_rows(r, opposite(x))
    norm2.push("far")
    gradient_rows(r, up(x))
    norm2.push("above")
    next(steps)
    next(down_ring)
    gradient_rows(r, down(x))
    norm2.push("below")
    next(steps)
    gradient_rows(r, x)
    norm2.push("own")
    next(steps)
    next(steps)
    dg, du = (ref[...].reshape(8 * ROWS, FPAD) for ref in (r.dg, r.du))

    def grads(i):
        wide = slice(i * 768, i * 768 + 768)
        left = r.x8[:, :, wide].reshape(8 * ROWS, 768).T
        r.g8[0, wide, :] = dot_nn(left, dg).astype(BF16)
        r.g8[1, wide, :] = dot_nn(left, du).astype(BF16)

    next(down_ring)
    grads(0)
    next(down_ring)

    def one(j, carry):
        wide = tile(j, 384)
        right = r.wd[j].reshape(384, FPAD)
        r.out8[:, :, :, wide] = dot_nt(act, right).astype(BF16).reshape(4, 2, ROWS, 384)
        return carry

    lax.fori_loop(0, 2, one, 0)
    next(down_ring)
    d_norm2 = next(steps)
    hidden = r.hid[...]
    scale2 = rms(hidden)
    xh2 = hidden * scale2
    e2 = d_norm2 * r.gains[1:2, :]
    d_hidden = r.c8[x * 2 + k].astype(F32) + scale2 * (
        e2 - xh2 * jnp.mean(e2 * xh2, axis=-1, keepdims=True)
    )
    r.dh[...] = d_hidden
    r.gain[...] = jnp.sum(d_norm2 * xh2, axis=0, keepdims=True)
    r.dbr[t] = d_hidden.astype(BF16)
    branch = gather_block(net, me, r.dbr)
    next(branch)
    grads(1)
    net.keep(r.g8, r.g)
    next(branch)
    lax.fori_loop(2, 4, one, 0)
    net.keep(r.out8, r.out)
    for _ in branch:
        pass
    for _ in down_ring:
        pass
    r.gd[h] = ring_bufs_d[6][...]
    net.finish()


def mid(*arrays):
    shapes = (
        ((4, 2, ROWS, D), BF16),
        ((2, D, FPAD), BF16),
        ((2, PIECE, FPAD), BF16),
        ((4, ROWS, D), BF16),
        ((ROWS, D), F32),
        ((1, D), F32),
    )
    return call(
        mid_kernel,
        MID_IN,
        arrays,
        dict(zip(MID_OUT, shapes)),
        ("cot8", "w", "wdn", "out", "g"),
        scratch_of(MID_SCRATCH) + [pltpu.VMEM(*s) for s in CHIP_BUFS]
        + ring_bufs((), FPAD, 640)
        + semaphores(64, 64, 12),
        1,
        63,
        "mid",
    )


def columns_by_row(rows_ref, blocks, right, out):
    count = right.shape[0]
    for i in range(4):
        left = rows_ref[blocks, :, i * 384 : (i + 1) * 384].reshape(count, 384)
        out[i] = dot_tn(left, right).astype(BF16).reshape(out.shape[1:])


def direct_bufs(width):
    far, line, one = (3, 4, PIECE, width), (4, PIECE, width), (PIECE, width)
    return [pltpu.VMEM(s, BF16) for s in (far, far, line, line, (3, *one), (3, *one), one, one)]


def reduce_direct(net, me, grad, bufs, landing):
    z, y, h = me.z, me.y, me.h
    g = 1 - h
    ra, rb, la, lb, sa, sb, own, other = bufs
    others = (2, 1, 3)

    def to_y(pick, bufs):
        at = [lax.rem(y + j, 4) for j in others]
        return [net.copy(pick(i), bufs.at[n], me.ring(z, i, h)) for n, i in enumerate(at)]

    def to_z(pick, bufs):
        at = [lax.rem(z + j, 4) for j in others]
        return [net.copy(pick(i), bufs.at[n], me.ring(i, y, h)) for n, i in enumerate(at)]

    def total(sent, first, bufs):
        for made in sent:
            made.wait_recv()
        return first.astype(F32) + (
            bufs[0].astype(F32) + bufs[1].astype(F32) + bufs[2].astype(F32)
        )

    a = to_z(lambda i: grad.at[i, :, h], ra)
    b = to_y(lambda i: grad.at[:, i, g], rb)
    yield
    lb[...] = total(b, grad[:, y, g], rb).astype(BF16)
    b = to_z(lambda i: lb.at[i], sb)
    la[...] = total(a, grad[z, :, h], ra).astype(BF16)
    a = to_y(lambda i: la.at[i], sa)
    yield
    other[...] = total(b, lb[z], sb).astype(BF16)
    last = net.copy(other, landing, me.ring(z, y, g))
    own[...] = total(a, la[y], sa).astype(BF16)
    yield
    last.wait_recv()


def attend_back(me, r, delta):
    queries = r.q[...].reshape(6 * HALF, HD)
    d_outs = r.dm[...].reshape(6 * HALF, HD)

    def step(j, last):
        keys = span_of(r.kv, j, 0)
        values = span_of(r.kv, j, 1)
        keys_t = keys.astype(F32).T.astype(BF16)
        allowed = masks_of(me, r.begin, j, last)
        for i, (half, head) in enumerate(TILES):
            raw = dot_nt(keys, r.q[half, head]) * ROOT2 - r.lse[i : i + 1, :]
            probs = jnp.exp2(jnp.where(allowed[half], raw, MASKED))
            d_probs = dot_nt(values, r.dm[half, head])
            r.probs[:, tile_lanes(i)] = probs.astype(BF16)
            r.d_raw[:, tile_lanes(i)] = (probs * (d_probs - delta[i])).astype(BF16)
        d_raw = r.d_raw[...]
        at = pl.ds(2 * j, 2)
        r.dkv[at, 0] = dot_nn(d_raw, queries).reshape(2, HALF, HD)
        r.dkv[at, 1] = dot_nn(r.probs[...], d_outs).reshape(2, HALF, HD)
        r.dq_t[...] += dot_nn(keys_t, d_raw)

    r.dq_t[...] = jnp.zeros_like(r.dq_t)
    step(me.c, True)

    def earlier(i, carry):
        step(me.c - 1 - i, False)
        return carry

    lax.fori_loop(0, me.c, earlier, 0)
    for i, (half, head) in enumerate(TILES):
        rows = tile_lanes(half)
        back = r.dq_t[:, tile_lanes(i)].T * INV_ROOT
        back = back * r.cos[rows, :] - pltpu.roll(back, HD // 2, 1) * r.sin[rows, :]
        r.dq[rows, head * HD : (head + 1) * HD] = back.astype(BF16)


def to_lines(ref, at, row):
    for i in range(row.shape[1] // HD):
        ref[pl.ds(at + i, 1), :] = row[:, i * HD : (i + 1) * HD]


class Total:
    def __init__(self, net, me, value, xb, yzb):
        self.net, self.me, self.xb, self.yzb = net, me, xb, yzb
        at = me.x * 2 + me.k
        xb[at] = value
        self.sent = []
        for j in range(4):
            for other in range(2):
                if j == 0 and other == 0:
                    continue
                core = me.k if other == 0 else 1 - me.k
                dev = me.chip(lax.rem(me.x + j, 4), core)
                self.sent.append(net.copy(xb.at[at], xb.at[at], dev))

    def second(self):
        net, me = self.net, self.me
        for made in self.sent:
            made.wait_recv()
        total = self.xb[0]
        for i in range(1, 8):
            total = total + self.xb[i]
        at = me.z * 4 + me.y
        self.yzb[at] = total
        self.sent = []
        for j in range(1, 16):
            z, y = lax.rem(me.z + j // 4, 4), lax.rem(me.y + j % 4, 4)
            piece = self.yzb.at[at]
            self.sent.append(net.copy(piece, piece, me.ring(z, y, me.h)))

    def final(self):
        for made in self.sent:
            made.wait_recv()
        total = self.yzb[0]
        for i in range(1, 16):
            total = total + self.yzb[i]
        return total


BACK_IN = ["outp", "gfeed", "dbr", "dh", "gain", "hid", "x", "small", "wo", "normed"]
BACK_IN += ["q", "kv", "att", "lse", "cos", "sin", "begin", "gains"]
BACK_OUT = ["result", "igrad", "gf", "gsm", "gpair", "total"]
BACK_SCRATCH = {
    "v_small": ((4, 4, 2, PIECE, 640), BF16),
    "v_wo": ((4, 4, 2, PIECE, QW), BF16),
    "v_normed": ((4, ROWS, D), BF16),
    "v_dbr": ((4, ROWS, D), BF16),
    "v_outp": ((4, ROWS, D), BF16),
    "v_kv": ((16, 2, HALF, HD), BF16),
    "mixed": ((512, QW), BF16),
    "dm": ((2, 3, HALF, HD), BF16),
    "dq": ((512, QW), BF16),
    "dkv": ((16, 2, HALF, HD), F32),
    "k_send": ((8, 2, HALF, HD), BF16),
    "k_recv": ((8, 2, HALF, HD), BF16),
    "k_far": ((7, 2, HALF, HD), BF16),
    "probs": ((SPAN, 6 * HALF), BF16),
    "d_raw": ((SPAN, 6 * HALF), BF16),
    "dq_t": ((HD, 6 * HALF), F32),
    "d_kv": ((2, HALF, HD), F32),
    "dpair": ((HALF, 2 * HD), BF16),
    "part": ((4, ROWS, D), F32),
    "s1": ((2, ROWS, D), BF16),
    "r1": ((2, ROWS, D), BF16),
    "s2": ((ROWS, D), BF16),
    "r2": ((ROWS, D), BF16),
    "g_q": ((4, 4, 2, PIECE, QW), BF16),
    "g_o": ((4, 4, 2, PIECE, QW), BF16),
    "g_kv": ((4, 4, 2, PIECE, 2 * HD), BF16),
    "p_send": ((4, 4, 2, PIECE, 2 * HD), BF16),
    "p_recv": ((4, 4, 2, PIECE, 2 * HD), BF16),
    "l_q": ((PIECE, QW), BF16),
    "l_o": ((PIECE, QW), BF16),
    "l_kv": ((PIECE, 2 * HD), BF16),
    "kv_own": ((PIECE, 2 * HD), BF16),
    "kv_far": ((PIECE, 2 * HD), BF16),
    "tot": ((40, HD), F32),
    "t_x": ((8, 40, HD), F32),
    "t_yz": ((16, 40, HD), F32),
}


def back_kernel(*refs):
    names = BACK_IN + BACK_OUT + list(BACK_SCRATCH)
    r = Refs(names, refs)
    rest = refs[len(names) :]
    f0_bufs, f1_bufs = rest[:16], rest[16:32]
    o_bufs, q_bufs, kv_bufs = (rest[i : i + 8] for i in (32, 40, 48))
    f0_loads, f1_loads, chip_bufs = rest[56:62], rest[62:68], rest[68:73]
    send, recv, local = rest[73:]
    me = Place()
    net = Net(send, recv, local)
    z, y, h, x, k, c, t = me.z, me.y, me.h, me.x, me.k, me.c, me.t
    load_dbr = net.here(r.dbr, r.v_dbr)
    load_wo = net.here(r.wo, r.v_wo)
    load_kv = net.here(r.kv, r.v_kv)
    load_normed = net.here(r.normed, r.v_normed)
    load_small = net.here(r.small, r.v_small)
    load_out = net.here(r.outp.at[:, k], r.v_outp)
    r.kv = r.v_kv
    barrier(
        [me.block(lax.rem(c + j, 8), k) for j in range(1, 8)]
        + [
            me.ring(lax.rem(z + j // 4, 4), lax.rem(y + j % 4, 4), h)
            for j in range(1, 16)
            if j // 4
        ]
        + [me.chip(lax.rem(x + j, 4), k) for j in range(1, 4)]
        + [me.chip(lax.rem(x + j, 4), 1 - k) for j in range(4)]
    )
    feed0 = reduce_ring(net, me, r.gfeed.at[0], 0, 640, f0_bufs, r.gf.at[h, 0], f0_loads)
    feed1 = reduce_ring(net, me, r.gfeed.at[1], 0, 640, f1_bufs, r.gf.at[h, 1], f1_loads)
    next(feed0)
    outs = ChipSum(net, me, r.outp, lambda i: r.v_outp[i], chip_bufs)
    for name in ("far", "above", "below", "own"):
        outs.push(name)
    out_steps = outs.steps()
    r.dkv[...] = jnp.zeros_like(r.dkv)
    r.tot[...] = jnp.zeros_like(r.tot)
    to_lines(r.tot, 0, r.gain[...])
    for half in range(2):
        for head in range(3):
            r.mixed[half * HALF : (half + 1) * HALF, head * HD : (head + 1) * HD] = r.att[
                half, head
            ].astype(BF16)
    load_wo.wait()
    load_dbr.wait()
    wo = r.v_wo[...].reshape(D, QW)
    d_mixed = dot_nn(r.v_dbr[...].reshape(512, D), wo)
    deltas = []
    for half in range(2):
        rows = slice(half * HALF, (half + 1) * HALF)
        for head in range(3):
            piece = d_mixed[rows, head * HD : (head + 1) * HD].astype(BF16)
            r.dm[half, head] = piece
            both = piece.astype(F32) * r.att[half, head]
            deltas.append(jnp.sum(both.T, axis=0, keepdims=True))
    load_out.wait()
    next(out_steps)
    load_kv.wait()
    next(feed1)
    attend_back(me, r, deltas)
    for p in range(8):
        r.k_send[p] = r.dkv[2 * p + 1 - k].astype(BF16)
    kx = net.copy(r.k_send, r.k_recv, me.core)
    next(feed0)
    kx.wait()
    for p in range(8):
        r.dkv[2 * p + k] += r.k_recv[p].astype(F32)
        r.k_send[p] = r.dkv[2 * p + k].astype(BF16)
    r.d_kv[...] = r.dkv[2 * c + k]
    k_sent = []
    order = (4, 3, 5, 2, 6, 1, 7)
    for i, j in enumerate(order):
        there = lax.rem(c + 8 - j, 8)
        k_sent.append(
            net.copy_if(c >= j, r.k_send.at[there], r.k_far.at[i], me.block(there, k))
        )
    next(feed1)
    next(out_steps)
    columns_by_row(r.v_dbr, slice(0, 4), r.mixed[...], r.g_o)
    ring_o = reduce_direct(net, me, r.g_o, o_bufs, r.l_o)
    next(ring_o)
    load_normed.wait()
    load_small.wait()
    columns_by_row(r.v_normed, slice(0, 4), r.dq[...], r.g_q)
    ring_q = reduce_direct(net, me, r.g_q, q_bufs, r.l_q)
    next(ring_q)
    next(out_steps)
    next(out_steps)
    to_lines(r.tot, 12 + 3 * t, jnp.sum(r.dq[...].astype(F32), axis=0, keepdims=True))
    wq = r.v_small[:, :, :, :, 0:QW].reshape(D, QW)
    for i in range(4):
        r.part[i] = dot_nt(r.dq[i * ROWS : (i + 1) * ROWS, :], wq)
    for i, (j, made) in enumerate(zip(order, k_sent)):

        @pl.when(c + j < 8)
        def _():
            made.wait_recv()
            r.d_kv[...] += r.k_far[i].astype(F32)

    d_kv = r.d_kv[...]
    half_rows = pl.ds(pl.multiple_of(k * HALF, HALF), HALF)
    cosine, sine = r.cos[half_rows, :], r.sin[half_rows, :]
    d_key = d_kv[0] * INV_ROOT
    r.dpair[:, 0:HD] = (d_key * cosine - pltpu.roll(d_key, HD // 2, 1) * sine).astype(BF16)
    r.dpair[:, HD : 2 * HD] = d_kv[1].astype(BF16)
    d_pair = r.dpair[...]
    wkv = r.v_small[:, :, :, :, QW:640].reshape(D, 2 * HD)
    for i in range(2):
        at = 2 * k + i
        r.part[at] = r.part[at] + dot_nt(d_pair[i * ROWS : (i + 1) * ROWS, :], wkv)
    norm1 = sum_block(net, me, r.part, r.s1, r.r1, r.s2, r.r2)
    next(norm1)
    columns_by_row(r.v_normed, pl.ds(2 * k, 2), d_pair, r.p_send)
    px = net.copy(r.p_send, r.p_recv, me.core)
    next(norm1)
    sums = jnp.sum(d_pair.astype(F32), axis=0, keepdims=True)
    to_lines(r.tot, 24 + me.xl, sums[:, :HD])
    to_lines(r.tot, 26 + me.xl, sums[:, HD:])
    px.wait_recv()
    r.g_kv[...] = (r.p_send[...].astype(F32) + r.p_recv[...].astype(F32)).astype(BF16)
    ring_kv = reduce_direct(net, me, r.g_kv, kv_bufs, r.l_kv)
    next(ring_kv)
    gain = jnp.zeros((1, D), F32)
    for i in range(4):
        gain = gain + jnp.sum(r.part[i] * r.v_normed[i].astype(F32), axis=0, keepdims=True)
    to_lines(r.tot, 28, gain / r.gains[0:1, :])
    total = Total(net, me, r.tot[...], r.t_x, r.t_yz)
    next(feed0)
    next(feed1)
    next(ring_o)
    next(ring_q)
    next(ring_kv)
    d_norm1 = next(norm1)
    total.second()
    next(feed0)
    flat = r.x[...].astype(F32)
    scale1 = rms(flat)
    xh1 = flat * scale1
    e1 = d_norm1 * r.gains[0:1, :]
    r.igrad[...] = r.dh[...] + scale1 * (
        e1 - xh1 * jnp.mean(e1 * xh1, axis=-1, keepdims=True)
    )
    next(ring_kv)
    next(feed1)
    next(ring_o)
    next(ring_q)
    next(feed0)
    next(feed1)
    r.result[...] = (r.hid[...] + next(out_steps)).astype(BF16)
    r.total[...] = total.final()
    for ring in (ring_o, ring_q, ring_kv):
        for _ in ring:
            pass
    su_q, su_o, su_kv = q_bufs[6], o_bufs[6], kv_bufs[6]
    pair_own = su_kv[...].astype(F32) + r.l_kv[...].astype(F32)
    r.kv_own[...] = pair_own.astype(BF16)
    pair_sent = net.copy(r.kv_own, r.kv_far, me.side)
    r.gsm[:, 0:QW] = su_q[...].astype(F32) + r.l_q[...].astype(F32)
    r.gsm[:, QW:] = su_o[...].astype(F32) + r.l_o[...].astype(F32)
    for ring in (feed0, feed1):
        for _ in ring:
            pass
    r.gf[h, 0] = f0_bufs[6][...]
    r.gf[h, 1] = f1_bufs[6][...]
    pair_sent.wait_recv()
    pieces = (r.kv_own[...].astype(F32), r.kv_far[...].astype(F32))
    for i, at in enumerate((me.xl, 1 - me.xl)):
        r.gpair[:, pl.ds(pl.multiple_of(at * HD, HD), HD)] = pieces[i][:, :HD]
        r.gpair[:, pl.ds(pl.multiple_of((2 + at) * HD, HD), HD)] = pieces[i][:, HD:]

    net.finish((kx,))


def back(*arrays):
    shapes = (
        ((ROWS, D), BF16),
        ((ROWS, D), F32),
        ((2, 2, PIECE, FPAD), BF16),
        ((PIECE, 2 * QW), F32),
        ((PIECE, 4 * HD), F32),
        ((40, HD), F32),
    )
    return call(
        back_kernel,
        BACK_IN,
        arrays,
        dict(zip(BACK_OUT, shapes)),
        ("outp", "gfeed", "dbr", "small", "wo", "normed", "kv"),
        scratch_of(BACK_SCRATCH)
        + ring_bufs((), FPAD, 640)
        + ring_bufs((), FPAD, 640)
        + direct_bufs(QW)
        + direct_bufs(QW)
        + direct_bufs(2 * HD)
        + [pltpu.VMEM((n, PIECE, FPAD), BF16) for n in (2, 2, 4)] * 4
        + [pltpu.VMEM(*s) for s in CHIP_BUFS]
        + semaphores(230, 230, 20),
        2,
        63,
        "back",
    )


def prep_kernel(lengths, wq, wp, wo, wf, biases, p1, po, p2, pd, bias, cos, sin, begin):
    me = Place()
    p1[:, 0:QW] = wq[...].astype(BF16)
    for i in range(2):
        at = pl.ds(pl.multiple_of(i * KV * HD + me.xl * HD, HD), HD)
        to = slice(QW + i * HD, QW + (i + 1) * HD)
        p1[:, to] = wp[:, at].astype(BF16)
        at = pl.ds(pl.multiple_of(HQ * HD + i * KV * HD + me.xl * HD, HD), HD)
        bias[:, to] = biases[:, at]
    bias[:, 0:QW] = biases[:, pl.ds(pl.multiple_of(me.t * QW, HD), QW)]
    po[...] = wo[...].astype(BF16)
    rest = FCOLS - FPAD
    for m in range(3):
        first, second = (p2.at[0, m], p2.at[1, m]) if m < 2 else (pd.at[0], pd.at[1])
        first[...] = wf[m, :, 0:FPAD].astype(BF16)
        tail = wf[m, :, FPAD:FCOLS].astype(BF16)
        second[...] = jnp.concatenate([tail, jnp.zeros((PIECE, FPAD - rest), BF16)], axis=1)

    def starts(index):
        end, found = lengths[0, 0], jnp.zeros_like(index)
        for i in range(3):
            found = jnp.where(index >= end, end, found)
            end = end + lengths[0, i + 1]
        return found

    first = me.c * 512
    along = lax.broadcasted_iota(jnp.int32, (2, HALF), 1)
    along = along + lax.broadcasted_iota(jnp.int32, (2, HALF), 0) * HALF + first
    begin[...] = starts(along)
    down_rows = lax.broadcasted_iota(jnp.int32, (512, HD), 0) + first
    position = (down_rows - starts(down_rows)).astype(F32)
    lane = lax.broadcasted_iota(jnp.int32, (512, HD), 1)
    steps = lax.rem(lane, HD // 2).astype(F32)
    angle = position * jnp.exp(-(2.0 * steps / HD) * math.log(ROPE_BASE))
    cos[...] = jnp.cos(angle)
    turned = jnp.sin(angle)
    sin[...] = jnp.where(lane < HD // 2, -turned, turned)


def prep(lengths, wq, wp, wo, wf, biases):
    shape = jax.ShapeDtypeStruct
    vmem = pl.BlockSpec(memory_space=pltpu.VMEM)
    return pl.pallas_call(
        prep_kernel,
        out_shape=(
            shape((PIECE, 640), BF16),
            shape((PIECE, QW), BF16),
            shape((2, 2, PIECE, FPAD), BF16),
            shape((2, PIECE, FPAD), BF16),
            shape((1, 640), F32),
            shape((512, HD), F32),
            shape((512, HD), F32),
            shape((2, HALF), jnp.int32),
        ),
        in_specs=[pl.BlockSpec(memory_space=pltpu.SMEM)] + [vmem] * 5,
        out_specs=(vmem,) * 8,
        compiler_params=pltpu.CompilerParams(vmem_limit_bytes=63 * 2**20),
        name="prep",
    )(lengths, wq, wp, wo, wf, biases)


def adamw(weight, mean_old, square_old, grad, rate, decay):
    mean_new = BETA_ONE * mean_old + (1.0 - BETA_ONE) * grad
    square_new = BETA_TWO * square_old + (1.0 - BETA_TWO) * grad * grad
    mean_hat = mean_new / (1.0 - BETA_ONE**STEP)
    square_hat = square_new / (1.0 - BETA_TWO**STEP)
    weight_new = weight - rate * (mean_hat / (jnp.sqrt(square_hat) + ADAM_EPS) + decay * weight)
    return (mean_new, square_new, weight_new)


RATES = {
    "query": (0.05, 0.1),
    "pair": (3.0 / math.sqrt(D), 0.1),
    "output": (3.0 / math.sqrt(max(HQ * HD // 256, 1)), 0.1),
    "feed": (0.05, 0.1),
    "gains": (1.5, 0.0),
    "biases": (0.5, 0.0),
}
STATE_SHAPES = {
    "query": (PIECE, QW),
    "pair": (PIECE, 2 * KV * HD),
    "output": (PIECE, QW),
    "feed": (3, PIECE, FCOLS),
    "gains": (2, D),
    "biases": (16, HD),
}


def as_row(ref, at):
    return jnp.concatenate([ref[at + i : at + i + 1, :] for i in range(D // HD)], axis=1)


def update_kernel(result, igrad, gf, gsm, gpair, total, gd, *refs):
    state, (result_out, igrad_out), news = refs[:18], refs[18:20], refs[20:]

    def update(i, name, grad, at=Ellipsis):
        olds = [ref[at] for ref in state[3 * i : 3 * i + 3]]
        for ref, new in zip(news[3 * i : 3 * i + 3], adamw(*olds, grad, *RATES[name])):
            ref[at] = new

    for m in range(3):
        for half, lanes in enumerate((slice(0, FPAD), slice(FPAD, FCOLS))):
            some = slice(0, lanes.stop - lanes.start)
            grad = gf[half, m, :, some] if m < 2 else gd[half, :, some]
            update(3, "feed", grad.astype(F32), (m, slice(None), lanes))
    result_out[...] = result[...]
    igrad_out[...] = igrad[...]
    update(0, "query", gsm[:, 0:QW])
    update(1, "pair", gpair[...])
    update(2, "output", gsm[:, QW : 2 * QW])
    update(4, "gains", jnp.concatenate([as_row(total, 28), as_row(total, 0)], axis=0))
    update(5, "biases", total[12:28, :])


def update_all(grads, state):
    vmem = pl.BlockSpec(memory_space=pltpu.VMEM)
    rows = [jax.ShapeDtypeStruct((ROWS, D), BF16), jax.ShapeDtypeStruct((ROWS, D), F32)]
    return pl.pallas_call(
        update_kernel,
        out_shape=rows + [jax.ShapeDtypeStruct(s, F32) for s in STATE_SHAPES.values() for _ in range(3)],
        in_specs=[vmem] * (len(grads) + len(state)),
        out_specs=[vmem] * (len(state) + 2),
        compiler_params=pltpu.CompilerParams(vmem_limit_bytes=63 * 2**20),
        name="update",
    )(*grads, *state)


def body(
    inputs,
    cotangent,
    lengths,
    query_weight,
    query_mean,
    query_square,
    pair_weight,
    pair_mean,
    pair_square,
    output_weight,
    output_mean,
    output_square,
    feed_weight,
    feed_mean,
    feed_square,
    gains,
    gains_mean,
    gains_square,
    biases,
    biases_mean,
    biases_square,
):
    feeds = [a.transpose(1, 0, 2) for a in (feed_weight, feed_mean, feed_square)]
    p1, po, p2, pd, bias, cosine, sine, begin = prep(
        lengths, query_weight, pair_weight, output_weight, feeds[0], biases.reshape(1, QKV)
    )
    feed, wd, small, wo, normed, q, kv, att, lse, hid, n2, cot8 = front(
        inputs, cotangent, gains, bias, cosine, sine, begin, p1, po, p2, pd
    )
    out, g_feed, g_down, dbr, dh, gain = mid(n2, cot8, feed.reshape(2, D, FPAD), wd, hid, gains)
    grads = back(
        out,
        g_feed.reshape(2, 4, 4, 2, PIECE, FPAD),
        *(dbr, dh, gain, hid, inputs, small, wo, normed),
        *(q, kv, att, lse, cosine, sine, begin, gains),
    )
    lines = lambda *arrays: [a.reshape(-1, HD) for a in arrays]
    made = list(update_all(
        (*grads, g_down),
        [query_weight, query_mean, query_square]
        + [pair_weight, pair_mean, pair_square]
        + [output_weight, output_mean, output_square]
        + feeds
        + [gains, gains_mean, gains_square]
        + lines(biases, biases_mean, biases_square),
    ))
    made[11:14] = [a.transpose(1, 0, 2) for a in made[11:14]]
    made[17:20] = [a.reshape(QKV) for a in made[17:20]]
    return tuple(made)


def solution(mesh):
    mesh = Mesh(mesh.devices.reshape(4, 4, 2, 4), AXES)
    rows = P(("dp", "y", "xh", "tensor"), None)
    cut = P(("dp", "y", "xh"), "tensor")
    pair = P(("dp", "y", "xh"), None)
    feed = P(("dp", "y", "xh"), None, "tensor")
    whole = P()
    in_specs = (rows, rows, P("dp", None))
    in_specs += (cut,) * 3 + (pair,) * 3 + (cut,) * 3 + (feed,) * 3 + (whole,) * 6
    out_specs = (rows, rows) + (cut,) * 3 + (pair,) * 3 + (cut,) * 3 + (feed,) * 3 + (whole,) * 6
    return jax.shard_map(body, mesh=mesh, in_specs=in_specs, out_specs=out_specs, check_vma=False)
```
